32 devices in a mesh: tm: 4 (over x, core), contact: 8 (over z, y).
Axes of the slice: x: 2, y: 2, z: 4, core: 2. Of those that a mesh axis runs over, the one named last changes fastest.
Arguments:
- signal: bfloat16 [8, 512, 4096], P(None, 'contact', 'tm'), may hold values from -6 to 6
- fir_taps: bfloat16 [512, 129], P('contact'), may hold values from -0.5 to 0.5
- neighbours: int32 [512, 4], replicated, may hold values from 0 to 511, as said below
- live_mask: int32 [512], replicated, may hold values 0 or 1
- lap_coef: float32 [512], replicated, may hold values from 0.1 to 1
- w_query: bfloat16 [256, 256], replicated, may hold values from -8 to 8
- w_key: bfloat16 [256, 256], replicated, may hold values from -8 to 8
- w_value: bfloat16 [256, 256], replicated, may hold values from -0.375 to 0.375
- w_out: bfloat16 [256, 256], replicated, may hold values from -0.375 to 0.375
- cotangent: bfloat16 [8, 512, 4096], P(None, 'contact', 'tm'), may hold values from -6 to 6
Outputs:
- attended: bfloat16 [8, 512, 4096], P(None, 'contact', 'tm')
- weight_grads: float32 [4, 256, 256], replicated
The draws below stay inside these ranges and needn't reach their ends.
Inputs may be any that keep to these rules, and one draw needn't show every extreme that they name: `neighbours`: entry [c, k] names a contact whose grid row (index // 16) differs from that of contact c by at most one and whose column (index % 16) differs by at most two.
All inputs are finite; a program needn't handle non-finite values.
Results may differ from the reference program's by a relative error of at most 0.011.
Values may be sent and summed in bfloat16 or wider, within the bound.
No kernel may reach another device: no remote copies, remote signals or barrier semaphores. Data moves between devices by JAX's collectives and lax.ppermute only.
A program may use at most 64 MiB of HBM per device.

```python
import math
import jax
import jax.numpy as jnp
from jax import lax

GRID_ROWS = 32
GRID_COLS = 16
CONTACTS = 512
NEIGHBOURS = 4
TAPS = 129
PATCH = 256
HEADS = 4
BATCH = 8
PATCHES = 16
SAMPLES = 4096


def projection(key, salt):
    matrix = jax.random.normal(jax.random.fold_in(key, salt), (PATCH, PATCH), jnp.float32) / math.sqrt(PATCH)
    return matrix


def draw_w_query(key, part):
    return projection(key, 1).astype(jnp.bfloat16)


def draw_w_key(key, part):
    return projection(key, 2).astype(jnp.bfloat16)


def draw_neighbours(key, part):
    contact_ids = jnp.arange(CONTACTS, dtype=jnp.int32)
    grid_row = contact_ids // GRID_COLS
    grid_col = contact_ids % GRID_COLS
    row_step = jax.random.randint(jax.random.fold_in(key, 21), (CONTACTS, NEIGHBOURS), -1, 2, dtype=jnp.int32)
    col_step = jax.random.randint(jax.random.fold_in(key, 22), (CONTACTS, NEIGHBOURS), -2, 3, dtype=jnp.int32)
    near_row = jnp.clip(grid_row[:, None] + row_step, 0, GRID_ROWS - 1)
    near_col = jnp.clip(grid_col[:, None] + col_step, 0, GRID_COLS - 1)
    return (near_row * GRID_COLS + near_col).astype(jnp.int32)


def touch_ends(drawn, key, smallest, largest):
    spot = [jax.random.randint(jax.random.fold_in(key, axis), (), 0, length) for axis, length in enumerate(drawn.shape)]
    widest = drawn.shape.index(max(drawn.shape))
    next_to = spot[:widest] + [(spot[widest] + 1) % drawn.shape[widest]] + spot[widest + 1:]
    return drawn.at[tuple(spot)].set(smallest).at[tuple(next_to)].set(largest)


def levels(key, shape, split, least, top_value):
    def one(axis_at, shards_of):
        steps = jax.random.uniform(jax.random.fold_in(jax.random.fold_in(key, 6), axis_at), (shards_of,), jnp.float32, least / len(split), top_value / len(split))
        return jnp.repeat(jnp.exp(steps), shape[axis_at] // shards_of).reshape((-1,) + (1,) * (len(shape) - axis_at - 1))

    level = one(*split[0])
    for cut in split[1:]:
        level = level * one(*cut)
    return level


def scatter_about(stream_key, extent, width, limit, pieces=(), kind=jnp.bfloat16):
    entries = jax.random.normal(stream_key, extent, jnp.float32) * width
    if len(pieces) > 0:
        entries = levels(stream_key, extent, pieces, -0.22, 0.18) * entries
    return jnp.clip(entries, min=-limit, max=limit).astype(kind)


def setup_inputs(seed: int = 0) -> dict:
    key_of = jax.random.split(jax.random.key(seed), 11)
    signal = scatter_about(key_of[0], (BATCH, CONTACTS, SAMPLES), 1.0, 6.0, ((1, 8), (2, 4)))
    fir_taps = scatter_about(key_of[1], (CONTACTS, TAPS), TAPS ** -0.5, 0.5, ((0, 8),))
    neighbours = draw_neighbours(jax.random.fold_in(key_of[10], 71), 0)
    live_mask = touch_ends((jax.random.randint(key_of[3], (CONTACTS,), 0, 16) < 15).astype(jnp.int32), jax.random.fold_in(key_of[3], 1), 0, 1)
    lap_coef = jnp.clip(jnp.exp(jax.random.uniform(key_of[4], (CONTACTS,), jnp.float32, math.log(0.1), math.log(1.0))), 0.1, 1.0)
    w_query = draw_w_query(jax.random.fold_in(key_of[10], 71), 0)
    w_key = draw_w_key(jax.random.fold_in(key_of[10], 71), 0)
    w_value = scatter_about(key_of[7], (PATCH, PATCH), PATCH ** -0.5, 0.375)
    w_out = scatter_about(key_of[8], (PATCH, PATCH), PATCH ** -0.5, 0.375)
    cotangent = scatter_about(key_of[9], (BATCH, CONTACTS, SAMPLES), 1.0, 6.0, ((1, 8), (2, 4)))
    return {"signal": signal, "fir_taps": fir_taps, "neighbours": neighbours, "live_mask": live_mask, "lap_coef": lap_coef, "w_query": w_query, "w_key": w_key, "w_value": w_value, "w_out": w_out, "cotangent": cotangent}


def contract(left, right, left_dim, right_dim):
    return lax.dot_general(left, right, (((left_dim,), (right_dim,)), ((), ())), preferred_element_type=jnp.float32)

def toeplitz(fir_taps):
    rim_width = fir_taps.shape[1] - 1
    source = jnp.arange(2 * rim_width, dtype=jnp.int32)[:, None]
    target = jnp.arange(rim_width, dtype=jnp.int32)[None, :]
    lag_table = (target + rim_width - source).astype(jnp.int32)
    inside = (lag_table >= 0) & (lag_table <= rim_width)
    picked = jnp.take(fir_taps, jnp.clip(lag_table, 0, rim_width).astype(jnp.int32), axis=1)
    return jnp.where(inside[None, :, :], picked, jnp.zeros_like(picked))

def laplace(field, centre, indices, nbr_alive, own_alive, coef):
    middle = centre.astype(jnp.float32)
    running = jnp.zeros_like(middle)
    for slot_index in range(indices.shape[1]):
        nearby = jnp.take(field, indices[:, slot_index], axis=-2).astype(jnp.float32)
        running = running + nbr_alive[:, slot_index][:, None] * (nearby - middle)
    return (own_alive[:, None] * (middle + coef[:, None] * running)).astype(jnp.bfloat16)

def one_head(query_head, key_head, value_head, back_head, key_alive, score_scale):
    scores = contract(query_head, key_head, 1, 1) * score_scale
    scores = jnp.where(key_alive[None, :] > 0, scores, -1e+30)
    top_score = lax.optimization_barrier(jnp.max(scores, axis=1, keepdims=True))
    raised = jnp.exp(scores - top_score)
    attn_prob = raised / lax.optimization_barrier(jnp.sum(raised, axis=1, keepdims=True))
    prob_low = attn_prob.astype(jnp.bfloat16)
    head_out = jnp.dot(prob_low, value_head, preferred_element_type=jnp.float32).astype(jnp.bfloat16)
    grad_value = contract(prob_low, back_head, 0, 0).astype(jnp.bfloat16)
    grad_prob = contract(back_head, value_head, 1, 1)
    row_inner = lax.optimization_barrier(jnp.sum(back_head.astype(jnp.float32) * head_out.astype(jnp.float32), axis=1, keepdims=True))
    grad_score = (attn_prob * (grad_prob - row_inner) * score_scale).astype(jnp.bfloat16)
    grad_query = jnp.dot(grad_score, key_head, preferred_element_type=jnp.float32).astype(jnp.bfloat16)
    grad_key = contract(grad_score, query_head, 0, 0).astype(jnp.bfloat16)
    return (head_out, grad_query, grad_key, grad_value)

def group_step(tokens, upstream, key_alive, w_query, w_key, w_value, w_out):
    as_float = tokens.astype(jnp.float32)
    normed = (as_float * lax.rsqrt(lax.optimization_barrier(jnp.mean(as_float * as_float, axis=1, keepdims=True)) + 1e-05)).astype(jnp.bfloat16)
    query_rows = jnp.dot(normed, w_query, preferred_element_type=jnp.float32).astype(jnp.bfloat16)
    key_rows = jnp.dot(normed, w_key, preferred_element_type=jnp.float32).astype(jnp.bfloat16)
    value_rows = jnp.dot(normed, w_value, preferred_element_type=jnp.float32).astype(jnp.bfloat16)
    back_signal = contract(upstream, w_out, 1, 1).astype(jnp.bfloat16)
    head_size = w_query.shape[1] // HEADS
    score_scale = head_size ** (-0.5)
    head_results = []
    for head_index in range(HEADS):
        lower = head_index * head_size
        upper = lower + head_size
        head_results.append(one_head(query_rows[:, lower:upper], key_rows[:, lower:upper], value_rows[:, lower:upper], back_signal[:, lower:upper], key_alive, score_scale))
    mixed_heads = jnp.concatenate([entry[0] for entry in head_results], axis=1)
    grad_query = jnp.concatenate([entry[1] for entry in head_results], axis=1)
    grad_key = jnp.concatenate([entry[2] for entry in head_results], axis=1)
    grad_value = jnp.concatenate([entry[3] for entry in head_results], axis=1)
    attended = jnp.dot(mixed_heads, w_out, preferred_element_type=jnp.float32).astype(jnp.bfloat16)
    grad_stack = jnp.stack([contract(normed, grad_query, 0, 0), contract(normed, grad_key, 0, 0), contract(normed, grad_value, 0, 0), contract(mixed_heads, upstream, 0, 0)])
    return (attended, grad_stack)

def reference(signal, fir_taps, neighbours, live_mask, lap_coef, w_query, w_key, w_value, w_out, cotangent):
    rim_width = TAPS - 1
    filter_table = toeplitz(fir_taps).astype(jnp.float32)
    alive_f = live_mask.astype(jnp.float32)
    nbr_alive = jnp.take(alive_f, neighbours)

    def section_one(one_row):
        extended = jnp.concatenate([jnp.zeros((CONTACTS, rim_width), jnp.bfloat16), one_row], axis=1).astype(jnp.float32)
        blocks = extended.reshape(CONTACTS, SAMPLES // rim_width + 1, rim_width)
        windows = jnp.concatenate([blocks[:, :-1], blocks[:, 1:]], axis=2)
        filtered = jnp.einsum('cjw,cwu->cju', windows, filter_table, precision=lax.Precision.HIGHEST)
        filtered = filtered.reshape(CONTACTS, SAMPLES).astype(jnp.bfloat16)
        return laplace(filtered, filtered, neighbours, nbr_alive, alive_f, lap_coef)
    ready = lax.map(section_one, signal)

    def to_groups(whole):
        return whole.reshape(BATCH, CONTACTS, PATCHES, PATCH).transpose(0, 2, 1, 3).reshape(BATCH * PATCHES, CONTACTS, PATCH)

    def run_group(running, inputs_pair):
        attended, grad_stack = group_step(inputs_pair[0], inputs_pair[1], alive_f, w_query, w_key, w_value, w_out)
        return (running + grad_stack, attended)
    running, attended = lax.scan(run_group, jnp.zeros((4, PATCH, PATCH), jnp.float32), (to_groups(ready), to_groups(cotangent)))
    attended = attended.reshape(BATCH, PATCHES, CONTACTS, PATCH).transpose(0, 2, 1, 3).reshape(BATCH, CONTACTS, SAMPLES)
    return (attended, running * (BATCH * PATCHES * CONTACTS) ** (-0.5))
```

```python
import functools

import jax
import jax.numpy as jnp
from jax import lax
from jax.experimental import pallas as pl
from jax.experimental.pallas import tpu as pltpu
from jax.sharding import PartitionSpec as P

HEADS = 4
F32 = jnp.float32
BF16 = jnp.bfloat16


def mm(left, right, left_dim=1, right_dim=0):
    return lax.dot_general(
        left, right, (((left_dim,), (right_dim,)), ((), ())), preferred_element_type=F32
    )


def filter_kernel(sig_ref, rim_ref, taps_ref, out_ref):
    batch, rows, slab = sig_ref.shape
    width = rim_ref.shape[2]
    blocks = slab // width
    signal = jnp.swapaxes(sig_ref[...].astype(F32), 0, 1)
    rim = jnp.swapaxes(rim_ref[...].astype(F32), 0, 1)
    results = []
    for row in range(rows):
        own = [signal[row, :, j * width : (j + 1) * width] for j in range(blocks)]
        current = jnp.concatenate(own, axis=0)
        before = jnp.concatenate([rim[row]] + own[:-1], axis=0)
        window = jnp.concatenate([before, current], axis=1).astype(BF16)
        spread = jnp.broadcast_to(taps_ref[row : row + 1, :], (width, 2 * width))
        rolled = pltpu.roll(spread, 0, 1, stride=1, stride_axis=0)
        table = jnp.concatenate([rolled[:, width:], rolled[:, :width]], axis=0).astype(BF16)
        product = mm(window, table)
        results.append(
            jnp.concatenate(
                [product[j * batch : (j + 1) * batch] for j in range(blocks)], axis=1
            )
        )
    out_ref[...] = jnp.swapaxes(jnp.stack(results, axis=0), 0, 1).astype(BF16)


def filter_all(signal, rim, taps):
    batch, contacts, slab = signal.shape
    width = rim.shape[2]
    rows = 16
    return pl.pallas_call(
        filter_kernel,
        grid=(contacts // rows,),
        in_specs=[
            pl.BlockSpec((batch, rows, slab), lambda i: (0, i, 0)),
            pl.BlockSpec((batch, rows, width), lambda i: (0, i, 0)),
            pl.BlockSpec((rows, 2 * width), lambda i: (i, 0)),
        ],
        out_specs=pl.BlockSpec((batch, rows, slab), lambda i: (0, i, 0)),
        out_shape=jax.ShapeDtypeStruct(signal.shape, BF16),
        compiler_params=pltpu.CompilerParams(vmem_limit_bytes=40 * 2**20),
        cost_estimate=pl.CostEstimate(
            flops=4 * batch * contacts * slab * width,
            bytes_accessed=4 * batch * contacts * slab,
            transcendentals=0,
        ),
        name="filter",
    )(signal, rim, taps)


def attend_kernel(
    feat_ref, up_ref, nbr_ref, live_row_ref, live_col_ref, coef_ref, wqkv_ref, wo_ref,
    out_ref, wg_ref, counts, alive_count, e_all, gs_all, v_blocks, k_blocks,
):
    contacts, width = feat_ref.shape
    head = width // HEADS
    scale = head ** (-0.5)
    step = pl.program_id(0)

    @pl.when(step == 0)
    def _():
        ids = lax.broadcasted_iota(jnp.int32, (contacts, contacts), 1)
        total = jnp.zeros((contacts, contacts), F32)
        for slot in range(nbr_ref.shape[1]):
            hit = nbr_ref[:, slot : slot + 1] == ids
            total = total + jnp.where(hit, live_row_ref[...], 0.0)
        counts[...] = total.astype(BF16)
        alive_count[...] = jnp.sum(total, axis=1, keepdims=True)
        wg_ref[...] = jnp.zeros_like(wg_ref)

    field = feat_ref[...]
    middle = field.astype(F32)
    beside = mm(counts[...], field)
    ready = live_col_ref[...] * (middle + coef_ref[...] * (beside - alive_count[...] * middle))
    ready = ready.astype(BF16).astype(F32)
    mean_square = jnp.mean(ready * ready, axis=1, keepdims=True)
    normed = (ready * lax.rsqrt(mean_square + 1e-05)).astype(BF16)
    upstream = up_ref[...]
    query = (mm(normed, wqkv_ref[:, :width]) * scale).astype(BF16)
    keys = mm(normed, wqkv_ref[:, width : 2 * width]).astype(BF16)
    value = mm(normed, wqkv_ref[:, 2 * width :]).astype(BF16)
    back = mm(upstream, wo_ref[...], 1, 1)
    lane_head = lax.broadcasted_iota(jnp.int32, (1, width), 1) // head
    masks = [(lane_head == h).astype(F32) for h in range(HEADS)]
    low_masks = [m.astype(BF16) for m in masks]
    bias = jnp.where(live_row_ref[...] > 0, 0.0, -1e30)
    inverse = jnp.zeros((contacts, width), F32)
    for h in range(HEADS):
        k_blocks[h * contacts : (h + 1) * contacts, :] = keys * low_masks[h]
        v_blocks[h * contacts : (h + 1) * contacts, :] = value * low_masks[h]
    for h in range(HEADS):
        scores = mm(query * low_masks[h], keys, 1, 1) + bias
        top = jnp.max(scores, axis=1, keepdims=True)
        raised = jnp.exp(scores - top)
        inverse = inverse + masks[h] * (1.0 / jnp.sum(raised, axis=1, keepdims=True))
        e_all[:, h * contacts : (h + 1) * contacts] = raised.astype(BF16)
    mixed = (mm(e_all[...], v_blocks[...]) * inverse).astype(BF16)
    out_ref[...] = mm(mixed, wo_ref[...]).astype(BF16)
    back_scaled = (back.astype(BF16).astype(F32) * inverse).astype(BF16)
    inner = back_scaled.astype(F32) * mixed.astype(F32)
    back_t = back_scaled.T
    query_t = query.T
    grad_value_t = []
    grad_key_t = []
    for h in range(HEADS):
        grad_prob = mm(back_scaled * low_masks[h], value, 1, 1)
        row_inner = jnp.sum(inner * masks[h], axis=1, keepdims=True)
        raised = e_all[:, h * contacts : (h + 1) * contacts]
        grad_score = (raised.astype(F32) * (grad_prob - row_inner)).astype(BF16)
        gs_all[:, h * contacts : (h + 1) * contacts] = grad_score
        grad_value_t.append(mm(back_t[h * head : (h + 1) * head], raised))
        grad_key_t.append(mm(query_t[h * head : (h + 1) * head], grad_score))
    grad_query = (mm(gs_all[...], k_blocks[...]) * scale).astype(BF16)
    grad_key_t = jnp.concatenate(grad_key_t, axis=0).astype(BF16)
    grad_value_t = jnp.concatenate(grad_value_t, axis=0).astype(BF16)
    wg_ref[0] += mm(normed.T, grad_query)
    wg_ref[1] += mm(grad_key_t, normed)
    wg_ref[2] += mm(grad_value_t, normed)
    wg_ref[3] += mm(mixed.T, upstream)

    @pl.when(step == pl.num_programs(0) - 1)
    def _():
        wg_ref[1] = wg_ref[1].T
        wg_ref[2] = wg_ref[2].T


def attend_all(features, upstream, neighbours, live_row, live_col, coef, w_qkv, w_out):
    contacts, span = features.shape
    width = w_out.shape[0]
    groups = span // width
    block = pl.BlockSpec((contacts, width), lambda i: (0, i))

    def whole(shape):
        return pl.BlockSpec(shape, lambda i: (0,) * len(shape))

    return pl.pallas_call(
        attend_kernel,
        grid=(groups,),
        in_specs=[
            block, block, whole(neighbours.shape), whole(live_row.shape), whole(live_col.shape),
            whole(coef.shape), whole(w_qkv.shape), whole(w_out.shape),
        ],
        out_specs=[block, whole((4, width, width))],
        out_shape=[
            jax.ShapeDtypeStruct(features.shape, BF16),
            jax.ShapeDtypeStruct((4, width, width), F32),
        ],
        scratch_shapes=[
            pltpu.VMEM((contacts, contacts), BF16),
            pltpu.VMEM((contacts, 1), F32),
            pltpu.VMEM((contacts, HEADS * contacts), BF16),
            pltpu.VMEM((contacts, HEADS * contacts), BF16),
            pltpu.VMEM((HEADS * contacts, width), BF16),
            pltpu.VMEM((HEADS * contacts, width), BF16),
        ],
        compiler_params=pltpu.CompilerParams(vmem_limit_bytes=48 * 2**20),
        cost_estimate=pl.CostEstimate(
            flops=groups * 4 * 10**9,
            bytes_accessed=6 * contacts * span,
            transcendentals=groups * HEADS * contacts * contacts,
        ),
        name="attend",
    )(features, upstream, neighbours, live_row, live_col, coef, w_qkv, w_out)


def exchange(value, axis):
    return lax.all_to_all(value, axis, split_axis=0, concat_axis=0, tiled=True)


def scatter_sum(value, axis):
    count = lax.axis_size(axis)
    parts = exchange(value.astype(BF16), axis)
    parts = parts.reshape((count, value.shape[0] // count) + value.shape[1:])
    return jnp.sum(parts.astype(F32), axis=0)


def gather(value, axis):
    count = lax.axis_size(axis)
    return exchange(jnp.concatenate([value] * count, axis=0), axis)


def local(
    signal, fir_taps, neighbours, live_mask, lap_coef, w_query, w_key, w_value, w_out, cotangent
):
    batch, contacts_here, slab = signal.shape
    rim_width = fir_taps.shape[1] - 1
    width = w_query.shape[0]
    tm_count = lax.axis_size("tm")
    count = lax.axis_size("contact")
    pieces = max(1, count // batch)

    def by_group(whole):
        if pieces == 1:
            return whole
        cut = whole.reshape(batch, contacts_here, pieces, slab // pieces)
        return cut.transpose(0, 2, 1, 3).reshape(batch * pieces, contacts_here, slab // pieces)

    def to_attend(whole):
        moved = lax.all_to_all(
            by_group(whole), "contact", split_axis=0, concat_axis=1, tiled=True
        )
        held = moved.shape[0]
        return moved.transpose(1, 0, 2).reshape(moved.shape[1], held * moved.shape[2])

    rim = lax.ppermute(
        signal[:, :, slab - rim_width :], "tm", [(i, i + 1) for i in range(tm_count - 1)]
    )
    upstream = to_attend(cotangent)
    taps = jnp.pad(fir_taps.astype(F32), ((0, 0), (0, 2 * rim_width - fir_taps.shape[1])))
    filtered = filter_all(signal, rim, taps)
    features = to_attend(filtered)
    alive = live_mask.astype(F32)
    attended, grads = attend_all(
        features, upstream, neighbours, alive[None, :], alive[:, None], lap_coef[:, None],
        jnp.concatenate([w_query, w_key, w_value], axis=1), w_out,
    )
    held = batch * pieces // count
    shaped = attended.reshape(attended.shape[0], held, slab // pieces).transpose(1, 0, 2)
    returned = lax.all_to_all(shaped, "contact", split_axis=1, concat_axis=0, tiled=True)
    if pieces > 1:
        returned = returned.reshape(batch, pieces, contacts_here, slab // pieces)
        returned = returned.transpose(0, 2, 1, 3).reshape(batch, contacts_here, slab)
    grad_scale = (batch * (slab // width) * tm_count * neighbours.shape[0]) ** (-0.5)
    part = scatter_sum(grads.reshape(4 * width, width), "tm")
    part = scatter_sum(part, "contact") * grad_scale
    summed = gather(gather(part.astype(BF16), "contact"), "tm")
    return (returned, summed.astype(F32).reshape(4, width, width))


def solution(mesh):
    in_specs = (
        P(None, "contact", "tm"),
        P("contact", None),
        P(),
        P(),
        P(),
        P(),
        P(),
        P(),
        P(),
        P(None, "contact", "tm"),
    )
    out_specs = (P(None, "contact", "tm"), P())
    return jax.shard_map(local, mesh=mesh, in_specs=in_specs, out_specs=out_specs, check_vma=False)
```

```python
import functools

import jax
import jax.numpy as jnp
from jax import lax
from jax.experimental import pallas as pl
from jax.experimental.pallas import tpu as pltpu
from jax.sharding import PartitionSpec as P

HEADS = 4
F32 = jnp.float32
BF16 = jnp.bfloat16


def mm(left, right, left_dim=1, right_dim=0):
    return lax.dot_general(
        left, right, (((left_dim,), (right_dim,)), ((), ())), preferred_element_type=F32
    )


def filter_kernel(sig_ref, rim_ref, taps_ref, out_ref):
    batch, rows, slab = sig_ref.shape
    width = rim_ref.shape[2]
    blocks = slab // width
    signal = jnp.swapaxes(sig_ref[...].astype(F32), 0, 1)
    rim = jnp.swapaxes(rim_ref[...].astype(F32), 0, 1)
    results = []
    for row in range(rows):
        own = [signal[row, :, j * width : (j + 1) * width] for j in range(blocks)]
        current = jnp.concatenate(own, axis=0)
        before = jnp.concatenate([rim[row]] + own[:-1], axis=0)
        window = jnp.concatenate([before, current], axis=1).astype(BF16)
        spread = jnp.broadcast_to(taps_ref[row : row + 1, :], (width, 2 * width))
        rolled = pltpu.roll(spread, 0, 1, stride=1, stride_axis=0)
        table = jnp.concatenate([rolled[:, width:], rolled[:, :width]], axis=0).astype(BF16)
        product = mm(window, table)
        results.append(
            jnp.concatenate(
                [product[j * batch : (j + 1) * batch] for j in range(blocks)], axis=1
            )
        )
    out_ref[...] = jnp.swapaxes(jnp.stack(results, axis=0), 0, 1).astype(BF16)


def filter_all(signal, rim, taps):
    batch, contacts, slab = signal.shape
    width = rim.shape[2]
    rows = 16
    return pl.pallas_call(
        filter_kernel,
        grid=(contacts // rows,),
        in_specs=[
            pl.BlockSpec((batch, rows, slab), lambda i: (0, i, 0)),
            pl.BlockSpec((batch, rows, width), lambda i: (0, i, 0)),
            pl.BlockSpec((rows, 2 * width), lambda i: (i, 0)),
        ],
        out_specs=pl.BlockSpec((batch, rows, slab), lambda i: (0, i, 0)),
        out_shape=jax.ShapeDtypeStruct(signal.shape, BF16),
        compiler_params=pltpu.CompilerParams(vmem_limit_bytes=40 * 2**20),
        cost_estimate=pl.CostEstimate(
            flops=4 * batch * contacts * slab * width,
            bytes_accessed=4 * batch * contacts * slab,
            transcendentals=0,
        ),
        name="filter",
    )(signal, rim, taps)


def head_masks(width):
    lane_head = lax.broadcasted_iota(jnp.int32, (1, width), 1) // (width // HEADS)
    return [(lane_head == h).astype(F32) for h in range(HEADS)]


def forward_kernel(
    feat_ref, small_ref, wqkv_ref, wo_ref,
    out_ref, prob_ref, value_ref, kblk_ref, query_t_ref, normed_ref, normed_t_ref, mixed_ref,
    mixed_t_ref, counts, columns, v_blocks,
):
    contacts, width = feat_ref.shape
    scale = (width // HEADS) ** (-0.5)
    slots = small_ref.shape[0] - 3

    @pl.when(pl.program_id(0) == 0)
    def _():
        small = small_ref[...]
        filler = jnp.zeros((128 - small.shape[0], contacts), F32)
        turned = jnp.concatenate([small, filler], axis=0).T
        ids = lax.broadcasted_iota(jnp.int32, (contacts, contacts), 1)
        total = jnp.zeros((contacts, contacts), F32)
        for slot in range(slots):
            hit = turned[:, slot + 2 : slot + 3].astype(jnp.int32) == ids
            total = total + jnp.where(hit, small[0:1], 0.0)
        counts[...] = total.astype(BF16)
        columns[:, 0:1] = turned[:, 0:1]
        columns[:, 1:2] = turned[:, 1:2]
        columns[:, 2:3] = jnp.sum(total, axis=1, keepdims=True)

    live = columns[:, 0:1]
    coef = columns[:, 1:2]
    field = feat_ref[...]
    middle = field.astype(F32)
    beside = mm(counts[...], field)
    ready = live * (middle + coef * (beside - columns[:, 2:3] * middle))
    ready = ready.astype(BF16).astype(F32)
    mean_square = jnp.mean(ready * ready, axis=1, keepdims=True)
    normed = (ready * lax.rsqrt(mean_square + 1e-05)).astype(BF16)
    query = (mm(normed, wqkv_ref[:, :width]) * scale).astype(BF16)
    keys = mm(normed, wqkv_ref[:, width : 2 * width]).astype(BF16)
    value = mm(normed, wqkv_ref[:, 2 * width :]).astype(BF16)
    masks = [m.astype(BF16) for m in head_masks(width)]
    bias = jnp.where(small_ref[0:1, :] > 0, 0.0, -1e30)
    for h in range(HEADS):
        kblk_ref[h * contacts : (h + 1) * contacts, :] = keys * masks[h]
        v_blocks[h * contacts : (h + 1) * contacts, :] = value * masks[h]
    for h in range(HEADS):
        scores = mm(query * masks[h], keys, 1, 1) + bias
        top = jnp.max(scores, axis=1, keepdims=True)
        raised = jnp.exp(scores - top)
        share = 1.0 / jnp.sum(raised, axis=1, keepdims=True)
        prob_ref[:, h * contacts : (h + 1) * contacts] = (raised * share).astype(BF16)
    mixed = mm(prob_ref[...], v_blocks[...]).astype(BF16)
    out_ref[...] = mm(mixed, wo_ref[...]).astype(BF16)
    value_ref[...] = value
    query_t_ref[...] = query.T
    normed_ref[...] = normed
    normed_t_ref[...] = normed.T
    mixed_ref[...] = mixed
    mixed_t_ref[...] = mixed.T


def backward_kernel(
    up_ref, prob_ref, value_ref, kblk_ref, query_t_ref, normed_ref, normed_t_ref, mixed_ref,
    mixed_t_ref, wo_ref, out_ref, total, gs_all,
):
    contacts, width = up_ref.shape
    head = width // HEADS
    scale = head ** (-0.5)
    step = pl.program_id(0)

    @pl.when(step == 0)
    def _():
        total[...] = jnp.zeros_like(total)

    upstream = up_ref[...]
    normed = normed_ref[...]
    value = value_ref[...]
    back = mm(upstream, wo_ref[...], 1, 1).astype(BF16)
    back_t = back.T
    inner = back.astype(F32) * mixed_ref[...].astype(F32)
    masks = head_masks(width)
    grad_value_t = []
    grad_key_t = []
    for h in range(HEADS):
        grad_prob = mm(back * masks[h].astype(BF16), value, 1, 1)
        row_inner = jnp.sum(inner * masks[h], axis=1, keepdims=True)
        prob = prob_ref[:, h * contacts : (h + 1) * contacts]
        grad_score = (prob.astype(F32) * (grad_prob - row_inner)).astype(BF16)
        gs_all[:, h * contacts : (h + 1) * contacts] = grad_score
        grad_value_t.append(mm(back_t[h * head : (h + 1) * head], prob))
        grad_key_t.append(mm(query_t_ref[h * head : (h + 1) * head, :], grad_score))
    grad_query = (mm(gs_all[...], kblk_ref[...]) * scale).astype(BF16)
    total[0] += mm(normed_t_ref[...], grad_query)
    total[1] += mm(jnp.concatenate(grad_key_t, axis=0).astype(BF16), normed)
    total[2] += mm(jnp.concatenate(grad_value_t, axis=0).astype(BF16), normed)
    total[3] += mm(mixed_t_ref[...], upstream)

    @pl.when(step == pl.num_programs(0) - 1)
    def _():
        out_ref[0] = total[0].astype(BF16)
        out_ref[1] = total[1].T.astype(BF16)
        out_ref[2] = total[2].T.astype(BF16)
        out_ref[3] = total[3].astype(BF16)


def whole(shape):
    return pl.BlockSpec(shape, lambda i: (0,) * len(shape))


def forward(features, small, w_qkv, w_out):
    contacts, span = features.shape
    width = w_out.shape[0]
    groups = span // width
    shapes = [
        (contacts, width), (contacts, HEADS * contacts), (contacts, width),
        (HEADS * contacts, width), (width, contacts), (contacts, width), (width, contacts),
        (contacts, width), (width, contacts),
    ]
    specs = [pl.BlockSpec(shape, lambda i: (0, i)) for shape in shapes]
    return pl.pallas_call(
        forward_kernel,
        grid=(groups,),
        in_specs=[specs[0], whole(small.shape), whole(w_qkv.shape), whole(w_out.shape)],
        out_specs=specs,
        out_shape=[
            jax.ShapeDtypeStruct((shape[0], groups * shape[1]), BF16) for shape in shapes
        ],
        scratch_shapes=[
            pltpu.VMEM((contacts, contacts), BF16),
            pltpu.VMEM((contacts, 128), F32),
            pltpu.VMEM((HEADS * contacts, width), BF16),
        ],
        compiler_params=pltpu.CompilerParams(vmem_limit_bytes=48 * 2**20),
        cost_estimate=pl.CostEstimate(
            flops=groups * 5 * 10**9,
            bytes_accessed=20 * contacts * span,
            transcendentals=groups * HEADS * contacts * contacts,
        ),
        name="forward",
    )(features, small, w_qkv, w_out)


def backward(upstream, kept, w_out):
    contacts, span = upstream.shape
    width = w_out.shape[0]
    groups = span // width
    inputs = [upstream] + list(kept)
    return pl.pallas_call(
        backward_kernel,
        grid=(groups,),
        in_specs=[
            pl.BlockSpec((item.shape[0], item.shape[1] // groups), lambda i: (0, i))
            for item in inputs
        ]
        + [whole(w_out.shape)],
        out_specs=whole((4, width, width)),
        out_shape=jax.ShapeDtypeStruct((4, width, width), BF16),
        scratch_shapes=[
            pltpu.VMEM((4, width, width), F32),
            pltpu.VMEM((contacts, HEADS * contacts), BF16),
        ],
        compiler_params=pltpu.CompilerParams(vmem_limit_bytes=48 * 2**20),
        cost_estimate=pl.CostEstimate(
            flops=groups * 5 * 10**9, bytes_accessed=20 * contacts * span, transcendentals=0
        ),
        name="backward",
    )(*inputs, w_out)


def exchange(value, axis):
    return lax.all_to_all(value, axis, split_axis=0, concat_axis=0, tiled=True)


def scatter_sum(value, axis):
    count = lax.axis_size(axis)
    parts = exchange(value.astype(BF16), axis)
    parts = parts.reshape((count, value.shape[0] // count) + value.shape[1:])
    return jnp.sum(parts.astype(F32), axis=0)


def gather(value, axis):
    count = lax.axis_size(axis)
    return exchange(jnp.concatenate([value] * count, axis=0), axis)


def local(
    signal, fir_taps, neighbours, live_mask, lap_coef, w_query, w_key, w_value, w_out, cotangent
):
    batch, contacts_here, slab = signal.shape
    rim_width = fir_taps.shape[1] - 1
    width = w_query.shape[0]
    tm_count = lax.axis_size("tm")
    count = lax.axis_size("contact")
    pieces = max(1, count // batch)

    def by_group(whole):
        if pieces == 1:
            return whole
        cut = whole.reshape(batch, contacts_here, pieces, slab // pieces)
        return cut.transpose(0, 2, 1, 3).reshape(batch * pieces, contacts_here, slab // pieces)

    def to_attend(whole):
        moved = lax.all_to_all(
            by_group(whole), "contact", split_axis=0, concat_axis=1, tiled=True
        )
        held = moved.shape[0]
        return moved.transpose(1, 0, 2).reshape(moved.shape[1], held * moved.shape[2])

    rim = lax.ppermute(
        signal[:, :, slab - rim_width :], "tm", [(i, i + 1) for i in range(tm_count - 1)]
    )
    taps = jnp.pad(fir_taps.astype(F32), ((0, 0), (0, 2 * rim_width - fir_taps.shape[1])))
    filtered = filter_all(signal, rim, taps)
    features = to_attend(filtered)
    cotangent, features = lax.optimization_barrier((cotangent, features))
    upstream = to_attend(cotangent)
    small = jnp.concatenate(
        [live_mask.astype(F32)[None], lap_coef[None], neighbours.T.astype(F32),
         jnp.zeros((1, neighbours.shape[0]), F32)],
        axis=0,
    )
    attended, *kept = forward(
        features, small, jnp.concatenate([w_query, w_key, w_value], axis=1), w_out
    )
    attended, upstream = lax.optimization_barrier((attended, upstream))
    held = batch * pieces // count
    shaped = attended.reshape(attended.shape[0], held, slab // pieces).transpose(1, 0, 2)
    shaped = shaped.reshape(held * count, contacts_here, slab // pieces)
    if held > 1:
        shaped = shaped.reshape(held, count, contacts_here, slab // pieces).transpose(1, 0, 2, 3)
        shaped = shaped.reshape(count * held, contacts_here, slab // pieces)
    returned = exchange(shaped, "contact")
    if pieces > 1:
        returned = returned.reshape(batch, pieces, contacts_here, slab // pieces)
        returned = returned.transpose(0, 2, 1, 3).reshape(batch, contacts_here, slab)
    grads = backward(upstream, kept, w_out)
    grad_scale = (batch * (slab // width) * tm_count * neighbours.shape[0]) ** (-0.5)
    part = scatter_sum(grads.reshape(4 * width, width), "tm")
    part = scatter_sum(part, "contact") * grad_scale
    summed = gather(gather(part.astype(BF16), "contact"), "tm")
    return (returned, summed.astype(F32).reshape(4, width, width))


def solution(mesh):
    in_specs = (
        P(None, "contact", "tm"),
        P("contact", None),
        P(),
        P(),
        P(),
        P(),
        P(),
        P(),
        P(),
        P(None, "contact", "tm"),
    )
    out_specs = (P(None, "contact", "tm"), P())
    return jax.shard_map(local, mesh=mesh, in_specs=in_specs, out_specs=out_specs, check_vma=False)
```

```python
import functools

import jax
import jax.numpy as jnp
from jax import lax
from jax.experimental import pallas as pl
from jax.experimental.pallas import tpu as pltpu
from jax.sharding import PartitionSpec as P

HEADS = 4
F32 = jnp.float32
BF16 = jnp.bfloat16


def mm(left, right, left_dim=1, right_dim=0):
    return lax.dot_general(
        left, right, (((left_dim,), (right_dim,)), ((), ())), preferred_element_type=F32
    )


def index_spec():
    return pl.BlockSpec(memory_space=pltpu.SMEM)


def params():
    return pltpu.CompilerParams(vmem_limit_bytes=56 * 2**20)


def filter_kernel(place_ref, sig_ref, rim_ref, taps_ref, *refs):
    out_refs, kept = refs[:-1], refs[-1]
    batch, rows, slab = sig_ref.shape
    width = rim_ref.shape[2]
    blocks = slab // width
    pieces = len(out_refs) // batch
    span = slab // pieces
    signal = jnp.swapaxes(sig_ref[...].astype(F32), 0, 1)
    rim = jnp.swapaxes(rim_ref[...].astype(F32), 0, 1)
    results = []
    for row in range(rows):
        own = [signal[row, :, j * width : (j + 1) * width] for j in range(blocks)]
        current = jnp.concatenate(own, axis=0)
        before = jnp.concatenate([rim[row]] + own[:-1], axis=0)
        window = jnp.concatenate([before, current], axis=1).astype(BF16)
        spread = jnp.broadcast_to(taps_ref[row : row + 1, :], (width, 2 * width))
        rolled = pltpu.roll(spread, 0, 1, stride=1, stride_axis=0)
        table = jnp.concatenate([rolled[:, width:], rolled[:, :width]], axis=0).astype(BF16)
        product = mm(window, table)
        results.append(
            jnp.concatenate(
                [product[j * batch : (j + 1) * batch] for j in range(blocks)], axis=1
            )
        )
    filtered = jnp.swapaxes(jnp.stack(results, axis=0), 0, 1).astype(BF16)
    for index in range(batch):
        for piece in range(pieces):
            kept[index * pieces + piece] = filtered[index, :, piece * span : (piece + 1) * span]
    me = place_ref[1]
    for k, out_ref in enumerate(out_refs):
        out_ref[...] = kept[me ^ k]


def filter_all(place, signal, rim, taps, count):
    batch, contacts, slab = signal.shape
    width = rim.shape[2]
    rows = 16
    span = slab * batch // count
    return pl.pallas_call(
        filter_kernel,
        grid=(contacts // rows,),
        in_specs=[
            index_spec(),
            pl.BlockSpec((batch, rows, slab), lambda i: (0, i, 0)),
            pl.BlockSpec((batch, rows, width), lambda i: (0, i, 0)),
            pl.BlockSpec((rows, 2 * width), lambda i: (i, 0)),
        ],
        out_specs=[pl.BlockSpec((rows, span), lambda i: (i, 0))] * count,
        out_shape=[jax.ShapeDtypeStruct((contacts, span), BF16)] * count,
        scratch_shapes=[pltpu.VMEM((count, rows, span), BF16)],
        compiler_params=params(),
        cost_estimate=pl.CostEstimate(
            flops=4 * batch * contacts * slab * width,
            bytes_accessed=4 * batch * contacts * slab,
            transcendentals=0,
        ),
        name="filter",
    )(place, signal, rim, taps)


def split_kernel(place_ref, in_ref, *refs):
    out_refs, kept = refs[:-1], refs[-1]
    batch, _, slab = in_ref.shape
    pieces = len(out_refs) // batch
    span = slab // pieces
    me = place_ref[1]
    if pieces == 1:
        for k, out_ref in enumerate(out_refs):
            out_ref[...] = in_ref[me ^ k]
    else:
        for index in range(batch):
            for piece in range(pieces):
                kept[index * pieces + piece] = in_ref[index, :, piece * span : (piece + 1) * span]
        for k, out_ref in enumerate(out_refs):
            out_ref[...] = kept[me ^ k]


def split(place, value, count):
    batch, contacts, slab = value.shape
    span = slab * batch // count
    shape = (contacts, span)
    return pl.pallas_call(
        split_kernel,
        in_specs=[index_spec(), pl.BlockSpec(value.shape, lambda: (0, 0, 0))],
        out_specs=[pl.BlockSpec(shape, lambda: (0, 0))] * count,
        out_shape=[jax.ShapeDtypeStruct(shape, BF16)] * count,
        scratch_shapes=[pltpu.VMEM((count,) + shape, BF16)],
        compiler_params=params(),
        name="split",
    )(place, value)


def join_kernel(place_ref, *refs):
    in_refs, out_ref, kept = refs[:-2], refs[-2], refs[-1]
    batch, _, slab = out_ref.shape
    pieces = len(in_refs) // batch
    span = slab // pieces
    me = place_ref[1]
    if pieces == 1:
        for k, in_ref in enumerate(in_refs):
            out_ref[me ^ k] = in_ref[...]
    else:
        for k, in_ref in enumerate(in_refs):
            kept[me ^ k] = in_ref[...]
        for index in range(batch):
            for piece in range(pieces):
                out_ref[index, :, piece * span : (piece + 1) * span] = kept[index * pieces + piece]


def join(place, parts, batch):
    contacts, span = parts[0].shape
    shape = (batch, contacts, span * len(parts) // batch)
    return pl.pallas_call(
        join_kernel,
        in_specs=[index_spec()] + [pl.BlockSpec((contacts, span), lambda: (0, 0))] * len(parts),
        out_specs=pl.BlockSpec(shape, lambda: (0, 0, 0)),
        out_shape=jax.ShapeDtypeStruct(shape, BF16),
        scratch_shapes=[pltpu.VMEM((len(parts), contacts, span), BF16)],
        compiler_params=params(),
        name="join",
    )(place, *parts)


def head_masks(width):
    lane_head = lax.broadcasted_iota(jnp.int32, (1, width), 1) // (width // HEADS)
    return [(lane_head == h).astype(F32) for h in range(HEADS)]


def forward_kernel(blocks, place_ref, small_ref, wqkv_ref, wo_ref, *refs):
    feat_refs, refs = refs[:blocks], refs[blocks:]
    out_refs, refs = refs[:blocks], refs[blocks:]
    (
        prob_ref, value_ref, kblk_ref, query_t_ref, normed_ref, normed_t_ref, mixed_ref,
        mixed_t_ref, counts, columns, live_row, v_blocks,
    ) = refs
    rows, width = feat_refs[0].shape
    contacts = rows * blocks
    scale = (width // HEADS) ** (-0.5)
    slots = small_ref.shape[0] - 3

    @pl.when(pl.program_id(0) == 0)
    def _():
        me = place_ref[1]
        small = small_ref[...]
        filler = jnp.zeros((128 - small.shape[0], contacts), F32)
        columns[...] = jnp.concatenate([small, filler], axis=0).T
        turned = jnp.concatenate(
            [columns[pl.ds(pl.multiple_of((me ^ k) * rows, rows), rows), :] for k in range(blocks)],
            axis=0,
        )
        alive = turned.T[0:1]
        live_row[...] = alive
        ids = lax.broadcasted_iota(jnp.int32, (contacts, contacts), 1)
        total = jnp.zeros((contacts, contacts), F32)
        for slot in range(slots):
            here = turned[:, slot + 2 : slot + 3].astype(jnp.int32) ^ (me * rows)
            total = total + jnp.where(here == ids, alive, 0.0)
        counts[...] = total.astype(BF16)
        columns[:, 0:1] = turned[:, 0:1]
        columns[:, 1:2] = turned[:, 1:2]
        columns[:, 2:3] = jnp.sum(total, axis=1, keepdims=True)

    live = columns[:, 0:1]
    coef = columns[:, 1:2]
    field = jnp.concatenate([ref[...] for ref in feat_refs], axis=0)
    middle = field.astype(F32)
    beside = mm(counts[...], field)
    ready = live * (middle + coef * (beside - columns[:, 2:3] * middle))
    ready = ready.astype(BF16).astype(F32)
    mean_square = jnp.mean(ready * ready, axis=1, keepdims=True)
    normed = (ready * lax.rsqrt(mean_square + 1e-05)).astype(BF16)
    query = (mm(normed, wqkv_ref[:, :width]) * scale).astype(BF16)
    keys = mm(normed, wqkv_ref[:, width : 2 * width]).astype(BF16)
    value = mm(normed, wqkv_ref[:, 2 * width :]).astype(BF16)
    masks = [m.astype(BF16) for m in head_masks(width)]
    bias = jnp.where(live_row[...] > 0, 0.0, -1e30)
    for h in range(HEADS):
        kblk_ref[h * contacts : (h + 1) * contacts, :] = keys * masks[h]
        v_blocks[h * contacts : (h + 1) * contacts, :] = value * masks[h]
    for h in range(HEADS):
        scores = mm(query * masks[h], keys, 1, 1) + bias
        top = jnp.max(scores, axis=1, keepdims=True)
        raised = jnp.exp(scores - top)
        share = 1.0 / jnp.sum(raised, axis=1, keepdims=True)
        prob_ref[:, h * contacts : (h + 1) * contacts] = (raised * share).astype(BF16)
    mixed = mm(prob_ref[...], v_blocks[...]).astype(BF16)
    attended = mm(mixed, wo_ref[...]).astype(BF16)
    for k, out_ref in enumerate(out_refs):
        out_ref[...] = attended[k * rows : (k + 1) * rows]
    value_ref[...] = value
    query_t_ref[...] = query.T
    normed_ref[...] = normed
    normed_t_ref[...] = normed.T
    mixed_ref[...] = mixed
    mixed_t_ref[...] = mixed.T


def backward_kernel(blocks, place_ref, wo_ref, *refs):
    up_refs, refs = refs[:blocks], refs[blocks:]
    (
        prob_ref, value_ref, kblk_ref, query_t_ref, normed_ref, normed_t_ref, mixed_ref,
        mixed_t_ref,
    ) = refs[:8]
    out_refs, total, gs_all, chunks = refs[8:-3], refs[-3], refs[-2], refs[-1]
    contacts, width = normed_ref.shape
    head = width // HEADS
    scale = head ** (-0.5)
    step = pl.program_id(0)

    @pl.when(step == 0)
    def _():
        total[...] = jnp.zeros_like(total)

    upstream = jnp.concatenate([ref[...] for ref in up_refs], axis=0)
    normed = normed_ref[...]
    value = value_ref[...]
    back = mm(upstream, wo_ref[...], 1, 1).astype(BF16)
    back_t = back.T
    inner = back.astype(F32) * mixed_ref[...].astype(F32)
    masks = head_masks(width)
    grad_value_t = []
    grad_key_t = []
    for h in range(HEADS):
        grad_prob = mm(back * masks[h].astype(BF16), value, 1, 1)
        row_inner = jnp.sum(inner * masks[h], axis=1, keepdims=True)
        prob = prob_ref[:, h * contacts : (h + 1) * contacts]
        grad_score = (prob.astype(F32) * (grad_prob - row_inner)).astype(BF16)
        gs_all[:, h * contacts : (h + 1) * contacts] = grad_score
        grad_value_t.append(mm(back_t[h * head : (h + 1) * head], prob))
        grad_key_t.append(mm(query_t_ref[h * head : (h + 1) * head, :], grad_score))
    grad_query = (mm(gs_all[...], kblk_ref[...]) * scale).astype(BF16)
    total[0] += mm(normed_t_ref[...], grad_query)
    total[1] += mm(jnp.concatenate(grad_key_t, axis=0).astype(BF16), normed)
    total[2] += mm(jnp.concatenate(grad_value_t, axis=0).astype(BF16), normed)
    total[3] += mm(mixed_t_ref[...], upstream)

    @pl.when(step == pl.num_programs(0) - 1)
    def _():
        count, rows = chunks.shape[:2]
        parts = [total[0], total[1].T, total[2].T, total[3]]
        for c in range(count):
            first = (c * rows) % width
            chunks[c] = parts[c * rows // width][first : first + rows].astype(BF16)
        me = place_ref[0]
        for k, out_ref in enumerate(out_refs):
            out_ref[...] = chunks[me ^ k]


def whole(shape):
    return pl.BlockSpec(shape, lambda i: (0,) * len(shape))


def forward(place, features, small, w_qkv, w_out):
    blocks = len(features)
    rows, span = features[0].shape
    contacts = rows * blocks
    width = w_out.shape[0]
    groups = span // width
    shapes = [(rows, width)] * blocks + [
        (contacts, HEADS * contacts), (contacts, width),
        (HEADS * contacts, width), (width, contacts), (contacts, width), (width, contacts),
        (contacts, width), (width, contacts),
    ]
    specs = [pl.BlockSpec(shape, lambda i: (0, i)) for shape in shapes]
    results = pl.pallas_call(
        functools.partial(forward_kernel, blocks),
        grid=(groups,),
        in_specs=[index_spec(), whole(small.shape), whole(w_qkv.shape), whole(w_out.shape)]
        + specs[:blocks],
        out_specs=specs,
        out_shape=[
            jax.ShapeDtypeStruct((shape[0], groups * shape[1]), BF16) for shape in shapes
        ],
        scratch_shapes=[
            pltpu.VMEM((contacts, contacts), BF16),
            pltpu.VMEM((contacts, 128), F32),
            pltpu.VMEM((1, contacts), F32),
            pltpu.VMEM((HEADS * contacts, width), BF16),
        ],
        compiler_params=params(),
        cost_estimate=pl.CostEstimate(
            flops=groups * 5 * 10**9,
            bytes_accessed=20 * contacts * span,
            transcendentals=groups * HEADS * contacts * contacts,
        ),
        name="forward",
    )(place, small, w_qkv, w_out, *features)
    return results[:blocks], results[blocks:]


def backward(place, upstream, kept, w_out, tm_count):
    blocks = len(upstream)
    rows, span = upstream[0].shape
    contacts = rows * blocks
    width = w_out.shape[0]
    groups = span // width
    inputs = list(upstream) + list(kept)
    chunk = (4 * width // tm_count, width)
    return pl.pallas_call(
        functools.partial(backward_kernel, blocks),
        grid=(groups,),
        in_specs=[index_spec(), whole(w_out.shape)]
        + [
            pl.BlockSpec((item.shape[0], item.shape[1] // groups), lambda i: (0, i))
            for item in inputs
        ],
        out_specs=[whole(chunk)] * tm_count,
        out_shape=[jax.ShapeDtypeStruct(chunk, BF16)] * tm_count,
        scratch_shapes=[
            pltpu.VMEM((4, width, width), F32),
            pltpu.VMEM((contacts, HEADS * contacts), BF16),
            pltpu.VMEM((tm_count,) + chunk, BF16),
        ],
        compiler_params=params(),
        cost_estimate=pl.CostEstimate(
            flops=groups * 5 * 10**9, bytes_accessed=20 * contacts * span, transcendentals=0
        ),
        name="backward",
    )(place, w_out, *inputs)


def add_split(place, parts, count):
    rows, width = parts[0].shape
    piece = rows // count
    ways = len(parts)

    def body(place_ref, *refs):
        total = refs[0][...].astype(F32)
        for ref in refs[1:ways]:
            total = total + ref[...].astype(F32)
        kept = refs[-1]
        for j in range(count):
            kept[j] = total[j * piece : (j + 1) * piece]
        for k, out_ref in enumerate(refs[ways:-1]):
            out_ref[...] = kept[place_ref[1] ^ k].astype(BF16)

    return pl.pallas_call(
        body,
        in_specs=[index_spec()] + [pl.BlockSpec((rows, width), lambda: (0, 0))] * ways,
        out_specs=[pl.BlockSpec((piece, width), lambda: (0, 0))] * count,
        out_shape=[jax.ShapeDtypeStruct((piece, width), BF16)] * count,
        scratch_shapes=[pltpu.VMEM((count, piece, width), F32)],
        compiler_params=params(),
        name="add_split",
    )(place, *parts)


def place_all(place, parts, count):
    rows, width = parts[0].shape
    piece = rows // count
    ways = len(parts)

    def body(place_ref, *refs):
        out_ref = refs[-1]
        for k in range(ways):
            block = refs[k][...].astype(F32)
            for j in range(count):
                out_ref[place_ref[0] ^ k, place_ref[1] ^ j] = block[j * piece : (j + 1) * piece]

    shape = (ways, count, piece, width)
    return pl.pallas_call(
        body,
        in_specs=[index_spec()] + [pl.BlockSpec((rows, width), lambda: (0, 0))] * ways,
        out_specs=pl.BlockSpec(shape, lambda: (0, 0, 0, 0)),
        out_shape=jax.ShapeDtypeStruct(shape, F32),
        compiler_params=params(),
        name="place_all",
    )(place, *parts)


def swap(value, axis, k):
    return lax.ppermute(value, axis, [(i, i ^ k) for i in range(lax.axis_size(axis))])


def swap_all(parts, axis):
    return [parts[0]] + [swap(parts[k], axis, k) for k in range(1, len(parts))]


def local(
    signal, fir_taps, neighbours, live_mask, lap_coef, w_query, w_key, w_value, w_out, cotangent
):
    batch, contacts_here, slab = signal.shape
    rim_width = fir_taps.shape[1] - 1
    width = w_query.shape[0]
    tm_count = lax.axis_size("tm")
    count = lax.axis_size("contact")
    place = jnp.stack([lax.axis_index("tm"), lax.axis_index("contact")]).astype(jnp.int32)

    rim = lax.ppermute(
        signal[:, :, slab - rim_width :], "tm", [(i, i + 1) for i in range(tm_count - 1)]
    )
    early = count // 2
    cotangents = split(place, cotangent, count)
    upstream = swap_all(cotangents[:early], "contact")
    taps = jnp.pad(fir_taps.astype(F32), ((0, 0), (0, 2 * rim_width - fir_taps.shape[1])))
    filtered = filter_all(place, signal, rim, taps, count)
    features = swap_all(filtered, "contact")
    features, late = lax.optimization_barrier((features, cotangents[early:]))
    upstream = upstream + [swap(late[k - early], "contact", k) for k in range(early, count)]
    small = jnp.concatenate(
        [live_mask.astype(F32)[None], lap_coef[None], neighbours.T.astype(F32),
         jnp.zeros((1, neighbours.shape[0]), F32)],
        axis=0,
    )
    attended, kept = forward(
        place, features, small, jnp.concatenate([w_query, w_key, w_value], axis=1), w_out
    )
    returned = swap_all(attended, "contact")
    grads = backward(place, upstream, kept, w_out, tm_count)
    grads = swap_all(grads, "tm")
    pieces = swap_all(add_split(place, grads, count), "contact")
    grad_scale = (batch * (slab // width) * tm_count * neighbours.shape[0]) ** (-0.5)
    mine = sum(piece.astype(F32) for piece in pieces) * grad_scale
    mine = mine.astype(BF16)
    chunk = jnp.concatenate(swap_all([mine] * count, "contact"), axis=0)
    summed = place_all(place, swap_all([chunk] * tm_count, "tm"), count)
    return (join(place, returned, batch), summed.reshape(4, width, width))


def solution(mesh):
    in_specs = (
        P(None, "contact", "tm"),
        P("contact", None),
        P(),
        P(),
        P(),
        P(),
        P(),
        P(),
        P(),
        P(None, "contact", "tm"),
    )
    out_specs = (P(None, "contact", "tm"), P())
    return jax.shard_map(local, mesh=mesh, in_specs=in_specs, out_specs=out_specs, check_vma=False)
```

```python
import functools

import jax
import jax.numpy as jnp
from jax import lax
from jax.experimental import pallas as pl
from jax.experimental.pallas import tpu as pltpu
from jax.sharding import PartitionSpec as P

HEADS = 4
F32 = jnp.float32
BF16 = jnp.bfloat16


def mm(left, right, left_dim=1, right_dim=0):
    return lax.dot_general(
        left, right, (((left_dim,), (right_dim,)), ((), ())), preferred_element_type=F32
    )


def index_spec():
    return pl.BlockSpec(memory_space=pltpu.SMEM)


def params():
    return pltpu.CompilerParams(vmem_limit_bytes=56 * 2**20)


def filter_kernel(place_ref, sig_ref, rim_ref, taps_ref, *refs):
    out_refs, kept = refs[:-1], refs[-1]
    batch, rows, slab = sig_ref.shape
    width = rim_ref.shape[2]
    blocks = slab // width
    pieces = len(out_refs) // batch
    span = slab // pieces
    signal = jnp.swapaxes(sig_ref[...].astype(F32), 0, 1)
    rim = jnp.swapaxes(rim_ref[...].astype(F32), 0, 1)
    taps = taps_ref[...].astype(F32)
    first = lax.broadcasted_iota(jnp.int32, (rows, width), 1) == 0
    taps = jnp.concatenate(
        [taps[:, :width], jnp.where(first, taps[:, width : width + 1], 0.0)], axis=1
    )
    results = []
    for row in range(rows):
        own = [signal[row, :, j * width : (j + 1) * width] for j in range(blocks)]
        current = jnp.concatenate(own, axis=0)
        before = jnp.concatenate([rim[row]] + own[:-1], axis=0)
        window = jnp.concatenate([before, current], axis=1).astype(BF16)
        spread = jnp.broadcast_to(taps[row : row + 1, :], (width, 2 * width))
        rolled = pltpu.roll(spread, 0, 1, stride=1, stride_axis=0)
        table = jnp.concatenate([rolled[:, width:], rolled[:, :width]], axis=0).astype(BF16)
        product = mm(window, table)
        results.append(
            jnp.concatenate(
                [product[j * batch : (j + 1) * batch] for j in range(blocks)], axis=1
            )
        )
    filtered = jnp.swapaxes(jnp.stack(results, axis=0), 0, 1).astype(BF16)
    for index in range(batch):
        for piece in range(pieces):
            kept[index * pieces + piece] = filtered[index, :, piece * span : (piece + 1) * span]
    me = place_ref[1]
    for k, out_ref in enumerate(out_refs):
        out_ref[...] = kept[me ^ k]


def filter_all(place, signal, rim, taps, count):
    batch, contacts, slab = signal.shape
    width = rim.shape[2]
    rows = 16
    span = slab * batch // count
    return pl.pallas_call(
        filter_kernel,
        grid=(contacts // rows,),
        in_specs=[
            index_spec(),
            pl.BlockSpec((batch, rows, slab), lambda i: (0, i, 0)),
            pl.BlockSpec((batch, rows, width), lambda i: (0, i, 0)),
            pl.BlockSpec((rows, taps.shape[1]), lambda i: (i, 0)),
        ],
        out_specs=[pl.BlockSpec((rows, span), lambda i: (i, 0))] * count,
        out_shape=[jax.ShapeDtypeStruct((contacts, span), BF16)] * count,
        scratch_shapes=[pltpu.VMEM((count, rows, span), BF16)],
        compiler_params=params(),
        cost_estimate=pl.CostEstimate(
            flops=4 * batch * contacts * slab * width,
            bytes_accessed=4 * batch * contacts * slab,
            transcendentals=0,
        ),
        name="filter",
    )(place, signal, rim, taps)


def head_masks(width):
    lane_head = lax.broadcasted_iota(jnp.int32, (1, width), 1) // (width // HEADS)
    return [(lane_head == h).astype(F32) for h in range(HEADS)]


def forward_kernel(
    blocks, place_ref, nbr_ref, live_ref, coef_ref, wq_ref, wk_ref, wv_ref, wo_ref, *refs
):
    feat_refs = refs[:blocks]
    (
        out_ref, prob_ref, value_ref, keys_ref, query_t_ref, normed_ref, normed_t_ref, mixed_ref,
        mixed_t_ref, counts, columns, packed, live_row,
    ) = refs[blocks:]
    rows, width = feat_refs[0].shape
    contacts = rows * blocks
    scale = (width // HEADS) ** (-0.5)
    slots = nbr_ref.shape[0]
    me = place_ref[1]

    @pl.when(pl.program_id(0) == 0)
    def _():
        packed[...] = jnp.zeros_like(packed)
        packed[0:1, :] = live_ref[...].astype(F32)
        packed[1:2, :] = coef_ref[...]
        for slot in range(slots):
            packed[2 + slot : 3 + slot, :] = nbr_ref[slot : slot + 1, :].astype(F32)
        columns[...] = packed[...].T
        turned = jnp.concatenate(
            [columns[pl.ds(pl.multiple_of((me ^ k) * rows, rows), rows), :] for k in range(blocks)],
            axis=0,
        )
        alive = turned.T[0:1]
        live_row[...] = alive
        ids = lax.broadcasted_iota(jnp.int32, (contacts, contacts), 1)
        total = jnp.zeros((contacts, contacts), F32)
        for slot in range(slots):
            here = turned[:, slot + 2 : slot + 3].astype(jnp.int32) ^ (me * rows)
            total = total + jnp.where(here == ids, alive, 0.0)
        counts[...] = total.astype(BF16)
        columns[:, 0:1] = turned[:, 0:1]
        columns[:, 1:2] = turned[:, 1:2]
        columns[:, 2:3] = jnp.sum(total, axis=1, keepdims=True)

    live = columns[:, 0:1]
    coef = columns[:, 1:2]
    field = jnp.concatenate([ref[...] for ref in feat_refs], axis=0)
    middle = field.astype(F32)
    beside = mm(counts[...], field)
    ready = live * (middle + coef * (beside - columns[:, 2:3] * middle))
    ready = ready.astype(BF16).astype(F32)
    mean_square = jnp.mean(ready * ready, axis=1, keepdims=True)
    normed = (ready * lax.rsqrt(mean_square + 1e-05)).astype(BF16)
    query = (mm(normed, wq_ref[...]) * scale).astype(BF16)
    keys = mm(normed, wk_ref[...]).astype(BF16)
    value = mm(normed, wv_ref[...]).astype(BF16)
    value_ref[...] = value
    keys_ref[...] = keys
    query_t_ref[...] = query.T
    normed_ref[...] = normed
    normed_t_ref[...] = normed.T
    masks = [m.astype(BF16) for m in head_masks(width)]
    bias = jnp.where(live_row[...] > 0, 0.0, -1e30)
    scores = mm(query * masks[0], keys, 1, 1)
    mixed = None
    for h in range(HEADS):
        following = mm(query * masks[h + 1], keys, 1, 1) if h + 1 < HEADS else None
        scores = scores + bias
        top = jnp.max(scores, axis=1, keepdims=True)
        raised = jnp.exp(scores - top)
        share = 1.0 / jnp.sum(raised, axis=1, keepdims=True)
        prob = (raised * share).astype(BF16)
        prob_ref[:, h * contacts : (h + 1) * contacts] = prob
        part = mm(prob, value * masks[h])
        mixed = part if mixed is None else mixed + part
        scores = following
    mixed = mixed.astype(BF16)
    attended = mm(mixed, wo_ref[...]).astype(BF16)
    for k in range(blocks):
        out_ref[me ^ k] = attended[k * rows : (k + 1) * rows]
    mixed_ref[...] = mixed
    mixed_t_ref[...] = mixed.T


def backward_kernel(
    blocks, place_ref, wo_ref, up_ref, prob_ref, value_ref, keys_ref, query_t_ref, normed_ref,
    normed_t_ref, mixed_ref, mixed_t_ref, *refs,
):
    out_refs, total, chunks = refs[:-2], refs[-2], refs[-1]
    contacts, width = normed_ref.shape
    head = width // HEADS
    scale = head ** (-0.5)
    step = pl.program_id(0)

    @pl.when(step == 0)
    def _():
        total[...] = jnp.zeros_like(total)

    me = place_ref[1]
    upstream = jnp.concatenate([up_ref[me ^ k] for k in range(blocks)], axis=0)
    normed = normed_ref[...]
    value = value_ref[...]
    keys = keys_ref[...]
    back = mm(upstream, wo_ref[...], 1, 1).astype(BF16)
    back_t = back.T
    inner = back.astype(F32) * mixed_ref[...].astype(F32)
    masks = head_masks(width)
    grad_value_t = []
    grad_key_t = []
    grad_query = None
    low = [m.astype(BF16) for m in masks]
    grad_prob = mm(back * low[0], value, 1, 1)
    for h in range(HEADS):
        following = mm(back * low[h + 1], value, 1, 1) if h + 1 < HEADS else None
        row_inner = jnp.sum(inner * masks[h], axis=1, keepdims=True)
        prob = prob_ref[:, h * contacts : (h + 1) * contacts]
        grad_value_t.append(mm(back_t[h * head : (h + 1) * head], prob))
        grad_score = (prob.astype(F32) * (grad_prob - row_inner)).astype(BF16)
        grad_key_t.append(mm(query_t_ref[h * head : (h + 1) * head, :], grad_score))
        part = mm(grad_score, keys * low[h])
        grad_query = part if grad_query is None else grad_query + part
        grad_prob = following
    grad_query = (grad_query * scale).astype(BF16)
    total[0] += mm(normed_t_ref[...], grad_query)
    total[1] += mm(jnp.concatenate(grad_key_t, axis=0).astype(BF16), normed)
    total[2] += mm(jnp.concatenate(grad_value_t, axis=0).astype(BF16), normed)
    total[3] += mm(mixed_t_ref[...], upstream)

    @pl.when(step == pl.num_programs(0) - 1)
    def _():
        count, rows = chunks.shape[:2]
        parts = [total[0], total[1].T, total[2].T, total[3]]
        for c in range(count):
            first = (c * rows) % width
            chunks[c] = parts[c * rows // width][first : first + rows].astype(BF16)
        for k, out_ref in enumerate(out_refs):
            out_ref[...] = chunks[place_ref[0] ^ k]


def whole(shape):
    return pl.BlockSpec(shape, lambda i: (0,) * len(shape))


def forward(place, features, neighbours, live, coef, weights):
    blocks = len(features)
    rows, span = features[0].shape
    contacts = rows * blocks
    width = weights[0].shape[0]
    groups = span // width
    shapes = [
        (contacts, HEADS * contacts), (contacts, width),
        (contacts, width), (width, contacts), (contacts, width), (width, contacts),
        (contacts, width), (width, contacts),
    ]
    small = [neighbours, live, coef] + list(weights)
    return pl.pallas_call(
        functools.partial(forward_kernel, blocks),
        grid=(groups,),
        in_specs=[index_spec()]
        + [whole(item.shape) for item in small]
        + [pl.BlockSpec((rows, width), lambda i: (0, i))] * blocks,
        out_specs=[pl.BlockSpec((blocks, rows, width), lambda i: (0, 0, i))]
        + [pl.BlockSpec(shape, lambda i: (0, i)) for shape in shapes],
        out_shape=[jax.ShapeDtypeStruct((blocks, rows, span), BF16)]
        + [jax.ShapeDtypeStruct((shape[0], groups * shape[1]), BF16) for shape in shapes],
        scratch_shapes=[
            pltpu.VMEM((contacts, contacts), BF16),
            pltpu.VMEM((contacts, 128), F32),
            pltpu.VMEM((128, contacts), F32),
            pltpu.VMEM((1, contacts), F32),
        ],
        compiler_params=params(),
        cost_estimate=pl.CostEstimate(
            flops=groups * 5 * 10**9,
            bytes_accessed=20 * contacts * span,
            transcendentals=groups * HEADS * contacts * contacts,
        ),
        name="forward",
    )(place, *small, *features)


def backward(place, upstream, kept, w_out, tm_count):
    blocks, rows, span = upstream.shape
    contacts = rows * blocks
    width = w_out.shape[0]
    groups = span // width
    chunk = (4 * width // tm_count, width)
    return pl.pallas_call(
        functools.partial(backward_kernel, blocks),
        grid=(groups,),
        in_specs=[
            index_spec(), whole(w_out.shape),
            pl.BlockSpec((blocks, rows, width), lambda i: (0, 0, i)),
        ]
        + [
            pl.BlockSpec((item.shape[0], item.shape[1] // groups), lambda i: (0, i))
            for item in kept
        ],
        out_specs=[whole(chunk)] * tm_count,
        out_shape=[jax.ShapeDtypeStruct(chunk, BF16)] * tm_count,
        scratch_shapes=[
            pltpu.VMEM((4, width, width), F32),
            pltpu.VMEM((tm_count,) + chunk, BF16),
        ],
        compiler_params=params(),
        cost_estimate=pl.CostEstimate(
            flops=groups * 5 * 10**9, bytes_accessed=20 * contacts * span, transcendentals=0
        ),
        name="backward",
    )(place, w_out, upstream, *kept)


def place_all(place, parts):
    rows, width = parts[0].shape
    ways = len(parts)

    def body(place_ref, *refs):
        for k in range(ways):
            refs[-1][place_ref[0] ^ k] = refs[k][...].astype(F32)

    shape = (ways, rows, width)
    return pl.pallas_call(
        body,
        in_specs=[index_spec()] + [pl.BlockSpec((rows, width), lambda: (0, 0))] * ways,
        out_specs=pl.BlockSpec(shape, lambda: (0, 0, 0)),
        out_shape=jax.ShapeDtypeStruct(shape, F32),
        compiler_params=params(),
        name="place_all",
    )(place, *parts)


def swap(value, axis, k):
    return lax.ppermute(value, axis, [(i, i ^ k) for i in range(lax.axis_size(axis))])


def swap_all(parts, axis):
    return [parts[0]] + [swap(parts[k], axis, k) for k in range(1, len(parts))]


def exchange(value, axis):
    return lax.all_to_all(value, axis, split_axis=0, concat_axis=0, tiled=True)


def local(
    signal, fir_taps, neighbours, live_mask, lap_coef, w_query, w_key, w_value, w_out, cotangent
):
    batch, contacts_here, slab = signal.shape
    rim_width = fir_taps.shape[1] - 1
    width = w_query.shape[0]
    tm_count = lax.axis_size("tm")
    count = lax.axis_size("contact")
    pieces = count // batch
    span = slab // pieces
    place = jnp.stack([lax.axis_index("tm"), lax.axis_index("contact")]).astype(jnp.int32)

    if pieces > 1:
        cotangent = cotangent.reshape(batch, contacts_here, pieces, span)
        cotangent = cotangent.transpose(0, 2, 1, 3).reshape(count, contacts_here, span)
    upstream = exchange(cotangent, "contact")
    rim = lax.ppermute(
        signal[:, :, slab - rim_width :], "tm", [(i, i + 1) for i in range(tm_count - 1)]
    )
    filtered = filter_all(place, signal, rim, fir_taps, count)
    features = swap_all(filtered, "contact")
    attended, *kept = forward(
        place, features, neighbours.T, live_mask[None], lap_coef[None],
        [w_query, w_key, w_value, w_out],
    )
    returned = exchange(attended, "contact")
    grads = backward(place, upstream, kept, w_out, tm_count)
    grads = swap_all(grads, "tm")
    part = sum(piece.astype(F32) for piece in grads).astype(BF16)
    part, returned = lax.optimization_barrier((part, returned))
    part = exchange(part, "contact").reshape(count, -1, width)
    grad_scale = (batch * (slab // width) * tm_count * neighbours.shape[0]) ** (-0.5)
    mine = (jnp.sum(part.astype(F32), axis=0) * grad_scale).astype(BF16)
    chunk = exchange(jnp.concatenate([mine] * count, axis=0), "contact")
    summed = place_all(place, swap_all([chunk] * tm_count, "tm"))
    if pieces > 1:
        returned = returned.reshape(batch, pieces, contacts_here, span)
        returned = returned.transpose(0, 2, 1, 3).reshape(batch, contacts_here, slab)
    return (returned, summed.reshape(4, width, width))


def solution(mesh):
    in_specs = (
        P(None, "contact", "tm"),
        P("contact", None),
        P(),
        P(),
        P(),
        P(),
        P(),
        P(),
        P(),
        P(None, "contact", "tm"),
    )
    out_specs = (P(None, "contact", "tm"), P())
    return jax.shard_map(local, mesh=mesh, in_specs=in_specs, out_specs=out_specs, check_vma=False)
```

```python
import functools

import jax
import jax.numpy as jnp
from jax import lax
from jax.experimental import pallas as pl
from jax.experimental.pallas import tpu as pltpu
from jax.sharding import PartitionSpec as P

HEADS = 4
F32 = jnp.float32
BF16 = jnp.bfloat16


def mm(left, right, left_dim=1, right_dim=0):
    return lax.dot_general(
        left, right, (((left_dim,), (right_dim,)), ((), ())), preferred_element_type=F32
    )


def index_spec():
    return pl.BlockSpec(memory_space=pltpu.SMEM)


def params():
    return pltpu.CompilerParams(vmem_limit_bytes=56 * 2**20)


def filter_kernel(place_ref, sig_ref, rim_ref, taps_ref, *refs):
    out_refs, kept = refs[:-1], refs[-1]
    batch, rows, slab = sig_ref.shape
    width = rim_ref.shape[2]
    blocks = slab // width
    pieces = len(out_refs) // batch
    span = slab // pieces
    signal = jnp.swapaxes(sig_ref[...].astype(F32), 0, 1)
    rim = jnp.swapaxes(rim_ref[...].astype(F32), 0, 1)
    taps = taps_ref[...].astype(F32)
    first = lax.broadcasted_iota(jnp.int32, (rows, width), 1) == 0
    taps = jnp.concatenate(
        [taps[:, :width], jnp.where(first, taps[:, width : width + 1], 0.0)], axis=1
    )
    results = []
    for row in range(rows):
        own = [signal[row, :, j * width : (j + 1) * width] for j in range(blocks)]
        current = jnp.concatenate(own, axis=0)
        before = jnp.concatenate([rim[row]] + own[:-1], axis=0)
        window = jnp.concatenate([before, current], axis=1).astype(BF16)
        spread = jnp.broadcast_to(taps[row : row + 1, :], (width, 2 * width))
        rolled = pltpu.roll(spread, 0, 1, stride=1, stride_axis=0)
        table = jnp.concatenate([rolled[:, width:], rolled[:, :width]], axis=0).astype(BF16)
        product = mm(window, table)
        results.append(
            jnp.concatenate(
                [product[j * batch : (j + 1) * batch] for j in range(blocks)], axis=1
            )
        )
    filtered = jnp.swapaxes(jnp.stack(results, axis=0), 0, 1).astype(BF16)
    for index in range(batch):
        for piece in range(pieces):
            kept[index * pieces + piece] = filtered[index, :, piece * span : (piece + 1) * span]
    me = place_ref[1]
    for k, out_ref in enumerate(out_refs):
        out_ref[...] = kept[me ^ k]


def filter_all(place, signal, rim, taps, count):
    batch, contacts, slab = signal.shape
    width = rim.shape[2]
    rows = 16
    span = slab * batch // count
    return pl.pallas_call(
        filter_kernel,
        grid=(contacts // rows,),
        in_specs=[
            index_spec(),
            pl.BlockSpec((batch, rows, slab), lambda i: (0, i, 0)),
            pl.BlockSpec((batch, rows, width), lambda i: (0, i, 0)),
            pl.BlockSpec((rows, taps.shape[1]), lambda i: (i, 0)),
        ],
        out_specs=[pl.BlockSpec((rows, span), lambda i: (i, 0))] * count,
        out_shape=[jax.ShapeDtypeStruct((contacts, span), BF16)] * count,
        scratch_shapes=[pltpu.VMEM((count, rows, span), BF16)],
        compiler_params=params(),
        cost_estimate=pl.CostEstimate(
            flops=4 * batch * contacts * slab * width,
            bytes_accessed=4 * batch * contacts * slab,
            transcendentals=0,
        ),
        name="filter",
    )(place, signal, rim, taps)


def head_masks(width):
    lane_head = lax.broadcasted_iota(jnp.int32, (1, width), 1) // (width // HEADS)
    return [(lane_head == h).astype(F32) for h in range(HEADS)]


def forward_kernel(
    blocks, place_ref, nbr_ref, live_ref, coef_ref, wq_ref, wk_ref, wv_ref, wo_ref, *refs
):
    feat_refs = refs[:blocks]
    (
        out_ref, prob_ref, value_ref, keys_ref, query_t_ref, normed_ref, normed_t_ref, mixed_ref,
        mixed_t_ref, counts, columns, packed, live_row,
    ) = refs[blocks:]
    rows, width = feat_refs[0].shape
    contacts = rows * blocks
    scale = (width // HEADS) ** (-0.5)
    slots = nbr_ref.shape[0]
    me = place_ref[1]

    @pl.when(pl.program_id(0) == 0)
    def _():
        packed[...] = jnp.zeros_like(packed)
        packed[0:1, :] = live_ref[...].astype(F32)
        packed[1:2, :] = coef_ref[...]
        for slot in range(slots):
            packed[2 + slot : 3 + slot, :] = nbr_ref[slot : slot + 1, :].astype(F32)
        columns[...] = packed[...].T
        turned = jnp.concatenate(
            [columns[pl.ds(pl.multiple_of((me ^ k) * rows, rows), rows), :] for k in range(blocks)],
            axis=0,
        )
        alive = turned.T[0:1]
        live_row[...] = alive
        ids = lax.broadcasted_iota(jnp.int32, (contacts, contacts), 1)
        total = jnp.zeros((contacts, contacts), F32)
        for slot in range(slots):
            here = turned[:, slot + 2 : slot + 3].astype(jnp.int32) ^ (me * rows)
            total = total + jnp.where(here == ids, alive, 0.0)
        counts[...] = total.astype(BF16)
        columns[:, 0:1] = turned[:, 0:1]
        columns[:, 1:2] = turned[:, 1:2]
        columns[:, 2:3] = jnp.sum(total, axis=1, keepdims=True)

    live = columns[:, 0:1]
    coef = columns[:, 1:2]
    field = jnp.concatenate([ref[...] for ref in feat_refs], axis=0)
    middle = field.astype(F32)
    beside = mm(counts[...], field)
    ready = live * (middle + coef * (beside - columns[:, 2:3] * middle))
    ready = ready.astype(BF16).astype(F32)
    mean_square = jnp.mean(ready * ready, axis=1, keepdims=True)
    normed = (ready * lax.rsqrt(mean_square + 1e-05)).astype(BF16)
    query = (mm(normed, wq_ref[...]) * scale).astype(BF16)
    keys = mm(normed, wk_ref[...]).astype(BF16)
    value = mm(normed, wv_ref[...]).astype(BF16)
    value_ref[...] = value
    keys_ref[...] = keys
    query_t_ref[...] = query.T
    normed_ref[...] = normed
    normed_t_ref[...] = normed.T
    masks = [m.astype(BF16) for m in head_masks(width)]
    bias = jnp.where(live_row[...] > 0, 0.0, -1e30)
    scores = mm(query * masks[0], keys, 1, 1)
    mixed = None
    for h in range(HEADS):
        following = mm(query * masks[h + 1], keys, 1, 1) if h + 1 < HEADS else None
        scores = scores + bias
        top = jnp.max(scores, axis=1, keepdims=True)
        raised = jnp.exp(scores - top)
        share = 1.0 / jnp.sum(raised, axis=1, keepdims=True)
        prob = (raised * share).astype(BF16)
        prob_ref[:, h * contacts : (h + 1) * contacts] = prob
        part = mm(prob, value * masks[h])
        mixed = part if mixed is None else mixed + part
        scores = following
    mixed = mixed.astype(BF16)
    attended = mm(mixed, wo_ref[...]).astype(BF16)
    for k in range(blocks):
        out_ref[me ^ k] = attended[k * rows : (k + 1) * rows]
    mixed_ref[...] = mixed
    mixed_t_ref[...] = mixed.T


def backward_kernel(
    blocks, place_ref, wo_ref, up_ref, late_ref, prob_ref, value_ref, keys_ref, query_t_ref, normed_ref,
    normed_t_ref, mixed_ref, mixed_t_ref, *refs,
):
    out_refs, total, chunks = refs[:-2], refs[-2], refs[-1]
    contacts, width = normed_ref.shape
    head = width // HEADS
    scale = head ** (-0.5)
    step = pl.program_id(0)

    @pl.when(step == 0)
    def _():
        total[...] = jnp.zeros_like(total)

    me = place_ref[1]
    upstream = jnp.concatenate(
        [ref[me ^ k] for k in range(blocks) for ref in (up_ref, late_ref)], axis=0
    )
    normed = normed_ref[...]
    value = value_ref[...]
    keys = keys_ref[...]
    back = mm(upstream, wo_ref[...], 1, 1).astype(BF16)
    back_t = back.T
    inner = back.astype(F32) * mixed_ref[...].astype(F32)
    masks = head_masks(width)
    grad_value_t = []
    grad_key_t = []
    grad_query = None
    low = [m.astype(BF16) for m in masks]
    grad_prob = mm(back * low[0], value, 1, 1)
    for h in range(HEADS):
        following = mm(back * low[h + 1], value, 1, 1) if h + 1 < HEADS else None
        row_inner = jnp.sum(inner * masks[h], axis=1, keepdims=True)
        prob = prob_ref[:, h * contacts : (h + 1) * contacts]
        grad_value_t.append(mm(back_t[h * head : (h + 1) * head], prob))
        grad_score = (prob.astype(F32) * (grad_prob - row_inner)).astype(BF16)
        grad_key_t.append(mm(query_t_ref[h * head : (h + 1) * head, :], grad_score))
        part = mm(grad_score, keys * low[h])
        grad_query = part if grad_query is None else grad_query + part
        grad_prob = following
    grad_query = (grad_query * scale).astype(BF16)
    total[0] += mm(normed_t_ref[...], grad_query)
    total[1] += mm(jnp.concatenate(grad_key_t, axis=0).astype(BF16), normed)
    total[2] += mm(jnp.concatenate(grad_value_t, axis=0).astype(BF16), normed)
    total[3] += mm(mixed_t_ref[...], upstream)

    @pl.when(step == pl.num_programs(0) - 1)
    def _():
        count, rows = chunks.shape[:2]
        parts = [total[0], total[1].T, total[2].T, total[3]]
        for c in range(count):
            first = (c * rows) % width
            chunks[c] = parts[c * rows // width][first : first + rows].astype(BF16)
        for k, out_ref in enumerate(out_refs):
            out_ref[...] = chunks[place_ref[0] ^ k]


def whole(shape):
    return pl.BlockSpec(shape, lambda i: (0,) * len(shape))


def forward(place, features, neighbours, live, coef, weights):
    blocks = len(features)
    rows, span = features[0].shape
    contacts = rows * blocks
    width = weights[0].shape[0]
    groups = span // width
    shapes = [
        (contacts, HEADS * contacts), (contacts, width),
        (contacts, width), (width, contacts), (contacts, width), (width, contacts),
        (contacts, width), (width, contacts),
    ]
    small = [neighbours, live, coef] + list(weights)
    return pl.pallas_call(
        functools.partial(forward_kernel, blocks),
        grid=(groups,),
        in_specs=[index_spec()]
        + [whole(item.shape) for item in small]
        + [pl.BlockSpec((rows, width), lambda i: (0, i))] * blocks,
        out_specs=[pl.BlockSpec((blocks, rows, width), lambda i: (0, 0, i))]
        + [pl.BlockSpec(shape, lambda i: (0, i)) for shape in shapes],
        out_shape=[jax.ShapeDtypeStruct((blocks, rows, span), BF16)]
        + [jax.ShapeDtypeStruct((shape[0], groups * shape[1]), BF16) for shape in shapes],
        scratch_shapes=[
            pltpu.VMEM((contacts, contacts), BF16),
            pltpu.VMEM((contacts, 128), F32),
            pltpu.VMEM((128, contacts), F32),
            pltpu.VMEM((1, contacts), F32),
        ],
        compiler_params=params(),
        cost_estimate=pl.CostEstimate(
            flops=groups * 5 * 10**9,
            bytes_accessed=20 * contacts * span,
            transcendentals=groups * HEADS * contacts * contacts,
        ),
        name="forward",
    )(place, *small, *features)


def backward(place, upstream, late, kept, w_out, tm_count):
    blocks, rows, span = upstream.shape
    contacts = 2 * rows * blocks
    width = w_out.shape[0]
    groups = span // width
    chunk = (4 * width // tm_count, width)
    return pl.pallas_call(
        functools.partial(backward_kernel, blocks),
        grid=(groups,),
        in_specs=[
            index_spec(), whole(w_out.shape),
            pl.BlockSpec((blocks, rows, width), lambda i: (0, 0, i)),
            pl.BlockSpec((blocks, rows, width), lambda i: (0, 0, i)),
        ]
        + [
            pl.BlockSpec((item.shape[0], item.shape[1] // groups), lambda i: (0, i))
            for item in kept
        ],
        out_specs=[whole(chunk)] * tm_count,
        out_shape=[jax.ShapeDtypeStruct(chunk, BF16)] * tm_count,
        scratch_shapes=[
            pltpu.VMEM((4, width, width), F32),
            pltpu.VMEM((tm_count,) + chunk, BF16),
        ],
        compiler_params=params(),
        cost_estimate=pl.CostEstimate(
            flops=groups * 5 * 10**9, bytes_accessed=20 * contacts * span, transcendentals=0
        ),
        name="backward",
    )(place, w_out, upstream, late, *kept)


def place_all(place, parts):
    rows, width = parts[0].shape
    ways = len(parts)

    def body(place_ref, *refs):
        for k in range(ways):
            refs[-1][place_ref[0] ^ k] = refs[k][...].astype(F32)

    shape = (ways, rows, width)
    return pl.pallas_call(
        body,
        in_specs=[index_spec()] + [pl.BlockSpec((rows, width), lambda: (0, 0))] * ways,
        out_specs=pl.BlockSpec(shape, lambda: (0, 0, 0)),
        out_shape=jax.ShapeDtypeStruct(shape, F32),
        compiler_params=params(),
        name="place_all",
    )(place, *parts)


def swap(value, axis, k):
    return lax.ppermute(value, axis, [(i, i ^ k) for i in range(lax.axis_size(axis))])


def swap_all(parts, axis):
    return [parts[0]] + [swap(parts[k], axis, k) for k in range(1, len(parts))]


def exchange(value, axis):
    return lax.all_to_all(value, axis, split_axis=0, concat_axis=0, tiled=True)


def local(
    signal, fir_taps, neighbours, live_mask, lap_coef, w_query, w_key, w_value, w_out, cotangent
):
    batch, contacts_here, slab = signal.shape
    rim_width = fir_taps.shape[1] - 1
    width = w_query.shape[0]
    tm_count = lax.axis_size("tm")
    count = lax.axis_size("contact")
    pieces = count // batch
    span = slab // pieces
    place = jnp.stack([lax.axis_index("tm"), lax.axis_index("contact")]).astype(jnp.int32)

    if pieces > 1:
        cotangent = cotangent.reshape(batch, contacts_here, pieces, span)
        cotangent = cotangent.transpose(0, 2, 1, 3).reshape(count, contacts_here, span)
    half = contacts_here // 2
    upstream = exchange(cotangent[:, :half], "contact")
    rim = lax.ppermute(
        signal[:, :, slab - rim_width :], "tm", [(i, i + 1) for i in range(tm_count - 1)]
    )
    filtered = filter_all(place, signal, rim, fir_taps, count)
    features = swap_all(filtered, "contact")
    features, upstream, late = lax.optimization_barrier(
        (features, upstream, cotangent[:, half:])
    )
    late = exchange(late, "contact")
    attended, *kept = forward(
        place, features, neighbours.T, live_mask[None], lap_coef[None],
        [w_query, w_key, w_value, w_out],
    )
    returned = exchange(attended, "contact")
    grads = backward(place, upstream, late, kept, w_out, tm_count)
    grads = swap_all(grads, "tm")
    part = sum(piece.astype(F32) for piece in grads).astype(BF16)
    part, _ = lax.optimization_barrier((part, returned))
    part = exchange(part, "contact").reshape(count, -1, width)
    grad_scale = (batch * (slab // width) * tm_count * neighbours.shape[0]) ** (-0.5)
    mine = (jnp.sum(part.astype(F32), axis=0) * grad_scale).astype(BF16)
    chunk = exchange(jnp.concatenate([mine] * count, axis=0), "contact")
    summed = place_all(place, swap_all([chunk] * tm_count, "tm"))
    if pieces > 1:
        returned = returned.reshape(batch, pieces, contacts_here, span)
        returned = returned.transpose(0, 2, 1, 3).reshape(batch, contacts_here, slab)
    return (returned, summed.reshape(4, width, width))


def solution(mesh):
    in_specs = (
        P(None, "contact", "tm"),
        P("contact", None),
        P(),
        P(),
        P(),
        P(),
        P(),
        P(),
        P(),
        P(None, "contact", "tm"),
    )
    out_specs = (P(None, "contact", "tm"), P())
    return jax.shard_map(local, mesh=mesh, in_specs=in_specs, out_specs=out_specs, check_vma=False)
```

```python
import functools

import jax
import jax.numpy as jnp
from jax import lax
from jax.experimental import pallas as pl
from jax.experimental.pallas import tpu as pltpu
from jax.sharding import PartitionSpec as P

HEADS = 4
F32 = jnp.float32
BF16 = jnp.bfloat16


def mm(left, right, left_dim=1, right_dim=0):
    return lax.dot_general(
        left, right, (((left_dim,), (right_dim,)), ((), ())), preferred_element_type=F32
    )


def index_spec():
    return pl.BlockSpec(memory_space=pltpu.SMEM)


def params():
    return pltpu.CompilerParams(vmem_limit_bytes=56 * 2**20)


def filter_kernel(place_ref, sig_ref, rim_ref, taps_ref, *refs):
    out_refs, kept = refs[:-1], refs[-1]
    batch, rows, slab = sig_ref.shape
    width = rim_ref.shape[2]
    blocks = slab // width
    pieces = len(out_refs) // batch
    span = slab // pieces
    signal = jnp.swapaxes(sig_ref[...].astype(F32), 0, 1)
    rim = jnp.swapaxes(rim_ref[...].astype(F32), 0, 1)
    taps = taps_ref[...].astype(F32)
    first = lax.broadcasted_iota(jnp.int32, (rows, width), 1) == 0
    taps = jnp.concatenate(
        [taps[:, :width], jnp.where(first, taps[:, width : width + 1], 0.0)], axis=1
    )
    results = []
    for row in range(rows):
        own = [signal[row, :, j * width : (j + 1) * width] for j in range(blocks)]
        current = jnp.concatenate(own, axis=0)
        before = jnp.concatenate([rim[row]] + own[:-1], axis=0)
        window = jnp.concatenate([before, current], axis=1).astype(BF16)
        spread = jnp.broadcast_to(taps[row : row + 1, :], (width, 2 * width))
        rolled = pltpu.roll(spread, 0, 1, stride=1, stride_axis=0)
        table = jnp.concatenate([rolled[:, width:], rolled[:, :width]], axis=0).astype(BF16)
        product = mm(window, table)
        results.append(
            jnp.concatenate(
                [product[j * batch : (j + 1) * batch] for j in range(blocks)], axis=1
            )
        )
    filtered = jnp.swapaxes(jnp.stack(results, axis=0), 0, 1).astype(BF16)
    for index in range(batch):
        for piece in range(pieces):
            kept[index * pieces + piece] = filtered[index, :, piece * span : (piece + 1) * span]
    me = place_ref[1]
    for k, out_ref in enumerate(out_refs):
        out_ref[...] = kept[me ^ k]


def filter_all(place, signal, rim, taps, count):
    batch, contacts, slab = signal.shape
    width = rim.shape[2]
    rows = 16
    span = slab * batch // count
    return pl.pallas_call(
        filter_kernel,
        grid=(contacts // rows,),
        in_specs=[
            index_spec(),
            pl.BlockSpec((batch, rows, slab), lambda i: (0, i, 0)),
            pl.BlockSpec((batch, rows, width), lambda i: (0, i, 0)),
            pl.BlockSpec((rows, taps.shape[1]), lambda i: (i, 0)),
        ],
        out_specs=[pl.BlockSpec((rows, span), lambda i: (i, 0))] * count,
        out_shape=[jax.ShapeDtypeStruct((contacts, span), BF16)] * count,
        scratch_shapes=[pltpu.VMEM((count, rows, span), BF16)],
        compiler_params=params(),
        cost_estimate=pl.CostEstimate(
            flops=4 * batch * contacts * slab * width,
            bytes_accessed=4 * batch * contacts * slab,
            transcendentals=0,
        ),
        name="filter",
    )(place, signal, rim, taps)


def head_masks(width):
    lane_head = lax.broadcasted_iota(jnp.int32, (1, width), 1) // (width // HEADS)
    return [(lane_head == h).astype(F32) for h in range(HEADS)]


def forward_kernel(
    blocks, place_ref, nbr_ref, live_ref, coef_ref, wq_ref, wk_ref, wv_ref, wo_ref, *refs
):
    feat_refs = refs[:blocks]
    (
        out_ref, prob_ref, value_ref, keys_ref, query_t_ref, normed_ref, normed_t_ref, mixed_ref,
        mixed_t_ref, counts, columns, packed, live_row,
    ) = refs[blocks:]
    rows, width = feat_refs[0].shape
    contacts = rows * blocks
    scale = (width // HEADS) ** (-0.5)
    slots = nbr_ref.shape[0]
    me = place_ref[1]

    @pl.when(pl.program_id(0) == 0)
    def _():
        packed[...] = jnp.zeros_like(packed)
        packed[0:1, :] = live_ref[...].astype(F32)
        packed[1:2, :] = coef_ref[...]
        for slot in range(slots):
            packed[2 + slot : 3 + slot, :] = nbr_ref[slot : slot + 1, :].astype(F32)
        columns[...] = packed[...].T
        turned = jnp.concatenate(
            [columns[pl.ds(pl.multiple_of((me ^ k) * rows, rows), rows), :] for k in range(blocks)],
            axis=0,
        )
        alive = turned.T[0:1]
        live_row[...] = alive
        ids = lax.broadcasted_iota(jnp.int32, (contacts, contacts), 1)
        total = jnp.zeros((contacts, contacts), F32)
        for slot in range(slots):
            here = turned[:, slot + 2 : slot + 3].astype(jnp.int32) ^ (me * rows)
            total = total + jnp.where(here == ids, alive, 0.0)
        counts[...] = total.astype(BF16)
        columns[:, 0:1] = turned[:, 0:1]
        columns[:, 1:2] = turned[:, 1:2]
        columns[:, 2:3] = jnp.sum(total, axis=1, keepdims=True)

    live = columns[:, 0:1]
    coef = columns[:, 1:2]
    field = jnp.concatenate([ref[...] for ref in feat_refs], axis=0)
    middle = field.astype(F32)
    beside = mm(counts[...], field)
    ready = live * (middle + coef * (beside - columns[:, 2:3] * middle))
    ready = ready.astype(BF16).astype(F32)
    mean_square = jnp.mean(ready * ready, axis=1, keepdims=True)
    normed = (ready * lax.rsqrt(mean_square + 1e-05)).astype(BF16)
    query = (mm(normed, wq_ref[...]) * scale).astype(BF16)
    keys = mm(normed, wk_ref[...]).astype(BF16)
    value = mm(normed, wv_ref[...]).astype(BF16)
    value_ref[...] = value
    keys_ref[...] = keys
    query_t_ref[...] = query.T
    normed_ref[...] = normed
    normed_t_ref[...] = normed.T
    masks = [m.astype(BF16) for m in head_masks(width)]
    bias = jnp.where(live_row[...] > 0, 0.0, -1e30)
    scores = mm(query * masks[0], keys, 1, 1)
    mixed = None
    for h in range(HEADS):
        following = mm(query * masks[h + 1], keys, 1, 1) if h + 1 < HEADS else None
        scores = scores + bias
        top = jnp.max(scores, axis=1, keepdims=True)
        raised = jnp.exp(scores - top)
        share = 1.0 / jnp.sum(raised, axis=1, keepdims=True)
        prob = (raised * share).astype(BF16)
        prob_ref[:, h * contacts : (h + 1) * contacts] = prob
        part = mm(prob, value * masks[h])
        mixed = part if mixed is None else mixed + part
        scores = following
    mixed = mixed.astype(BF16)
    attended = mm(mixed, wo_ref[...]).astype(BF16)
    for k in range(blocks):
        out_ref[me ^ k] = attended[k * rows : (k + 1) * rows]
    mixed_ref[...] = mixed
    mixed_t_ref[...] = mixed.T


def backward_kernel(
    blocks, place_ref, wo_ref, up_ref, prob_ref, value_ref, keys_ref, query_t_ref, normed_ref,
    normed_t_ref, mixed_ref, mixed_t_ref, *refs,
):
    out_refs, total, chunks = refs[:-2], refs[-2], refs[-1]
    contacts, width = normed_ref.shape
    head = width // HEADS
    scale = head ** (-0.5)
    step = pl.program_id(0)

    @pl.when(step == 0)
    def _():
        total[...] = jnp.zeros_like(total)

    me = place_ref[1]
    upstream = jnp.concatenate([up_ref[me ^ k] for k in range(blocks)], axis=0)
    normed = normed_ref[...]
    value = value_ref[...]
    keys = keys_ref[...]
    back = mm(upstream, wo_ref[...], 1, 1).astype(BF16)
    back_t = back.T
    inner = back.astype(F32) * mixed_ref[...].astype(F32)
    masks = head_masks(width)
    grad_value_t = []
    grad_key_t = []
    grad_query = None
    low = [m.astype(BF16) for m in masks]
    grad_prob = mm(back * low[0], value, 1, 1)
    for h in range(HEADS):
        following = mm(back * low[h + 1], value, 1, 1) if h + 1 < HEADS else None
        row_inner = jnp.sum(inner * masks[h], axis=1, keepdims=True)
        prob = prob_ref[:, h * contacts : (h + 1) * contacts]
        grad_value_t.append(mm(back_t[h * head : (h + 1) * head], prob))
        grad_score = (prob.astype(F32) * (grad_prob - row_inner)).astype(BF16)
        grad_key_t.append(mm(query_t_ref[h * head : (h + 1) * head, :], grad_score))
        part = mm(grad_score, keys * low[h])
        grad_query = part if grad_query is None else grad_query + part
        grad_prob = following
    grad_query = (grad_query * scale).astype(BF16)
    total[0] += mm(normed_t_ref[...], grad_query)
    total[1] += mm(jnp.concatenate(grad_key_t, axis=0).astype(BF16), normed)
    total[2] += mm(jnp.concatenate(grad_value_t, axis=0).astype(BF16), normed)
    total[3] += mm(mixed_t_ref[...], upstream)

    @pl.when(step == pl.num_programs(0) - 1)
    def _():
        count, rows = chunks.shape[:2]
        parts = [total[0], total[1].T, total[2].T, total[3]]
        for c in range(count):
            first = (c * rows) % width
            chunks[c] = parts[c * rows // width][first : first + rows].astype(BF16)
        for k, out_ref in enumerate(out_refs):
            out_ref[...] = chunks[place_ref[0] ^ k]


def whole(shape):
    return pl.BlockSpec(shape, lambda i: (0,) * len(shape))


def forward(place, features, neighbours, live, coef, weights):
    blocks = len(features)
    rows, span = features[0].shape
    contacts = rows * blocks
    width = weights[0].shape[0]
    groups = span // width
    shapes = [
        (contacts, HEADS * contacts), (contacts, width),
        (contacts, width), (width, contacts), (contacts, width), (width, contacts),
        (contacts, width), (width, contacts),
    ]
    small = [neighbours, live, coef] + list(weights)
    return pl.pallas_call(
        functools.partial(forward_kernel, blocks),
        grid=(groups,),
        in_specs=[index_spec()]
        + [whole(item.shape) for item in small]
        + [pl.BlockSpec((rows, width), lambda i: (0, i))] * blocks,
        out_specs=[pl.BlockSpec((blocks, rows, width), lambda i: (0, 0, i))]
        + [pl.BlockSpec(shape, lambda i: (0, i)) for shape in shapes],
        out_shape=[jax.ShapeDtypeStruct((blocks, rows, span), BF16)]
        + [jax.ShapeDtypeStruct((shape[0], groups * shape[1]), BF16) for shape in shapes],
        scratch_shapes=[
            pltpu.VMEM((contacts, contacts), BF16),
            pltpu.VMEM((contacts, 128), F32),
            pltpu.VMEM((128, contacts), F32),
            pltpu.VMEM((1, contacts), F32),
        ],
        compiler_params=params(),
        cost_estimate=pl.CostEstimate(
            flops=groups * 5 * 10**9,
            bytes_accessed=20 * contacts * span,
            transcendentals=groups * HEADS * contacts * contacts,
        ),
        name="forward",
    )(place, *small, *features)


def backward(place, upstream, kept, w_out, tm_count):
    blocks, rows, span = upstream.shape
    contacts = rows * blocks
    width = w_out.shape[0]
    groups = span // width
    chunk = (4 * width // tm_count, width)
    return pl.pallas_call(
        functools.partial(backward_kernel, blocks),
        grid=(groups,),
        in_specs=[
            index_spec(), whole(w_out.shape),
            pl.BlockSpec((blocks, rows, width), lambda i: (0, 0, i)),
        ]
        + [
            pl.BlockSpec((item.shape[0], item.shape[1] // groups), lambda i: (0, i))
            for item in kept
        ],
        out_specs=[whole(chunk)] * tm_count,
        out_shape=[jax.ShapeDtypeStruct(chunk, BF16)] * tm_count,
        scratch_shapes=[
            pltpu.VMEM((4, width, width), F32),
            pltpu.VMEM((tm_count,) + chunk, BF16),
        ],
        compiler_params=params(),
        cost_estimate=pl.CostEstimate(
            flops=groups * 5 * 10**9, bytes_accessed=20 * contacts * span, transcendentals=0
        ),
        name="backward",
    )(place, w_out, upstream, *kept)


def place_all(place, parts):
    rows, width = parts[0].shape
    ways = len(parts)

    def body(place_ref, *refs):
        for k in range(ways):
            refs[-1][place_ref[0] ^ k] = refs[k][...].astype(F32)

    shape = (ways, rows, width)
    return pl.pallas_call(
        body,
        in_specs=[index_spec()] + [pl.BlockSpec((rows, width), lambda: (0, 0))] * ways,
        out_specs=pl.BlockSpec(shape, lambda: (0, 0, 0)),
        out_shape=jax.ShapeDtypeStruct(shape, F32),
        compiler_params=params(),
        name="place_all",
    )(place, *parts)


def swap(value, axis, k):
    return lax.ppermute(value, axis, [(i, i ^ k) for i in range(lax.axis_size(axis))])


def swap_all(parts, axis):
    return [parts[0]] + [swap(parts[k], axis, k) for k in range(1, len(parts))]


def exchange(value, axis):
    return lax.all_to_all(value, axis, split_axis=0, concat_axis=0, tiled=True)


def local(
    signal, fir_taps, neighbours, live_mask, lap_coef, w_query, w_key, w_value, w_out, cotangent
):
    batch, contacts_here, slab = signal.shape
    rim_width = fir_taps.shape[1] - 1
    width = w_query.shape[0]
    tm_count = lax.axis_size("tm")
    count = lax.axis_size("contact")
    pieces = count // batch
    span = slab // pieces
    place = jnp.stack([lax.axis_index("tm"), lax.axis_index("contact")]).astype(jnp.int32)

    if pieces > 1:
        cotangent = cotangent.reshape(batch, contacts_here, pieces, span)
        cotangent = cotangent.transpose(0, 2, 1, 3).reshape(count, contacts_here, span)
    rim = lax.ppermute(
        signal[:, :, slab - rim_width :], "tm", [(i, i + 1) for i in range(tm_count - 1)]
    )
    filtered = filter_all(place, signal, rim, fir_taps, count)
    features = swap_all(filtered, "contact")
    features, cotangent = lax.optimization_barrier((features, cotangent))
    upstream = exchange(cotangent, "contact")
    attended, *kept = forward(
        place, features, neighbours.T, live_mask[None], lap_coef[None],
        [w_query, w_key, w_value, w_out],
    )
    returned = exchange(attended, "contact")
    grads = backward(place, upstream, kept, w_out, tm_count)
    grads = swap_all(grads, "tm")
    part = sum(piece.astype(F32) for piece in grads).astype(BF16)
    part, _ = lax.optimization_barrier((part, returned))
    part = exchange(part, "contact").reshape(count, -1, width)
    grad_scale = (batch * (slab // width) * tm_count * neighbours.shape[0]) ** (-0.5)
    mine = (jnp.sum(part.astype(F32), axis=0) * grad_scale).astype(BF16)
    chunk = exchange(jnp.concatenate([mine] * count, axis=0), "contact")
    summed = place_all(place, swap_all([chunk] * tm_count, "tm"))
    if pieces > 1:
        returned = returned.reshape(batch, pieces, contacts_here, span)
        returned = returned.transpose(0, 2, 1, 3).reshape(batch, contacts_here, slab)
    return (returned, summed.reshape(4, width, width))


def solution(mesh):
    in_specs = (
        P(None, "contact", "tm"),
        P("contact", None),
        P(),
        P(),
        P(),
        P(),
        P(),
        P(),
        P(),
        P(None, "contact", "tm"),
    )
    out_specs = (P(None, "contact", "tm"), P())
    return jax.shard_map(local, mesh=mesh, in_specs=in_specs, out_specs=out_specs, check_vma=False)
```

```python
import functools

import jax
import jax.numpy as jnp
from jax import lax
from jax.experimental import pallas as pl
from jax.experimental.pallas import tpu as pltpu
from jax.sharding import PartitionSpec as P

HEADS = 4
F32 = jnp.float32
BF16 = jnp.bfloat16


def mm(left, right, left_dim=1, right_dim=0):
    return lax.dot_general(
        left, right, (((left_dim,), (right_dim,)), ((), ())), preferred_element_type=F32
    )


def index_spec():
    return pl.BlockSpec(memory_space=pltpu.SMEM)


def params():
    return pltpu.CompilerParams(vmem_limit_bytes=56 * 2**20)


def filter_kernel(place_ref, sig_ref, rim_ref, taps_ref, *refs):
    out_refs, kept = refs[:-1], refs[-1]
    batch, rows, slab = sig_ref.shape
    width = rim_ref.shape[2]
    blocks = slab // width
    pieces = len(out_refs) // batch
    span = slab // pieces
    signal = jnp.swapaxes(sig_ref[...].astype(F32), 0, 1)
    rim = jnp.swapaxes(rim_ref[...].astype(F32), 0, 1)
    taps = taps_ref[...].astype(F32)
    first = lax.broadcasted_iota(jnp.int32, (rows, width), 1) == 0
    taps = jnp.concatenate(
        [taps[:, :width], jnp.where(first, taps[:, width : width + 1], 0.0)], axis=1
    )
    results = []
    for row in range(rows):
        own = [signal[row, :, j * width : (j + 1) * width] for j in range(blocks)]
        current = jnp.concatenate(own, axis=0)
        before = jnp.concatenate([rim[row]] + own[:-1], axis=0)
        window = jnp.concatenate([before, current], axis=1).astype(BF16)
        spread = jnp.broadcast_to(taps[row : row + 1, :], (width, 2 * width))
        rolled = pltpu.roll(spread, 0, 1, stride=1, stride_axis=0)
        table = jnp.concatenate([rolled[:, width:], rolled[:, :width]], axis=0).astype(BF16)
        product = mm(window, table)
        results.append(
            jnp.concatenate(
                [product[j * batch : (j + 1) * batch] for j in range(blocks)], axis=1
            )
        )
    filtered = jnp.swapaxes(jnp.stack(results, axis=0), 0, 1).astype(BF16)
    for index in range(batch):
        for piece in range(pieces):
            kept[index * pieces + piece] = filtered[index, :, piece * span : (piece + 1) * span]
    me = place_ref[1]
    for k, out_ref in enumerate(out_refs):
        out_ref[...] = kept[me ^ k]


def filter_all(place, signal, rim, taps, count):
    batch, contacts, slab = signal.shape
    width = rim.shape[2]
    rows = 16
    span = slab * batch // count
    return pl.pallas_call(
        filter_kernel,
        grid=(contacts // rows,),
        in_specs=[
            index_spec(),
            pl.BlockSpec((batch, rows, slab), lambda i: (0, i, 0)),
            pl.BlockSpec((batch, rows, width), lambda i: (0, i, 0)),
            pl.BlockSpec((rows, taps.shape[1]), lambda i: (i, 0)),
        ],
        out_specs=[pl.BlockSpec((rows, span), lambda i: (i, 0))] * count,
        out_shape=[jax.ShapeDtypeStruct((contacts, span), BF16)] * count,
        scratch_shapes=[pltpu.VMEM((count, rows, span), BF16)],
        compiler_params=params(),
        cost_estimate=pl.CostEstimate(
            flops=4 * batch * contacts * slab * width,
            bytes_accessed=4 * batch * contacts * slab,
            transcendentals=0,
        ),
        name="filter",
    )(place, signal, rim, taps)


def head_masks(width):
    lane_head = lax.broadcasted_iota(jnp.int32, (1, width), 1) // (width // HEADS)
    return [(lane_head == h).astype(F32) for h in range(HEADS)]


def forward_kernel(
    blocks, place_ref, nbr_ref, live_ref, coef_ref, wq_ref, wk_ref, wv_ref, wo_ref, *refs
):
    feat_refs = refs[:blocks]
    (
        out_ref, prob_ref, value_ref, keys_ref, query_t_ref, normed_ref, normed_t_ref, mixed_ref,
        mixed_t_ref, counts, columns, packed, live_row,
    ) = refs[blocks:]
    rows, width = feat_refs[0].shape
    contacts = rows * blocks
    scale = (width // HEADS) ** (-0.5)
    slots = nbr_ref.shape[0]
    me = place_ref[1]

    @pl.when(pl.program_id(0) == 0)
    def _():
        packed[...] = jnp.zeros_like(packed)
        packed[0:1, :] = live_ref[...].astype(F32)
        packed[1:2, :] = coef_ref[...]
        for slot in range(slots):
            packed[2 + slot : 3 + slot, :] = nbr_ref[slot : slot + 1, :].astype(F32)
        columns[...] = packed[...].T
        turned = jnp.concatenate(
            [columns[pl.ds(pl.multiple_of((me ^ k) * rows, rows), rows), :] for k in range(blocks)],
            axis=0,
        )
        alive = turned.T[0:1]
        live_row[...] = alive
        ids = lax.broadcasted_iota(jnp.int32, (contacts, contacts), 1)
        total = jnp.zeros((contacts, contacts), F32)
        for slot in range(slots):
            here = turned[:, slot + 2 : slot + 3].astype(jnp.int32) ^ (me * rows)
            total = total + jnp.where(here == ids, alive, 0.0)
        counts[...] = total.astype(BF16)
        columns[:, 0:1] = turned[:, 0:1]
        columns[:, 1:2] = turned[:, 1:2]
        columns[:, 2:3] = jnp.sum(total, axis=1, keepdims=True)

    live = columns[:, 0:1]
    coef = columns[:, 1:2]
    field = jnp.concatenate([ref[...] for ref in feat_refs], axis=0)
    middle = field.astype(F32)
    beside = mm(counts[...], field)
    ready = live * (middle + coef * (beside - columns[:, 2:3] * middle))
    ready = ready.astype(BF16).astype(F32)
    mean_square = jnp.mean(ready * ready, axis=1, keepdims=True)
    normed = (ready * lax.rsqrt(mean_square + 1e-05)).astype(BF16)
    query = (mm(normed, wq_ref[...]) * scale).astype(BF16)
    keys = mm(normed, wk_ref[...]).astype(BF16)
    value = mm(normed, wv_ref[...]).astype(BF16)
    value_ref[...] = value
    keys_ref[...] = keys
    query_t_ref[...] = query.T
    normed_ref[...] = normed
    normed_t_ref[...] = normed.T
    masks = [m.astype(BF16) for m in head_masks(width)]
    bias = jnp.where(live_row[...] > 0, 0.0, -1e30)
    scores = mm(query * masks[0], keys, 1, 1)
    mixed = None
    for h in range(HEADS):
        following = mm(query * masks[h + 1], keys, 1, 1) if h + 1 < HEADS else None
        scores = scores + bias
        top = jnp.max(scores, axis=1, keepdims=True)
        raised = jnp.exp(scores - top)
        share = 1.0 / jnp.sum(raised, axis=1, keepdims=True)
        prob = (raised * share).astype(BF16)
        prob_ref[:, h * contacts : (h + 1) * contacts] = prob
        part = mm(prob, value * masks[h])
        mixed = part if mixed is None else mixed + part
        scores = following
    mixed = mixed.astype(BF16)
    attended = mm(mixed, wo_ref[...]).astype(BF16)
    for k in range(blocks):
        out_ref[me ^ k] = attended[k * rows : (k + 1) * rows]
    mixed_ref[...] = mixed
    mixed_t_ref[...] = mixed.T


def backward_kernel(
    blocks, place_ref, wo_ref, up_ref, prob_ref, value_ref, keys_ref, query_t_ref, normed_ref,
    normed_t_ref, mixed_ref, mixed_t_ref, *refs,
):
    out_refs, total, chunks = refs[:-2], refs[-2], refs[-1]
    contacts, width = normed_ref.shape
    head = width // HEADS
    scale = head ** (-0.5)
    step = pl.program_id(0)

    @pl.when(step == 0)
    def _():
        total[...] = jnp.zeros_like(total)

    me = place_ref[1]
    upstream = jnp.concatenate([up_ref[me ^ k] for k in range(blocks)], axis=0)
    normed = normed_ref[...]
    value = value_ref[...]
    keys = keys_ref[...]
    back = mm(upstream, wo_ref[...], 1, 1).astype(BF16)
    back_t = back.T
    inner = back.astype(F32) * mixed_ref[...].astype(F32)
    masks = head_masks(width)
    grad_value_t = []
    grad_key_t = []
    grad_query = None
    low = [m.astype(BF16) for m in masks]
    grad_prob = mm(back * low[0], value, 1, 1)
    for h in range(HEADS):
        following = mm(back * low[h + 1], value, 1, 1) if h + 1 < HEADS else None
        row_inner = jnp.sum(inner * masks[h], axis=1, keepdims=True)
        prob = prob_ref[:, h * contacts : (h + 1) * contacts]
        grad_value_t.append(mm(back_t[h * head : (h + 1) * head], prob))
        grad_score = (prob.astype(F32) * (grad_prob - row_inner)).astype(BF16)
        grad_key_t.append(mm(query_t_ref[h * head : (h + 1) * head, :], grad_score))
        part = mm(grad_score, keys * low[h])
        grad_query = part if grad_query is None else grad_query + part
        grad_prob = following
    grad_query = (grad_query * scale).astype(BF16)
    total[0] += mm(normed_t_ref[...], grad_query)
    total[1] += mm(jnp.concatenate(grad_key_t, axis=0).astype(BF16), normed)
    total[2] += mm(jnp.concatenate(grad_value_t, axis=0).astype(BF16), normed)
    total[3] += mm(mixed_t_ref[...], upstream)

    @pl.when(step == pl.num_programs(0) - 1)
    def _():
        count, rows = chunks.shape[:2]
        parts = [total[0], total[1].T, total[2].T, total[3]]
        for c in range(count):
            first = (c * rows) % width
            chunks[c] = parts[c * rows // width][first : first + rows].astype(BF16)
        for k, out_ref in enumerate(out_refs):
            out_ref[...] = chunks[place_ref[0] ^ k]


def whole(shape):
    return pl.BlockSpec(shape, lambda i: (0,) * len(shape))


def forward(place, features, neighbours, live, coef, weights):
    blocks = len(features)
    rows, span = features[0].shape
    contacts = rows * blocks
    width = weights[0].shape[0]
    groups = span // width
    shapes = [
        (contacts, HEADS * contacts), (contacts, width),
        (contacts, width), (width, contacts), (contacts, width), (width, contacts),
        (contacts, width), (width, contacts),
    ]
    small = [neighbours, live, coef] + list(weights)
    return pl.pallas_call(
        functools.partial(forward_kernel, blocks),
        grid=(groups,),
        in_specs=[index_spec()]
        + [whole(item.shape) for item in small]
        + [pl.BlockSpec((rows, width), lambda i: (0, i))] * blocks,
        out_specs=[pl.BlockSpec((blocks, rows, width), lambda i: (0, 0, i))]
        + [pl.BlockSpec(shape, lambda i: (0, i)) for shape in shapes],
        out_shape=[jax.ShapeDtypeStruct((blocks, rows, span), BF16)]
        + [jax.ShapeDtypeStruct((shape[0], groups * shape[1]), BF16) for shape in shapes],
        scratch_shapes=[
            pltpu.VMEM((contacts, contacts), BF16),
            pltpu.VMEM((contacts, 128), F32),
            pltpu.VMEM((128, contacts), F32),
            pltpu.VMEM((1, contacts), F32),
        ],
        compiler_params=params(),
        cost_estimate=pl.CostEstimate(
            flops=groups * 5 * 10**9,
            bytes_accessed=20 * contacts * span,
            transcendentals=groups * HEADS * contacts * contacts,
        ),
        name="forward",
    )(place, *small, *features)


def backward(place, upstream, kept, w_out, tm_count):
    blocks, rows, span = upstream.shape
    contacts = rows * blocks
    width = w_out.shape[0]
    groups = span // width
    chunk = (4 * width // tm_count, width)
    return pl.pallas_call(
        functools.partial(backward_kernel, blocks),
        grid=(groups,),
        in_specs=[
            index_spec(), whole(w_out.shape),
            pl.BlockSpec((blocks, rows, width), lambda i: (0, 0, i)),
        ]
        + [
            pl.BlockSpec((item.shape[0], item.shape[1] // groups), lambda i: (0, i))
            for item in kept
        ],
        out_specs=[whole(chunk)] * tm_count,
        out_shape=[jax.ShapeDtypeStruct(chunk, BF16)] * tm_count,
        scratch_shapes=[
            pltpu.VMEM((4, width, width), F32),
            pltpu.VMEM((tm_count,) + chunk, BF16),
        ],
        compiler_params=params(),
        cost_estimate=pl.CostEstimate(
            flops=groups * 5 * 10**9, bytes_accessed=20 * contacts * span, transcendentals=0
        ),
        name="backward",
    )(place, w_out, upstream, *kept)


def place_all(place, parts):
    rows, width = parts[0].shape
    ways = len(parts)

    def body(place_ref, *refs):
        for k in range(ways):
            refs[-1][place_ref[0] ^ k] = refs[k][...].astype(F32)

    shape = (ways, rows, width)
    return pl.pallas_call(
        body,
        in_specs=[index_spec()] + [pl.BlockSpec((rows, width), lambda: (0, 0))] * ways,
        out_specs=pl.BlockSpec(shape, lambda: (0, 0, 0)),
        out_shape=jax.ShapeDtypeStruct(shape, F32),
        compiler_params=params(),
        name="place_all",
    )(place, *parts)


def swap(value, axis, k):
    return lax.ppermute(value, axis, [(i, i ^ k) for i in range(lax.axis_size(axis))])


def swap_all(parts, axis):
    moved = [swap(parts[k], axis, k) for k in range(len(parts) - 1, 0, -1)]
    return [parts[0]] + moved[::-1]


def exchange(value, axis):
    return lax.all_to_all(value, axis, split_axis=0, concat_axis=0, tiled=True)


def local(
    signal, fir_taps, neighbours, live_mask, lap_coef, w_query, w_key, w_value, w_out, cotangent
):
    batch, contacts_here, slab = signal.shape
    rim_width = fir_taps.shape[1] - 1
    width = w_query.shape[0]
    tm_count = lax.axis_size("tm")
    count = lax.axis_size("contact")
    pieces = count // batch
    span = slab // pieces
    place = jnp.stack([lax.axis_index("tm"), lax.axis_index("contact")]).astype(jnp.int32)

    if pieces > 1:
        cotangent = cotangent.reshape(batch, contacts_here, pieces, span)
        cotangent = cotangent.transpose(0, 2, 1, 3).reshape(count, contacts_here, span)
    rim = lax.ppermute(
        signal[:, :, slab - rim_width :], "tm", [(i, i + 1) for i in range(tm_count - 1)]
    )
    filtered = filter_all(place, signal, rim, fir_taps, count)
    features = swap_all(filtered, "contact")
    arrived = count - max(2, count // 4)
    features[arrived:], cotangent = lax.optimization_barrier((features[arrived:], cotangent))
    upstream = exchange(cotangent, "contact")
    attended, *kept = forward(
        place, features, neighbours.T, live_mask[None], lap_coef[None],
        [w_query, w_key, w_value, w_out],
    )
    returned = exchange(attended, "contact")
    grads = backward(place, upstream, kept, w_out, tm_count)
    grads = swap_all(grads, "tm")
    part = sum(piece.astype(F32) for piece in grads).astype(BF16)
    part, _ = lax.optimization_barrier((part, returned))
    part = exchange(part, "contact").reshape(count, -1, width)
    grad_scale = (batch * (slab // width) * tm_count * neighbours.shape[0]) ** (-0.5)
    mine = (jnp.sum(part.astype(F32), axis=0) * grad_scale).astype(BF16)
    chunk = exchange(jnp.concatenate([mine] * count, axis=0), "contact")
    summed = place_all(place, swap_all([chunk] * tm_count, "tm"))
    if pieces > 1:
        returned = returned.reshape(batch, pieces, contacts_here, span)
        returned = returned.transpose(0, 2, 1, 3).reshape(batch, contacts_here, slab)
    return (returned, summed.reshape(4, width, width))


def solution(mesh):
    in_specs = (
        P(None, "contact", "tm"),
        P("contact", None),
        P(),
        P(),
        P(),
        P(),
        P(),
        P(),
        P(),
        P(None, "contact", "tm"),
    )
    out_specs = (P(None, "contact", "tm"), P())
    return jax.shard_map(local, mesh=mesh, in_specs=in_specs, out_specs=out_specs, check_vma=False)
```

```python
import functools

import jax
import jax.numpy as jnp
from jax import lax
from jax.experimental import pallas as pl
from jax.experimental.pallas import tpu as pltpu
from jax.sharding import PartitionSpec as P

HEADS = 4
F32 = jnp.float32
BF16 = jnp.bfloat16


def mm(left, right, left_dim=1, right_dim=0):
    return lax.dot_general(
        left, right, (((left_dim,), (right_dim,)), ((), ())), preferred_element_type=F32
    )


def index_spec():
    return pl.BlockSpec(memory_space=pltpu.SMEM)


def params():
    return pltpu.CompilerParams(vmem_limit_bytes=56 * 2**20)


def filter_kernel(place_ref, sig_ref, rim_ref, taps_ref, *refs):
    out_refs, kept = refs[:-1], refs[-1]
    batch, rows, slab = sig_ref.shape
    width = rim_ref.shape[2]
    blocks = slab // width
    pieces = len(out_refs) // batch
    span = slab // pieces
    signal = jnp.swapaxes(sig_ref[...].astype(F32), 0, 1)
    rim = jnp.swapaxes(rim_ref[...].astype(F32), 0, 1)
    taps = taps_ref[...].astype(F32)
    first = lax.broadcasted_iota(jnp.int32, (rows, width), 1) == 0
    taps = jnp.concatenate(
        [taps[:, :width], jnp.where(first, taps[:, width : width + 1], 0.0)], axis=1
    )
    results = []
    for row in range(rows):
        own = [signal[row, :, j * width : (j + 1) * width] for j in range(blocks)]
        current = jnp.concatenate(own, axis=0)
        before = jnp.concatenate([rim[row]] + own[:-1], axis=0)
        window = jnp.concatenate([before, current], axis=1).astype(BF16)
        spread = jnp.broadcast_to(taps[row : row + 1, :], (width, 2 * width))
        rolled = pltpu.roll(spread, 0, 1, stride=1, stride_axis=0)
        table = jnp.concatenate([rolled[:, width:], rolled[:, :width]], axis=0).astype(BF16)
        product = mm(window, table)
        results.append(
            jnp.concatenate(
                [product[j * batch : (j + 1) * batch] for j in range(blocks)], axis=1
            )
        )
    filtered = jnp.swapaxes(jnp.stack(results, axis=0), 0, 1).astype(BF16)
    for index in range(batch):
        for piece in range(pieces):
            kept[index * pieces + piece] = filtered[index, :, piece * span : (piece + 1) * span]
    me = place_ref[1]
    for k, out_ref in enumerate(out_refs):
        out_ref[...] = kept[me ^ k]


def filter_all(place, signal, rim, taps, count):
    batch, contacts, slab = signal.shape
    width = rim.shape[2]
    rows = 16
    span = slab * batch // count
    return pl.pallas_call(
        filter_kernel,
        grid=(contacts // rows,),
        in_specs=[
            index_spec(),
            pl.BlockSpec((batch, rows, slab), lambda i: (0, i, 0)),
            pl.BlockSpec((batch, rows, width), lambda i: (0, i, 0)),
            pl.BlockSpec((rows, taps.shape[1]), lambda i: (i, 0)),
        ],
        out_specs=[pl.BlockSpec((rows, span), lambda i: (i, 0))] * count,
        out_shape=[jax.ShapeDtypeStruct((contacts, span), BF16)] * count,
        scratch_shapes=[pltpu.VMEM((count, rows, span), BF16)],
        compiler_params=params(),
        cost_estimate=pl.CostEstimate(
            flops=4 * batch * contacts * slab * width,
            bytes_accessed=4 * batch * contacts * slab,
            transcendentals=0,
        ),
        name="filter",
    )(place, signal, rim, taps)


def head_masks(width):
    lane_head = lax.broadcasted_iota(jnp.int32, (1, width), 1) // (width // HEADS)
    return [(lane_head == h).astype(F32) for h in range(HEADS)]


def forward_kernel(
    blocks, place_ref, nbr_ref, live_ref, coef_ref, wq_ref, wk_ref, wv_ref, wo_ref, *refs
):
    feat_refs = refs[:blocks]
    (
        out_ref, prob_ref, value_ref, keys_ref, query_t_ref, normed_ref, normed_t_ref, mixed_ref,
        mixed_t_ref, inverse_ref, counts, columns, packed, live_row,
    ) = refs[blocks:]
    rows, width = feat_refs[0].shape
    contacts = rows * blocks
    scale = (width // HEADS) ** (-0.5)
    slots = nbr_ref.shape[0]
    me = place_ref[1]

    @pl.when(pl.program_id(0) == 0)
    def _():
        packed[...] = jnp.zeros_like(packed)
        packed[0:1, :] = live_ref[...].astype(F32)
        packed[1:2, :] = coef_ref[...]
        for slot in range(slots):
            packed[2 + slot : 3 + slot, :] = nbr_ref[slot : slot + 1, :].astype(F32)
        columns[...] = packed[...].T
        turned = jnp.concatenate(
            [columns[pl.ds(pl.multiple_of((me ^ k) * rows, rows), rows), :] for k in range(blocks)],
            axis=0,
        )
        alive = turned.T[0:1]
        live_row[...] = alive
        ids = lax.broadcasted_iota(jnp.int32, (contacts, contacts), 1)
        total = jnp.zeros((contacts, contacts), F32)
        for slot in range(slots):
            here = turned[:, slot + 2 : slot + 3].astype(jnp.int32) ^ (me * rows)
            total = total + jnp.where(here == ids, alive, 0.0)
        counts[...] = total.astype(BF16)
        columns[:, 0:1] = turned[:, 0:1]
        columns[:, 1:2] = turned[:, 1:2]
        columns[:, 2:3] = jnp.sum(total, axis=1, keepdims=True)

    live = columns[:, 0:1]
    coef = columns[:, 1:2]
    field = jnp.concatenate([ref[...] for ref in feat_refs], axis=0)
    middle = field.astype(F32)
    beside = mm(counts[...], field)
    ready = live * (middle + coef * (beside - columns[:, 2:3] * middle))
    ready = ready.astype(BF16).astype(F32)
    mean_square = jnp.mean(ready * ready, axis=1, keepdims=True)
    normed = (ready * lax.rsqrt(mean_square + 1e-05)).astype(BF16)
    query = (mm(normed, wq_ref[...]) * scale).astype(BF16)
    keys = mm(normed, wk_ref[...]).astype(BF16)
    value = mm(normed, wv_ref[...]).astype(BF16)
    value_ref[...] = value
    keys_ref[...] = keys
    query_t_ref[...] = query.T
    normed_ref[...] = normed
    normed_t_ref[...] = normed.T
    masks = [m.astype(BF16) for m in head_masks(width)]
    bias = jnp.where(live_row[...] > 0, 0.0, -1e30)
    block = min(64, contacts)
    lane_head = lax.broadcasted_iota(jnp.int32, (block, width), 1) // (width // HEADS)
    shares = [[] for _ in range(contacts // block)]
    scores = mm(query * masks[0], keys, 1, 1)
    mixed = None
    for h in range(HEADS):
        following = mm(query * masks[h + 1], keys, 1, 1) if h + 1 < HEADS else None
        columns_h = slice(h * contacts, (h + 1) * contacts)
        for r, share in enumerate(shares):
            here = slice(r * block, (r + 1) * block)
            part = scores[here] + bias
            raised = jnp.exp(part - jnp.max(part, axis=1, keepdims=True))
            prob_ref[here, columns_h] = raised.astype(BF16)
            share.append(1.0 / jnp.sum(raised, axis=1, keepdims=True))
        part = mm(prob_ref[:, columns_h], value * masks[h])
        mixed = part if mixed is None else mixed + part
        scores = following
    for r, share in enumerate(shares):
        here = slice(r * block, (r + 1) * block)
        inverse = jnp.broadcast_to(share[0], (block, width))
        for h in range(1, HEADS):
            inverse = jnp.where(lane_head >= h, share[h], inverse)
        inverse_ref[here, :] = inverse
    mixed = (mixed * inverse_ref[...]).astype(BF16)
    attended = mm(mixed, wo_ref[...]).astype(BF16)
    for k in range(blocks):
        out_ref[me ^ k] = attended[k * rows : (k + 1) * rows]
    mixed_ref[...] = mixed
    mixed_t_ref[...] = mixed.T


def backward_kernel(
    blocks, place_ref, wo_ref, up_ref, prob_ref, value_ref, keys_ref, query_t_ref, normed_ref,
    normed_t_ref, mixed_ref, mixed_t_ref, inverse_ref, *refs,
):
    out_refs, total, chunks, changes = refs[:-3], refs[-3], refs[-2], refs[-1]
    contacts, width = normed_ref.shape
    head = width // HEADS
    scale = head ** (-0.5)
    step = pl.program_id(0)

    @pl.when(step == 0)
    def _():
        total[...] = jnp.zeros_like(total)

    me = place_ref[1]
    upstream = jnp.concatenate([up_ref[me ^ k] for k in range(blocks)], axis=0)
    normed = normed_ref[...]
    value = value_ref[...]
    keys = keys_ref[...]
    back = mm(upstream, wo_ref[...], 1, 1).astype(BF16)
    back = (back.astype(F32) * inverse_ref[...]).astype(BF16)
    back_t = back.T
    inner = back.astype(F32) * mixed_ref[...].astype(F32)
    masks = head_masks(width)
    grad_value_t = []
    grad_key_t = []
    grad_query = None
    low = [m.astype(BF16) for m in masks]
    block = min(64, contacts)
    grad_prob = mm(back * low[0], value, 1, 1)
    for h in range(HEADS):
        following = mm(back * low[h + 1], value, 1, 1) if h + 1 < HEADS else None
        columns_h = slice(h * contacts, (h + 1) * contacts)
        grad_value_t.append(mm(back_t[h * head : (h + 1) * head], prob_ref[:, columns_h]))
        for r in range(contacts // block):
            here = slice(r * block, (r + 1) * block)
            row_inner = jnp.sum(inner[here] * masks[h], axis=1, keepdims=True)
            shift = (grad_prob[here] - row_inner).astype(BF16)
            changes[here, columns_h] = prob_ref[here, columns_h] * shift
        grad_score = changes[:, columns_h]
        grad_key_t.append(mm(query_t_ref[h * head : (h + 1) * head, :], grad_score))
        part = mm(grad_score, keys * low[h])
        grad_query = part if grad_query is None else grad_query + part
        grad_prob = following
    grad_query = (grad_query * scale).astype(BF16)
    total[0] += mm(normed_t_ref[...], grad_query)
    total[1] += mm(jnp.concatenate(grad_key_t, axis=0).astype(BF16), normed)
    total[2] += mm(jnp.concatenate(grad_value_t, axis=0).astype(BF16), normed)
    total[3] += mm(mixed_t_ref[...], upstream)

    @pl.when(step == pl.num_programs(0) - 1)
    def _():
        count, rows = chunks.shape[:2]
        parts = [total[0], total[1].T, total[2].T, total[3]]
        for c in range(count):
            first = (c * rows) % width
            chunks[c] = parts[c * rows // width][first : first + rows].astype(BF16)
        for k, out_ref in enumerate(out_refs):
            out_ref[...] = chunks[place_ref[0] ^ k]


def whole(shape):
    return pl.BlockSpec(shape, lambda i: (0,) * len(shape))


def forward(place, features, neighbours, live, coef, weights):
    blocks = len(features)
    rows, span = features[0].shape
    contacts = rows * blocks
    width = weights[0].shape[0]
    groups = span // width
    shapes = [
        (contacts, HEADS * contacts), (contacts, width),
        (contacts, width), (width, contacts), (contacts, width), (width, contacts),
        (contacts, width), (width, contacts), (contacts, width),
    ]
    small = [neighbours, live, coef] + list(weights)
    return pl.pallas_call(
        functools.partial(forward_kernel, blocks),
        grid=(groups,),
        in_specs=[index_spec()]
        + [whole(item.shape) for item in small]
        + [pl.BlockSpec((rows, width), lambda i: (0, i))] * blocks,
        out_specs=[pl.BlockSpec((blocks, rows, width), lambda i: (0, 0, i))]
        + [pl.BlockSpec(shape, lambda i: (0, i)) for shape in shapes],
        out_shape=[jax.ShapeDtypeStruct((blocks, rows, span), BF16)]
        + [
            jax.ShapeDtypeStruct((shape[0], groups * shape[1]), kind)
            for shape, kind in zip(shapes, [BF16] * (len(shapes) - 1) + [F32])
        ],
        scratch_shapes=[
            pltpu.VMEM((contacts, contacts), BF16),
            pltpu.VMEM((contacts, 128), F32),
            pltpu.VMEM((128, contacts), F32),
            pltpu.VMEM((1, contacts), F32),
        ],
        compiler_params=params(),
        cost_estimate=pl.CostEstimate(
            flops=groups * 5 * 10**9,
            bytes_accessed=20 * contacts * span,
            transcendentals=groups * HEADS * contacts * contacts,
        ),
        name="forward",
    )(place, *small, *features)


def backward(place, upstream, kept, w_out, tm_count):
    blocks, rows, span = upstream.shape
    contacts = rows * blocks
    width = w_out.shape[0]
    groups = span // width
    chunk = (4 * width // tm_count, width)
    return pl.pallas_call(
        functools.partial(backward_kernel, blocks),
        grid=(groups,),
        in_specs=[
            index_spec(), whole(w_out.shape),
            pl.BlockSpec((blocks, rows, width), lambda i: (0, 0, i)),
        ]
        + [
            pl.BlockSpec((item.shape[0], item.shape[1] // groups), lambda i: (0, i))
            for item in kept
        ],
        out_specs=[whole(chunk)] * tm_count,
        out_shape=[jax.ShapeDtypeStruct(chunk, BF16)] * tm_count,
        scratch_shapes=[
            pltpu.VMEM((4, width, width), F32),
            pltpu.VMEM((tm_count,) + chunk, BF16),
            pltpu.VMEM((contacts, HEADS * contacts), BF16),
        ],
        compiler_params=params(),
        cost_estimate=pl.CostEstimate(
            flops=groups * 5 * 10**9, bytes_accessed=20 * contacts * span, transcendentals=0
        ),
        name="backward",
    )(place, w_out, upstream, *kept)


def place_all(place, parts):
    rows, width = parts[0].shape
    ways = len(parts)

    def body(place_ref, *refs):
        for k in range(ways):
            refs[-1][place_ref[0] ^ k] = refs[k][...].astype(F32)

    shape = (ways, rows, width)
    return pl.pallas_call(
        body,
        in_specs=[index_spec()] + [pl.BlockSpec((rows, width), lambda: (0, 0))] * ways,
        out_specs=pl.BlockSpec(shape, lambda: (0, 0, 0)),
        out_shape=jax.ShapeDtypeStruct(shape, F32),
        compiler_params=params(),
        name="place_all",
    )(place, *parts)


def swap(value, axis, k):
    return lax.ppermute(value, axis, [(i, i ^ k) for i in range(lax.axis_size(axis))])


def swap_all(parts, axis):
    moved = [swap(parts[k], axis, k) for k in range(len(parts) - 1, 0, -1)]
    return [parts[0]] + moved[::-1]


def exchange(value, axis):
    return lax.all_to_all(value, axis, split_axis=0, concat_axis=0, tiled=True)


def local(
    signal, fir_taps, neighbours, live_mask, lap_coef, w_query, w_key, w_value, w_out, cotangent
):
    batch, contacts_here, slab = signal.shape
    rim_width = fir_taps.shape[1] - 1
    width = w_query.shape[0]
    tm_count = lax.axis_size("tm")
    count = lax.axis_size("contact")
    pieces = count // batch
    span = slab // pieces
    place = jnp.stack([lax.axis_index("tm"), lax.axis_index("contact")]).astype(jnp.int32)

    if pieces > 1:
        cotangent = cotangent.reshape(batch, contacts_here, pieces, span)
        cotangent = cotangent.transpose(0, 2, 1, 3).reshape(count, contacts_here, span)
    rim = lax.ppermute(
        signal[:, :, slab - rim_width :], "tm", [(i, i + 1) for i in range(tm_count - 1)]
    )
    filtered = filter_all(place, signal, rim, fir_taps, count)
    far = {k: swap(filtered[k], "contact", k) for k in range(count - 1, count // 2 - 1, -1)}
    far[count - 1], near = lax.optimization_barrier((far[count - 1], filtered[1 : count // 2]))
    features = [filtered[0]] + [swap(near[k - 1], "contact", k) for k in range(1, count // 2)]
    features += [far[k] for k in range(count // 2, count)]
    arrived = count - max(2, count // 4)
    features[arrived:], cotangent = lax.optimization_barrier((features[arrived:], cotangent))
    upstream = exchange(cotangent, "contact")
    attended, *kept = forward(
        place, features, neighbours.T, live_mask[None], lap_coef[None],
        [w_query, w_key, w_value, w_out],
    )
    returned = exchange(attended, "contact")
    grads = backward(place, upstream, kept, w_out, tm_count)
    grads = swap_all(grads, "tm")
    part = sum(piece.astype(F32) for piece in grads).astype(BF16)
    part, _ = lax.optimization_barrier((part, returned))
    part = exchange(part, "contact").reshape(count, -1, width)
    grad_scale = (batch * (slab // width) * tm_count * neighbours.shape[0]) ** (-0.5)
    mine = (jnp.sum(part.astype(F32), axis=0) * grad_scale).astype(BF16)
    chunk = exchange(jnp.concatenate([mine] * count, axis=0), "contact")
    summed = place_all(place, swap_all([chunk] * tm_count, "tm"))
    if pieces > 1:
        returned = returned.reshape(batch, pieces, contacts_here, span)
        returned = returned.transpose(0, 2, 1, 3).reshape(batch, contacts_here, slab)
    return (returned, summed.reshape(4, width, width))


def solution(mesh):
    in_specs = (
        P(None, "contact", "tm"),
        P("contact", None),
        P(),
        P(),
        P(),
        P(),
        P(),
        P(),
        P(),
        P(None, "contact", "tm"),
    )
    out_specs = (P(None, "contact", "tm"), P())
    return jax.shard_map(local, mesh=mesh, in_specs=in_specs, out_specs=out_specs, check_vma=False)
```

```python
import functools

import jax
import jax.numpy as jnp
from jax import lax
from jax.experimental import pallas as pl
from jax.experimental.pallas import tpu as pltpu
from jax.sharding import PartitionSpec as P

HEADS = 4
F32 = jnp.float32
BF16 = jnp.bfloat16


def mm(left, right, left_dim=1, right_dim=0):
    return lax.dot_general(
        left, right, (((left_dim,), (right_dim,)), ((), ())), preferred_element_type=F32
    )


def index_spec():
    return pl.BlockSpec(memory_space=pltpu.SMEM)


def params():
    return pltpu.CompilerParams(vmem_limit_bytes=56 * 2**20)


def filter_kernel(place_ref, sig_ref, rim_ref, taps_ref, *refs):
    out_refs, kept = refs[:-1], refs[-1]
    batch, rows, slab = sig_ref.shape
    width = rim_ref.shape[2]
    blocks = slab // width
    pieces = len(out_refs) // batch
    span = slab // pieces
    signal = jnp.swapaxes(sig_ref[...].astype(F32), 0, 1)
    rim = jnp.swapaxes(rim_ref[...].astype(F32), 0, 1)
    taps = taps_ref[...].astype(F32)
    first = lax.broadcasted_iota(jnp.int32, (rows, width), 1) == 0
    taps = jnp.concatenate(
        [taps[:, :width], jnp.where(first, taps[:, width : width + 1], 0.0)], axis=1
    )
    results = []
    for row in range(rows):
        own = [signal[row, :, j * width : (j + 1) * width] for j in range(blocks)]
        current = jnp.concatenate(own, axis=0)
        before = jnp.concatenate([rim[row]] + own[:-1], axis=0)
        window = jnp.concatenate([before, current], axis=1).astype(BF16)
        spread = jnp.broadcast_to(taps[row : row + 1, :], (width, 2 * width))
        rolled = pltpu.roll(spread, 0, 1, stride=1, stride_axis=0)
        table = jnp.concatenate([rolled[:, width:], rolled[:, :width]], axis=0).astype(BF16)
        product = mm(window, table)
        results.append(
            jnp.concatenate(
                [product[j * batch : (j + 1) * batch] for j in range(blocks)], axis=1
            )
        )
    filtered = jnp.swapaxes(jnp.stack(results, axis=0), 0, 1).astype(BF16)
    for index in range(batch):
        for piece in range(pieces):
            kept[index * pieces + piece] = filtered[index, :, piece * span : (piece + 1) * span]
    me = place_ref[1]
    for k, out_ref in enumerate(out_refs):
        out_ref[...] = kept[me ^ k]


def filter_all(place, signal, rim, taps, count):
    batch, contacts, slab = signal.shape
    width = rim.shape[2]
    rows = 16
    span = slab * batch // count
    return pl.pallas_call(
        filter_kernel,
        grid=(contacts // rows,),
        in_specs=[
            index_spec(),
            pl.BlockSpec((batch, rows, slab), lambda i: (0, i, 0)),
            pl.BlockSpec((batch, rows, width), lambda i: (0, i, 0)),
            pl.BlockSpec((rows, taps.shape[1]), lambda i: (i, 0)),
        ],
        out_specs=[pl.BlockSpec((rows, span), lambda i: (i, 0))] * count,
        out_shape=[jax.ShapeDtypeStruct((contacts, span), BF16)] * count,
        scratch_shapes=[pltpu.VMEM((count, rows, span), BF16)],
        compiler_params=params(),
        cost_estimate=pl.CostEstimate(
            flops=4 * batch * contacts * slab * width,
            bytes_accessed=4 * batch * contacts * slab,
            transcendentals=0,
        ),
        name="filter",
    )(place, signal, rim, taps)


def pair_masks(pair):
    lane = lax.broadcasted_iota(jnp.int32, (1, pair), 1)
    return [(lane < pair // 2).astype(F32).astype(BF16), (lane >= pair // 2).astype(F32).astype(BF16)]


def head_masks(width):
    lane_head = lax.broadcasted_iota(jnp.int32, (1, width), 1) // (width // HEADS)
    return [(lane_head == h).astype(F32) for h in range(HEADS)]


def forward_kernel(
    blocks, place_ref, nbr_ref, live_ref, coef_ref, wq_ref, wk_ref, wv_ref, wo_ref, *refs
):
    feat_refs = refs[:blocks]
    (
        out_ref, prob_ref, value_t_ref, keys_ref, query_t_ref, normed_ref, normed_t_ref, mixed_ref,
        mixed_t_ref, inverse_ref, counts, columns, packed, live_row, turned_w,
    ) = refs[blocks:]
    rows, width = feat_refs[0].shape
    contacts = rows * blocks
    scale = (width // HEADS) ** (-0.5)
    slots = nbr_ref.shape[0]
    me = place_ref[1]

    @pl.when(pl.program_id(0) == 0)
    def _():
        packed[...] = jnp.zeros_like(packed)
        packed[0:1, :] = live_ref[...].astype(F32)
        packed[1:2, :] = coef_ref[...]
        for slot in range(slots):
            packed[2 + slot : 3 + slot, :] = nbr_ref[slot : slot + 1, :].astype(F32)
        columns[...] = packed[...].T
        turned = jnp.concatenate(
            [columns[pl.ds(pl.multiple_of((me ^ k) * rows, rows), rows), :] for k in range(blocks)],
            axis=0,
        )
        alive = turned.T[0:1]
        live_row[...] = alive
        ids = lax.broadcasted_iota(jnp.int32, (contacts, contacts), 1)
        total = jnp.zeros((contacts, contacts), F32)
        for slot in range(slots):
            here = turned[:, slot + 2 : slot + 3].astype(jnp.int32) ^ (me * rows)
            total = total + jnp.where(here == ids, alive, 0.0)
        counts[...] = total.astype(BF16)
        columns[:, 0:1] = turned[:, 0:1]
        columns[:, 1:2] = turned[:, 1:2]
        columns[:, 2:3] = jnp.sum(total, axis=1, keepdims=True)
        turned_w[0] = wq_ref[...].T
        turned_w[1] = wk_ref[...].T
        turned_w[2] = wv_ref[...].T

    live = columns[:, 0:1]
    coef = columns[:, 1:2]
    field = jnp.concatenate([ref[...] for ref in feat_refs], axis=0)
    middle = field.astype(F32)
    beside = mm(counts[...], field)
    ready = live * (middle + coef * (beside - columns[:, 2:3] * middle))
    ready = ready.astype(BF16).astype(F32)
    mean_square = jnp.mean(ready * ready, axis=1, keepdims=True)
    normed = (ready * lax.rsqrt(mean_square + 1e-05)).astype(BF16)
    query = (mm(normed, wq_ref[...]) * scale).astype(BF16)
    keys = mm(normed, wk_ref[...]).astype(BF16)
    value = mm(normed, wv_ref[...]).astype(BF16)
    normed_t = normed.T
    keys_t = mm(turned_w[1], normed_t).astype(BF16)
    value_t_ref[...] = mm(turned_w[2], normed_t).astype(BF16)
    keys_ref[...] = keys
    query_t_ref[...] = (mm(turned_w[0], normed_t) * scale).astype(BF16)
    normed_ref[...] = normed
    normed_t_ref[...] = normed_t
    pair = 2 * width // HEADS
    masks = pair_masks(pair)

    def score(h):
        lanes = slice(h // 2 * pair, (h // 2 + 1) * pair)
        return mm(query[:, lanes] * masks[h % 2], keys_t[lanes, :])

    bias = jnp.where(live_row[...] > 0, 0.0, -1e30)
    block = min(64, contacts)
    lane_head = lax.broadcasted_iota(jnp.int32, (block, width), 1) // (width // HEADS)
    shares = [[] for _ in range(contacts // block)]
    scores = score(0)
    mixed = [None] * (HEADS // 2)
    for h in range(HEADS):
        following = score(h + 1) if h + 1 < HEADS else None
        columns_h = slice(h * contacts, (h + 1) * contacts)
        for r, share in enumerate(shares):
            here = slice(r * block, (r + 1) * block)
            part = scores[here] + bias
            raised = jnp.exp(part - jnp.max(part, axis=1, keepdims=True))
            prob_ref[here, columns_h] = raised.astype(BF16)
            share.append(1.0 / jnp.sum(raised, axis=1, keepdims=True))
        lanes = slice(h // 2 * pair, (h // 2 + 1) * pair)
        part = mm(prob_ref[:, columns_h], value[:, lanes] * masks[h % 2])
        mixed[h // 2] = part if h % 2 == 0 else mixed[h // 2] + part
        scores = following
    for r, share in enumerate(shares):
        here = slice(r * block, (r + 1) * block)
        inverse = jnp.broadcast_to(share[0], (block, width))
        for h in range(1, HEADS):
            inverse = jnp.where(lane_head >= h, share[h], inverse)
        inverse_ref[here, :] = inverse
    mixed = (jnp.concatenate(mixed, axis=1) * inverse_ref[...]).astype(BF16)
    attended = mm(mixed, wo_ref[...]).astype(BF16)
    for k in range(blocks):
        out_ref[me ^ k] = attended[k * rows : (k + 1) * rows]
    mixed_ref[...] = mixed
    mixed_t_ref[...] = mixed.T


def backward_kernel(
    blocks, place_ref, wo_ref, up_ref, prob_ref, value_t_ref, keys_ref, query_t_ref, normed_ref,
    normed_t_ref, mixed_ref, mixed_t_ref, inverse_ref, *refs,
):
    out_refs, (total, chunks, changes, turned_w) = refs[:-4], refs[-4:]
    contacts, width = normed_ref.shape
    head = width // HEADS
    scale = head ** (-0.5)
    step = pl.program_id(0)

    @pl.when(step == 0)
    def _():
        total[...] = jnp.zeros_like(total)
        turned_w[...] = wo_ref[...].T

    me = place_ref[1]
    upstream = jnp.concatenate([up_ref[me ^ k] for k in range(blocks)], axis=0)
    normed = normed_ref[...]
    keys = keys_ref[...]
    back = mm(upstream, turned_w[...]).astype(BF16)
    back = (back.astype(F32) * inverse_ref[...]).astype(BF16)
    back_t = back.T
    inner = back.astype(F32) * mixed_ref[...].astype(F32)
    masks = head_masks(width)
    grad_value_t = []
    grad_key_t = []
    pair = 2 * head
    grad_query = [None] * (HEADS // 2)
    low = pair_masks(pair)

    def change(h):
        lanes = slice(h // 2 * pair, (h // 2 + 1) * pair)
        return mm(back[:, lanes] * low[h % 2], value_t_ref[lanes, :])

    block = min(64, contacts)
    grad_prob = change(0)
    for h in range(HEADS):
        following = change(h + 1) if h + 1 < HEADS else None
        columns_h = slice(h * contacts, (h + 1) * contacts)
        grad_value_t.append(mm(back_t[h * head : (h + 1) * head], prob_ref[:, columns_h]))
        for r in range(contacts // block):
            here = slice(r * block, (r + 1) * block)
            row_inner = jnp.sum(inner[here] * masks[h], axis=1, keepdims=True)
            shift = (grad_prob[here] - row_inner).astype(BF16)
            changes[here, columns_h] = prob_ref[here, columns_h] * shift
        grad_score = changes[:, columns_h]
        grad_key_t.append(mm(query_t_ref[h * head : (h + 1) * head, :], grad_score))
        lanes = slice(h // 2 * pair, (h // 2 + 1) * pair)
        part = mm(grad_score, keys[:, lanes] * low[h % 2])
        grad_query[h // 2] = part if h % 2 == 0 else grad_query[h // 2] + part
        grad_prob = following
    grad_query = (jnp.concatenate(grad_query, axis=1) * scale).astype(BF16)
    total[0] += mm(normed_t_ref[...], grad_query)
    total[1] += mm(jnp.concatenate(grad_key_t, axis=0).astype(BF16), normed)
    total[2] += mm(jnp.concatenate(grad_value_t, axis=0).astype(BF16), normed)
    total[3] += mm(mixed_t_ref[...], upstream)

    @pl.when(step == pl.num_programs(0) - 1)
    def _():
        count, rows = chunks.shape[:2]
        parts = [total[0], total[1].T, total[2].T, total[3]]
        for c in range(count):
            first = (c * rows) % width
            chunks[c] = parts[c * rows // width][first : first + rows].astype(BF16)
        for k, out_ref in enumerate(out_refs):
            out_ref[...] = chunks[place_ref[0] ^ k]


def whole(shape):
    return pl.BlockSpec(shape, lambda i: (0,) * len(shape))


def forward(place, features, neighbours, live, coef, weights):
    blocks = len(features)
    rows, span = features[0].shape
    contacts = rows * blocks
    width = weights[0].shape[0]
    groups = span // width
    shapes = [
        (contacts, HEADS * contacts), (width, contacts),
        (contacts, width), (width, contacts), (contacts, width), (width, contacts),
        (contacts, width), (width, contacts), (contacts, width),
    ]
    small = [neighbours, live, coef] + list(weights)
    return pl.pallas_call(
        functools.partial(forward_kernel, blocks),
        grid=(groups,),
        in_specs=[index_spec()]
        + [whole(item.shape) for item in small]
        + [pl.BlockSpec((rows, width), lambda i: (0, i))] * blocks,
        out_specs=[pl.BlockSpec((blocks, rows, width), lambda i: (0, 0, i))]
        + [pl.BlockSpec(shape, lambda i: (0, i)) for shape in shapes],
        out_shape=[jax.ShapeDtypeStruct((blocks, rows, span), BF16)]
        + [
            jax.ShapeDtypeStruct((shape[0], groups * shape[1]), kind)
            for shape, kind in zip(shapes, [BF16] * (len(shapes) - 1) + [F32])
        ],
        scratch_shapes=[
            pltpu.VMEM((contacts, contacts), BF16),
            pltpu.VMEM((contacts, 128), F32),
            pltpu.VMEM((128, contacts), F32),
            pltpu.VMEM((1, contacts), F32),
            pltpu.VMEM((3, width, width), BF16),
        ],
        compiler_params=params(),
        cost_estimate=pl.CostEstimate(
            flops=groups * 5 * 10**9,
            bytes_accessed=20 * contacts * span,
            transcendentals=groups * HEADS * contacts * contacts,
        ),
        name="forward",
    )(place, *small, *features)


def backward(place, upstream, kept, w_out, tm_count):
    blocks, rows, span = upstream.shape
    contacts = rows * blocks
    width = w_out.shape[0]
    groups = span // width
    chunk = (4 * width // tm_count, width)
    return pl.pallas_call(
        functools.partial(backward_kernel, blocks),
        grid=(groups,),
        in_specs=[
            index_spec(), whole(w_out.shape),
            pl.BlockSpec((blocks, rows, width), lambda i: (0, 0, i)),
        ]
        + [
            pl.BlockSpec((item.shape[0], item.shape[1] // groups), lambda i: (0, i))
            for item in kept
        ],
        out_specs=[whole(chunk)] * tm_count,
        out_shape=[jax.ShapeDtypeStruct(chunk, BF16)] * tm_count,
        scratch_shapes=[
            pltpu.VMEM((4, width, width), F32),
            pltpu.VMEM((tm_count,) + chunk, BF16),
            pltpu.VMEM((contacts, HEADS * contacts), BF16),
            pltpu.VMEM((width, width), BF16),
        ],
        compiler_params=params(),
        cost_estimate=pl.CostEstimate(
            flops=groups * 5 * 10**9, bytes_accessed=20 * contacts * span, transcendentals=0
        ),
        name="backward",
    )(place, w_out, upstream, *kept)


def place_all(place, parts):
    rows, width = parts[0].shape
    ways = len(parts)

    def body(place_ref, *refs):
        for k in range(ways):
            refs[-1][place_ref[0] ^ k] = refs[k][...].astype(F32)

    shape = (ways, rows, width)
    return pl.pallas_call(
        body,
        in_specs=[index_spec()] + [pl.BlockSpec((rows, width), lambda: (0, 0))] * ways,
        out_specs=pl.BlockSpec(shape, lambda: (0, 0, 0)),
        out_shape=jax.ShapeDtypeStruct(shape, F32),
        compiler_params=params(),
        name="place_all",
    )(place, *parts)


def swap(value, axis, k):
    return lax.ppermute(value, axis, [(i, i ^ k) for i in range(lax.axis_size(axis))])


def swap_all(parts, axis):
    moved = [swap(parts[k], axis, k) for k in range(len(parts) - 1, 0, -1)]
    return [parts[0]] + moved[::-1]


def exchange(value, axis):
    return lax.all_to_all(value, axis, split_axis=0, concat_axis=0, tiled=True)


def local(
    signal, fir_taps, neighbours, live_mask, lap_coef, w_query, w_key, w_value, w_out, cotangent
):
    batch, contacts_here, slab = signal.shape
    rim_width = fir_taps.shape[1] - 1
    width = w_query.shape[0]
    tm_count = lax.axis_size("tm")
    count = lax.axis_size("contact")
    pieces = count // batch
    span = slab // pieces
    place = jnp.stack([lax.axis_index("tm"), lax.axis_index("contact")]).astype(jnp.int32)

    if pieces > 1:
        cotangent = cotangent.reshape(batch, contacts_here, pieces, span)
        cotangent = cotangent.transpose(0, 2, 1, 3).reshape(count, contacts_here, span)
    rim = lax.ppermute(
        signal[:, :, slab - rim_width :], "tm", [(i, i + 1) for i in range(tm_count - 1)]
    )
    filtered = filter_all(place, signal, rim, fir_taps, count)
    features = swap_all(filtered, "contact")
    arrived = count - max(2, count // 4)
    features[arrived:], cotangent = lax.optimization_barrier((features[arrived:], cotangent))
    upstream = exchange(cotangent, "contact")
    attended, *kept = forward(
        place, features, neighbours.T, live_mask[None], lap_coef[None],
        [w_query, w_key, w_value, w_out],
    )
    returned = exchange(attended, "contact")
    grads = backward(place, upstream, kept, w_out, tm_count)
    grads = swap_all(grads, "tm")
    part = sum(piece.astype(F32) for piece in grads).astype(BF16)
    part, _ = lax.optimization_barrier((part, returned))
    part = exchange(part, "contact").reshape(count, -1, width)
    grad_scale = (batch * (slab // width) * tm_count * neighbours.shape[0]) ** (-0.5)
    mine = (jnp.sum(part.astype(F32), axis=0) * grad_scale).astype(BF16)
    chunk = exchange(jnp.concatenate([mine] * count, axis=0), "contact")
    summed = place_all(place, swap_all([chunk] * tm_count, "tm"))
    if pieces > 1:
        returned = returned.reshape(batch, pieces, contacts_here, span)
        returned = returned.transpose(0, 2, 1, 3).reshape(batch, contacts_here, slab)
    return (returned, summed.reshape(4, width, width))


def solution(mesh):
    in_specs = (
        P(None, "contact", "tm"),
        P("contact", None),
        P(),
        P(),
        P(),
        P(),
        P(),
        P(),
        P(),
        P(None, "contact", "tm"),
    )
    out_specs = (P(None, "contact", "tm"), P())
    return jax.shard_map(local, mesh=mesh, in_specs=in_specs, out_specs=out_specs, check_vma=False)
```

```python
import functools

import jax
import jax.numpy as jnp
from jax import lax
from jax.experimental import pallas as pl
from jax.experimental.pallas import tpu as pltpu
from jax.sharding import PartitionSpec as P

HEADS = 4
F32 = jnp.float32
BF16 = jnp.bfloat16


def mm(left, right, left_dim=1, right_dim=0):
    return lax.dot_general(
        left, right, (((left_dim,), (right_dim,)), ((), ())), preferred_element_type=F32
    )


def index_spec():
    return pl.BlockSpec(memory_space=pltpu.SMEM)


def params():
    return pltpu.CompilerParams(vmem_limit_bytes=63 * 2**20)


def filter_kernel(place_ref, sig_ref, rim_ref, taps_ref, *refs):
    out_refs, kept = refs[:-1], refs[-1]
    batch, rows, slab = sig_ref.shape
    width = rim_ref.shape[2]
    blocks = slab // width
    pieces = len(out_refs) // batch
    span = slab // pieces
    signal = jnp.swapaxes(sig_ref[...].astype(F32), 0, 1)
    rim = jnp.swapaxes(rim_ref[...].astype(F32), 0, 1)
    taps = taps_ref[...].astype(F32)
    first = lax.broadcasted_iota(jnp.int32, (rows, width), 1) == 0
    taps = jnp.concatenate(
        [taps[:, :width], jnp.where(first, taps[:, width : width + 1], 0.0)], axis=1
    )
    results = []
    for row in range(rows):
        own = [signal[row, :, j * width : (j + 1) * width] for j in range(blocks)]
        current = jnp.concatenate(own, axis=0)
        before = jnp.concatenate([rim[row]] + own[:-1], axis=0)
        window = jnp.concatenate([before, current], axis=1).astype(BF16)
        spread = jnp.broadcast_to(taps[row : row + 1, :], (width, 2 * width))
        rolled = pltpu.roll(spread, 0, 1, stride=1, stride_axis=0)
        table = jnp.concatenate([rolled[:, width:], rolled[:, :width]], axis=0).astype(BF16)
        product = mm(window, table)
        results.append(
            jnp.concatenate(
                [product[j * batch : (j + 1) * batch] for j in range(blocks)], axis=1
            )
        )
    filtered = jnp.swapaxes(jnp.stack(results, axis=0), 0, 1).astype(BF16)
    for index in range(batch):
        for piece in range(pieces):
            kept[index * pieces + piece] = filtered[index, :, piece * span : (piece + 1) * span]
    me = place_ref[1]
    for k, out_ref in enumerate(out_refs):
        out_ref[...] = kept[me ^ k]


def filter_all(place, signal, rim, taps, count):
    batch, contacts, slab = signal.shape
    width = rim.shape[2]
    rows = 16
    span = slab * batch // count
    return pl.pallas_call(
        filter_kernel,
        grid=(contacts // rows,),
        in_specs=[
            index_spec(),
            pl.BlockSpec((batch, rows, slab), lambda i: (0, i, 0)),
            pl.BlockSpec((batch, rows, width), lambda i: (0, i, 0)),
            pl.BlockSpec((rows, taps.shape[1]), lambda i: (i, 0)),
        ],
        out_specs=[pl.BlockSpec((rows, span), lambda i: (i, 0))] * count,
        out_shape=[jax.ShapeDtypeStruct((contacts, span), BF16)] * count,
        scratch_shapes=[pltpu.VMEM((count, rows, span), BF16)],
        compiler_params=params(),
        cost_estimate=pl.CostEstimate(
            flops=4 * batch * contacts * slab * width,
            bytes_accessed=4 * batch * contacts * slab,
            transcendentals=0,
        ),
        name="filter",
    )(place, signal, rim, taps)


def pair_masks(pair):
    lane = lax.broadcasted_iota(jnp.int32, (1, pair), 1)
    return [(lane < pair // 2).astype(F32).astype(BF16), (lane >= pair // 2).astype(F32).astype(BF16)]


def head_masks(width):
    lane_head = lax.broadcasted_iota(jnp.int32, (1, width), 1) // (width // HEADS)
    return [(lane_head == h).astype(F32) for h in range(HEADS)]


def forward_kernel(
    blocks, place_ref, nbr_ref, live_ref, coef_ref, wq_ref, wk_ref, wv_ref, wo_ref, *refs
):
    feat_refs = refs[:blocks]
    (
        out_ref, prob_ref, value_ref, keys_ref, query_t_ref, normed_ref, normed_t_ref, mixed_ref,
        mixed_t_ref, inverse_ref, counts, columns, packed, live_row, turned_w,
    ) = refs[blocks:]
    rows, width = feat_refs[0].shape
    contacts = rows * blocks
    scale = (width // HEADS) ** (-0.5)
    slots = nbr_ref.shape[0]
    me = place_ref[1]

    @pl.when(pl.program_id(0) == 0)
    def _():
        packed[...] = jnp.zeros_like(packed)
        packed[0:1, :] = live_ref[...].astype(F32)
        packed[1:2, :] = coef_ref[...]
        for slot in range(slots):
            packed[2 + slot : 3 + slot, :] = nbr_ref[slot : slot + 1, :].astype(F32)
        columns[...] = packed[...].T
        turned = jnp.concatenate(
            [columns[pl.ds(pl.multiple_of((me ^ k) * rows, rows), rows), :] for k in range(blocks)],
            axis=0,
        )
        alive = turned.T[0:1]
        live_row[...] = alive
        ids = lax.broadcasted_iota(jnp.int32, (contacts, contacts), 1)
        total = jnp.zeros((contacts, contacts), F32)
        for slot in range(slots):
            here = turned[:, slot + 2 : slot + 3].astype(jnp.int32) ^ (me * rows)
            total = total + jnp.where(here == ids, alive, 0.0)
        counts[...] = total.astype(BF16)
        columns[:, 0:1] = turned[:, 0:1]
        columns[:, 1:2] = turned[:, 1:2]
        columns[:, 2:3] = jnp.sum(total, axis=1, keepdims=True)
        turned_w[0] = wq_ref[...].T
        turned_w[1] = wk_ref[...].T

    live = columns[:, 0:1]
    coef = columns[:, 1:2]
    field = jnp.concatenate([ref[...] for ref in feat_refs], axis=0)
    middle = field.astype(F32)
    beside = mm(counts[...], field)
    ready = live * (middle + coef * (beside - columns[:, 2:3] * middle))
    ready = ready.astype(BF16).astype(F32)
    mean_square = jnp.mean(ready * ready, axis=1, keepdims=True)
    normed = (ready * lax.rsqrt(mean_square + 1e-05)).astype(BF16)
    query = (mm(normed, wq_ref[...]) * scale).astype(BF16)
    keys = mm(normed, wk_ref[...]).astype(BF16)
    value = mm(normed, wv_ref[...]).astype(BF16)
    normed_t = normed.T
    keys_t = mm(turned_w[1], normed_t).astype(BF16)
    value_ref[...] = value
    keys_ref[...] = keys
    query_t_ref[...] = (mm(turned_w[0], normed_t) * scale).astype(BF16)
    normed_ref[...] = normed
    normed_t_ref[...] = normed_t
    pair = 2 * width // HEADS
    masks = pair_masks(pair)

    def score(h):
        lanes = slice(h // 2 * pair, (h // 2 + 1) * pair)
        return mm(query[:, lanes] * masks[h % 2], keys_t[lanes, :])

    bias = jnp.where(live_row[...] > 0, 0.0, -1e30)
    block = min(64, contacts)
    scores = score(0)
    products = []
    for h in range(HEADS):
        following = score(h + 1) if h + 1 < HEADS else None
        columns_h = slice(h * contacts, (h + 1) * contacts)
        for r in range(contacts // block):
            here = slice(r * block, (r + 1) * block)
            part = scores[here] + bias
            raised = jnp.exp(part - jnp.max(part, axis=1, keepdims=True))
            prob_ref[here, columns_h] = raised.astype(BF16)
        lanes = slice(h // 2 * pair, (h // 2 + 1) * pair)
        with_ones = value[:, lanes] * masks[h % 2] + masks[1 - h % 2]
        products.append(mm(prob_ref[:, columns_h], with_ones))
        scores = following
    low_lanes = lax.broadcasted_iota(jnp.int32, (contacts, pair), 1) < pair // 2
    mixed = []
    for p in range(HEADS // 2):
        even, odd = products[2 * p], products[2 * p + 1]
        inverse = 1.0 / pltpu.roll(jnp.where(low_lanes, odd, even), pair // 2, 1)
        inverse_ref[:, p * pair : (p + 1) * pair] = inverse
        mixed.append((jnp.where(low_lanes, even, odd) * inverse).astype(BF16))
    mixed = jnp.concatenate(mixed, axis=1)
    attended = mm(mixed, wo_ref[...]).astype(BF16)
    for k in range(blocks):
        out_ref[me ^ k] = attended[k * rows : (k + 1) * rows]
    mixed_ref[...] = mixed
    mixed_t_ref[...] = mixed.T


def backward_kernel(
    blocks, place_ref, wo_ref, up_ref, prob_ref, value_ref, keys_ref, query_t_ref, normed_ref,
    normed_t_ref, mixed_ref, mixed_t_ref, inverse_ref, *refs,
):
    out_refs, total, chunks, changes = refs[:-3], refs[-3], refs[-2], refs[-1]
    contacts, width = normed_ref.shape
    head = width // HEADS
    scale = head ** (-0.5)
    step = pl.program_id(0)

    @pl.when(step == 0)
    def _():
        total[...] = jnp.zeros_like(total)

    me = place_ref[1]
    upstream = jnp.concatenate([up_ref[me ^ k] for k in range(blocks)], axis=0)
    normed = normed_ref[...]
    value = value_ref[...]
    keys = keys_ref[...]
    back = mm(upstream, wo_ref[...], 1, 1).astype(BF16)
    back = (back.astype(F32) * inverse_ref[...]).astype(BF16)
    back_t = back.T
    inner = back.astype(F32) * mixed_ref[...].astype(F32)
    masks = head_masks(width)
    grad_value_t = []
    grad_key_t = []
    grad_query = None
    low = [m.astype(BF16) for m in masks]
    block = min(64, contacts)
    grad_prob = mm(back * low[0], value, 1, 1)
    for h in range(HEADS):
        following = mm(back * low[h + 1], value, 1, 1) if h + 1 < HEADS else None
        columns_h = slice(h * contacts, (h + 1) * contacts)
        grad_value_t.append(mm(back_t[h * head : (h + 1) * head], prob_ref[:, columns_h]))
        for r in range(contacts // block):
            here = slice(r * block, (r + 1) * block)
            row_inner = jnp.sum(inner[here] * masks[h], axis=1, keepdims=True)
            shift = (grad_prob[here] - row_inner).astype(BF16)
            changes[here, columns_h] = prob_ref[here, columns_h] * shift
        grad_score = changes[:, columns_h]
        grad_key_t.append(mm(query_t_ref[h * head : (h + 1) * head, :], grad_score))
        part = mm(grad_score, keys * low[h])
        grad_query = part if grad_query is None else grad_query + part
        grad_prob = following
    grad_query = (grad_query * scale).astype(BF16)
    total[0] += mm(normed_t_ref[...], grad_query)
    total[1] += mm(jnp.concatenate(grad_key_t, axis=0).astype(BF16), normed)
    total[2] += mm(jnp.concatenate(grad_value_t, axis=0).astype(BF16), normed)
    total[3] += mm(mixed_t_ref[...], upstream)

    @pl.when(step == pl.num_programs(0) - 1)
    def _():
        count, rows = chunks.shape[:2]
        parts = [total[0], total[1].T, total[2].T, total[3]]
        for c in range(count):
            first = (c * rows) % width
            chunks[c] = parts[c * rows // width][first : first + rows].astype(BF16)
        for k, out_ref in enumerate(out_refs):
            out_ref[...] = chunks[place_ref[0] ^ k]


def whole(shape):
    return pl.BlockSpec(shape, lambda i: (0,) * len(shape))


def forward(place, features, neighbours, live, coef, weights):
    blocks = len(features)
    rows, span = features[0].shape
    contacts = rows * blocks
    width = weights[0].shape[0]
    groups = span // width
    shapes = [
        (contacts, HEADS * contacts), (contacts, width),
        (contacts, width), (width, contacts), (contacts, width), (width, contacts),
        (contacts, width), (width, contacts), (contacts, width),
    ]
    small = [neighbours, live, coef] + list(weights)
    return pl.pallas_call(
        functools.partial(forward_kernel, blocks),
        grid=(groups,),
        in_specs=[index_spec()]
        + [whole(item.shape) for item in small]
        + [pl.BlockSpec((rows, width), lambda i: (0, i))] * blocks,
        out_specs=[pl.BlockSpec((blocks, rows, width), lambda i: (0, 0, i))]
        + [pl.BlockSpec(shape, lambda i: (0, i)) for shape in shapes],
        out_shape=[jax.ShapeDtypeStruct((blocks, rows, span), BF16)]
        + [
            jax.ShapeDtypeStruct((shape[0], groups * shape[1]), kind)
            for shape, kind in zip(shapes, [BF16] * (len(shapes) - 1) + [F32])
        ],
        scratch_shapes=[
            pltpu.VMEM((contacts, contacts), BF16),
            pltpu.VMEM((contacts, 128), F32),
            pltpu.VMEM((128, contacts), F32),
            pltpu.VMEM((1, contacts), F32),
            pltpu.VMEM((2, width, width), BF16),
        ],
        compiler_params=params(),
        cost_estimate=pl.CostEstimate(
            flops=groups * 5 * 10**9,
            bytes_accessed=20 * contacts * span,
            transcendentals=groups * HEADS * contacts * contacts,
        ),
        name="forward",
    )(place, *small, *features)


def backward(place, upstream, kept, w_out, tm_count):
    blocks, rows, span = upstream.shape
    contacts = rows * blocks
    width = w_out.shape[0]
    groups = span // width
    chunk = (4 * width // tm_count, width)
    return pl.pallas_call(
        functools.partial(backward_kernel, blocks),
        grid=(groups,),
        in_specs=[
            index_spec(), whole(w_out.shape),
            pl.BlockSpec((blocks, rows, width), lambda i: (0, 0, i)),
        ]
        + [
            pl.BlockSpec((item.shape[0], item.shape[1] // groups), lambda i: (0, i))
            for item in kept
        ],
        out_specs=[whole(chunk)] * tm_count,
        out_shape=[jax.ShapeDtypeStruct(chunk, BF16)] * tm_count,
        scratch_shapes=[
            pltpu.VMEM((4, width, width), F32),
            pltpu.VMEM((tm_count,) + chunk, BF16),
            pltpu.VMEM((contacts, HEADS * contacts), BF16),
        ],
        compiler_params=params(),
        cost_estimate=pl.CostEstimate(
            flops=groups * 5 * 10**9, bytes_accessed=20 * contacts * span, transcendentals=0
        ),
        name="backward",
    )(place, w_out, upstream, *kept)


def place_all(place, parts):
    rows, width = parts[0].shape
    ways = len(parts)

    def body(place_ref, *refs):
        for k in range(ways):
            refs[-1][place_ref[0] ^ k] = refs[k][...].astype(F32)

    shape = (ways, rows, width)
    return pl.pallas_call(
        body,
        in_specs=[index_spec()] + [pl.BlockSpec((rows, width), lambda: (0, 0))] * ways,
        out_specs=pl.BlockSpec(shape, lambda: (0, 0, 0)),
        out_shape=jax.ShapeDtypeStruct(shape, F32),
        compiler_params=params(),
        name="place_all",
    )(place, *parts)


def swap(value, axis, k):
    return lax.ppermute(value, axis, [(i, i ^ k) for i in range(lax.axis_size(axis))])


def swap_all(parts, axis):
    moved = [swap(parts[k], axis, k) for k in range(len(parts) - 1, 0, -1)]
    return [parts[0]] + moved[::-1]


def exchange(value, axis):
    return lax.all_to_all(value, axis, split_axis=0, concat_axis=0, tiled=True)


def local(
    signal, fir_taps, neighbours, live_mask, lap_coef, w_query, w_key, w_value, w_out, cotangent
):
    batch, contacts_here, slab = signal.shape
    rim_width = fir_taps.shape[1] - 1
    width = w_query.shape[0]
    tm_count = lax.axis_size("tm")
    count = lax.axis_size("contact")
    pieces = count // batch
    span = slab // pieces
    place = jnp.stack([lax.axis_index("tm"), lax.axis_index("contact")]).astype(jnp.int32)

    if pieces > 1:
        cotangent = cotangent.reshape(batch, contacts_here, pieces, span)
        cotangent = cotangent.transpose(0, 2, 1, 3).reshape(count, contacts_here, span)
    rim = lax.ppermute(
        signal[:, :, slab - rim_width :], "tm", [(i, i + 1) for i in range(tm_count - 1)]
    )
    filtered = filter_all(place, signal, rim, fir_taps, count)
    features = swap_all(filtered, "contact")
    arrived = count - max(2, count // 4)
    features[arrived:], cotangent = lax.optimization_barrier((features[arrived:], cotangent))
    upstream = exchange(cotangent, "contact")
    attended, *kept = forward(
        place, features, neighbours.T, live_mask[None], lap_coef[None],
        [w_query, w_key, w_value, w_out],
    )
    returned = exchange(attended, "contact")
    grads = backward(place, upstream, kept, w_out, tm_count)
    grads = swap_all(grads, "tm")
    part = sum(piece.astype(F32) for piece in grads).astype(BF16)
    part, _ = lax.optimization_barrier((part, returned))
    part = exchange(part, "contact").reshape(count, -1, width)
    grad_scale = (batch * (slab // width) * tm_count * neighbours.shape[0]) ** (-0.5)
    mine = (jnp.sum(part.astype(F32), axis=0) * grad_scale).astype(BF16)
    chunk = exchange(jnp.concatenate([mine] * count, axis=0), "contact")
    summed = place_all(place, swap_all([chunk] * tm_count, "tm"))
    if pieces > 1:
        returned = returned.reshape(batch, pieces, contacts_here, span)
        returned = returned.transpose(0, 2, 1, 3).reshape(batch, contacts_here, slab)
    return (returned, summed.reshape(4, width, width))


def solution(mesh):
    in_specs = (
        P(None, "contact", "tm"),
        P("contact", None),
        P(),
        P(),
        P(),
        P(),
        P(),
        P(),
        P(),
        P(None, "contact", "tm"),
    )
    out_specs = (P(None, "contact", "tm"), P())
    return jax.shard_map(local, mesh=mesh, in_specs=in_specs, out_specs=out_specs, check_vma=False)
```

```python
import functools

import jax
import jax.numpy as jnp
from jax import lax
from jax.experimental import pallas as pl
from jax.experimental.pallas import tpu as pltpu
from jax.sharding import PartitionSpec as P

HEADS = 4
F32 = jnp.float32
BF16 = jnp.bfloat16


def mm(left, right, left_dim=1, right_dim=0):
    return lax.dot_general(
        left, right, (((left_dim,), (right_dim,)), ((), ())), preferred_element_type=F32
    )


def index_spec():
    return pl.BlockSpec(memory_space=pltpu.SMEM)


def params():
    return pltpu.CompilerParams(vmem_limit_bytes=56 * 2**20)


def filter_kernel(place_ref, sig_ref, rim_ref, taps_ref, *refs):
    out_refs, kept = refs[:-1], refs[-1]
    batch, rows, slab = sig_ref.shape
    width = rim_ref.shape[2]
    blocks = slab // width
    pieces = len(out_refs) // batch
    span = slab // pieces
    signal = jnp.swapaxes(sig_ref[...].astype(F32), 0, 1)
    rim = jnp.swapaxes(rim_ref[...].astype(F32), 0, 1)
    taps = taps_ref[...].astype(F32)
    first = lax.broadcasted_iota(jnp.int32, (rows, width), 1) == 0
    taps = jnp.concatenate(
        [taps[:, :width], jnp.where(first, taps[:, width : width + 1], 0.0)], axis=1
    )
    results = []
    for row in range(rows):
        own = [signal[row, :, j * width : (j + 1) * width] for j in range(blocks)]
        current = jnp.concatenate(own, axis=0)
        before = jnp.concatenate([rim[row]] + own[:-1], axis=0)
        window = jnp.concatenate([before, current], axis=1).astype(BF16)
        spread = jnp.broadcast_to(taps[row : row + 1, :], (width, 2 * width))
        rolled = pltpu.roll(spread, 0, 1, stride=1, stride_axis=0)
        table = jnp.concatenate([rolled[:, width:], rolled[:, :width]], axis=0).astype(BF16)
        product = mm(window, table)
        results.append(
            jnp.concatenate(
                [product[j * batch : (j + 1) * batch] for j in range(blocks)], axis=1
            )
        )
    filtered = jnp.swapaxes(jnp.stack(results, axis=0), 0, 1).astype(BF16)
    for index in range(batch):
        for piece in range(pieces):
            kept[index * pieces + piece] = filtered[index, :, piece * span : (piece + 1) * span]
    me = place_ref[1]
    for k, out_ref in enumerate(out_refs):
        out_ref[...] = kept[me ^ k]


def filter_all(place, signal, rim, taps, count):
    batch, contacts, slab = signal.shape
    width = rim.shape[2]
    rows = 16
    span = slab * batch // count
    return pl.pallas_call(
        filter_kernel,
        grid=(contacts // rows,),
        in_specs=[
            index_spec(),
            pl.BlockSpec((batch, rows, slab), lambda i: (0, i, 0)),
            pl.BlockSpec((batch, rows, width), lambda i: (0, i, 0)),
            pl.BlockSpec((rows, taps.shape[1]), lambda i: (i, 0)),
        ],
        out_specs=[pl.BlockSpec((rows, span), lambda i: (i, 0))] * count,
        out_shape=[jax.ShapeDtypeStruct((contacts, span), BF16)] * count,
        scratch_shapes=[pltpu.VMEM((count, rows, span), BF16)],
        compiler_params=params(),
        cost_estimate=pl.CostEstimate(
            flops=4 * batch * contacts * slab * width,
            bytes_accessed=4 * batch * contacts * slab,
            transcendentals=0,
        ),
        name="filter",
    )(place, signal, rim, taps)


def pair_masks(pair):
    lane = lax.broadcasted_iota(jnp.int32, (1, pair), 1)
    return [(lane < pair // 2).astype(F32).astype(BF16), (lane >= pair // 2).astype(F32).astype(BF16)]


def head_masks(width):
    lane_head = lax.broadcasted_iota(jnp.int32, (1, width), 1) // (width // HEADS)
    return [(lane_head == h).astype(F32) for h in range(HEADS)]


def forward_kernel(
    blocks, place_ref, nbr_ref, live_ref, coef_ref, wq_ref, wk_ref, wv_ref, wo_ref, *refs
):
    feat_refs = refs[:blocks]
    (
        out_ref, prob_ref, value_ref, keys_ref, query_t_ref, normed_ref, normed_t_ref, mixed_ref,
        mixed_t_ref, inverse_ref, counts, columns, packed, live_row, turned_w,
    ) = refs[blocks:]
    rows, width = feat_refs[0].shape
    contacts = rows * blocks
    scale = (width // HEADS) ** (-0.5)
    slots = nbr_ref.shape[0]
    me = place_ref[1]

    @pl.when(pl.program_id(0) == 0)
    def _():
        packed[...] = jnp.zeros_like(packed)
        packed[0:1, :] = live_ref[...].astype(F32)
        packed[1:2, :] = coef_ref[...]
        for slot in range(slots):
            packed[2 + slot : 3 + slot, :] = nbr_ref[slot : slot + 1, :].astype(F32)
        columns[...] = packed[...].T
        turned = jnp.concatenate(
            [columns[pl.ds(pl.multiple_of((me ^ k) * rows, rows), rows), :] for k in range(blocks)],
            axis=0,
        )
        alive = turned.T[0:1]
        live_row[...] = alive
        ids = lax.broadcasted_iota(jnp.int32, (contacts, contacts), 1)
        total = jnp.zeros((contacts, contacts), F32)
        for slot in range(slots):
            here = turned[:, slot + 2 : slot + 3].astype(jnp.int32) ^ (me * rows)
            total = total + jnp.where(here == ids, alive, 0.0)
        counts[...] = total.astype(BF16)
        columns[:, 0:1] = turned[:, 0:1]
        columns[:, 1:2] = turned[:, 1:2]
        columns[:, 2:3] = jnp.sum(total, axis=1, keepdims=True)
        turned_w[0] = wq_ref[...].T
        turned_w[1] = wk_ref[...].T

    live = columns[:, 0:1]
    coef = columns[:, 1:2]
    field = jnp.concatenate([ref[...] for ref in feat_refs], axis=0)
    middle = field.astype(F32)
    beside = mm(counts[...], field)
    ready = live * (middle + coef * (beside - columns[:, 2:3] * middle))
    ready = ready.astype(BF16).astype(F32)
    mean_square = jnp.mean(ready * ready, axis=1, keepdims=True)
    normed = (ready * lax.rsqrt(mean_square + 1e-05)).astype(BF16)
    query = (mm(normed, wq_ref[...]) * scale).astype(BF16)
    keys = mm(normed, wk_ref[...]).astype(BF16)
    value = mm(normed, wv_ref[...]).astype(BF16)
    normed_t = normed.T
    keys_t = mm(turned_w[1], normed_t).astype(BF16)
    value_ref[...] = value
    keys_ref[...] = keys
    query_t_ref[...] = (mm(turned_w[0], normed_t) * scale).astype(BF16)
    normed_ref[...] = normed
    normed_t_ref[...] = normed_t
    pair = 2 * width // HEADS
    masks = pair_masks(pair)

    def score(h):
        lanes = slice(h // 2 * pair, (h // 2 + 1) * pair)
        return mm(query[:, lanes] * masks[h % 2], keys_t[lanes, :])

    bias = jnp.where(live_row[...] > 0, 0.0, -1e30)
    block = min(64, contacts)
    scores = score(0)
    products = []
    for h in range(HEADS):
        following = score(h + 1) if h + 1 < HEADS else None
        columns_h = slice(h * contacts, (h + 1) * contacts)
        for r in range(contacts // block):
            here = slice(r * block, (r + 1) * block)
            part = scores[here] + bias
            raised = jnp.exp(part - jnp.max(part, axis=1, keepdims=True))
            prob_ref[here, columns_h] = raised.astype(BF16)
        lanes = slice(h // 2 * pair, (h // 2 + 1) * pair)
        with_ones = value[:, lanes] * masks[h % 2] + masks[1 - h % 2]
        products.append(mm(prob_ref[:, columns_h], with_ones))
        scores = following
    low_lanes = lax.broadcasted_iota(jnp.int32, (contacts, pair), 1) < pair // 2
    mixed = []
    for p in range(HEADS // 2):
        even, odd = products[2 * p], products[2 * p + 1]
        inverse = 1.0 / pltpu.roll(jnp.where(low_lanes, odd, even), pair // 2, 1)
        inverse_ref[:, p * pair : (p + 1) * pair] = inverse
        mixed.append((jnp.where(low_lanes, even, odd) * inverse).astype(BF16))
    mixed = jnp.concatenate(mixed, axis=1)
    attended = mm(mixed, wo_ref[...]).astype(BF16)
    for k in range(blocks):
        out_ref[me ^ k] = attended[k * rows : (k + 1) * rows]
    mixed_ref[...] = mixed
    mixed_t_ref[...] = mixed.T


def backward_kernel(
    blocks, place_ref, wo_ref, up_ref, prob_ref, value_ref, keys_ref, query_t_ref, normed_ref,
    normed_t_ref, mixed_ref, mixed_t_ref, inverse_ref, *refs,
):
    out_refs, total, chunks, changes = refs[:-3], refs[-3], refs[-2], refs[-1]
    contacts, width = normed_ref.shape
    head = width // HEADS
    scale = head ** (-0.5)
    step = pl.program_id(0)

    @pl.when(step == 0)
    def _():
        total[...] = jnp.zeros_like(total)

    me = place_ref[1]
    upstream = jnp.concatenate([up_ref[me ^ k] for k in range(blocks)], axis=0)
    normed = normed_ref[...]
    value = value_ref[...]
    keys = keys_ref[...]
    back = mm(upstream, wo_ref[...], 1, 1).astype(BF16)
    back = (back.astype(F32) * inverse_ref[...]).astype(BF16)
    back_t = back.T
    inner = back.astype(F32) * mixed_ref[...].astype(F32)
    masks = head_masks(width)
    grad_value_t = []
    grad_key_t = []
    grad_query = None
    low = [m.astype(BF16) for m in masks]
    block = min(64, contacts)
    grad_prob = mm(back * low[0], value, 1, 1)
    for h in range(HEADS):
        following = mm(back * low[h + 1], value, 1, 1) if h + 1 < HEADS else None
        columns_h = slice(h * contacts, (h + 1) * contacts)
        grad_value_t.append(mm(back_t[h * head : (h + 1) * head], prob_ref[:, columns_h]))
        for r in range(contacts // block):
            here = slice(r * block, (r + 1) * block)
            row_inner = jnp.sum(inner[here] * masks[h], axis=1, keepdims=True)
            shift = (grad_prob[here] - row_inner).astype(BF16)
            changes[here, columns_h] = prob_ref[here, columns_h] * shift
        grad_score = changes[:, columns_h]
        grad_key_t.append(mm(query_t_ref[h * head : (h + 1) * head, :], grad_score))
        part = mm(grad_score, keys * low[h])
        grad_query = part if grad_query is None else grad_query + part
        grad_prob = following
    grad_query = (grad_query * scale).astype(BF16)
    total[0] += mm(normed_t_ref[...], grad_query)
    total[1] += mm(jnp.concatenate(grad_key_t, axis=0).astype(BF16), normed)
    total[2] += mm(jnp.concatenate(grad_value_t, axis=0).astype(BF16), normed)
    total[3] += mm(mixed_t_ref[...], upstream)

    @pl.when(step == pl.num_programs(0) - 1)
    def _():
        count, rows = chunks.shape[:2]
        parts = [total[0], total[1].T, total[2].T, total[3]]
        for c in range(count):
            first = (c * rows) % width
            chunks[c] = parts[c * rows // width][first : first + rows].astype(BF16)
        for k, out_ref in enumerate(out_refs):
            out_ref[...] = chunks[place_ref[0] ^ k]


def whole(shape):
    return pl.BlockSpec(shape, lambda i: (0,) * len(shape))


def forward(place, features, neighbours, live, coef, weights):
    blocks = len(features)
    rows, span = features[0].shape
    contacts = rows * blocks
    width = weights[0].shape[0]
    groups = span // width
    shapes = [
        (contacts, HEADS * contacts), (contacts, width),
        (contacts, width), (width, contacts), (contacts, width), (width, contacts),
        (contacts, width), (width, contacts), (contacts, width),
    ]
    small = [neighbours, live, coef] + list(weights)
    return pl.pallas_call(
        functools.partial(forward_kernel, blocks),
        grid=(groups,),
        in_specs=[index_spec()]
        + [whole(item.shape) for item in small]
        + [pl.BlockSpec((rows, width), lambda i: (0, i))] * blocks,
        out_specs=[pl.BlockSpec((blocks, rows, width), lambda i: (0, 0, i))]
        + [pl.BlockSpec(shape, lambda i: (0, i)) for shape in shapes],
        out_shape=[jax.ShapeDtypeStruct((blocks, rows, span), BF16)]
        + [
            jax.ShapeDtypeStruct((shape[0], groups * shape[1]), kind)
            for shape, kind in zip(shapes, [BF16] * (len(shapes) - 1) + [F32])
        ],
        scratch_shapes=[
            pltpu.VMEM((contacts, contacts), BF16),
            pltpu.VMEM((contacts, 128), F32),
            pltpu.VMEM((128, contacts), F32),
            pltpu.VMEM((1, contacts), F32),
            pltpu.VMEM((2, width, width), BF16),
        ],
        compiler_params=params(),
        cost_estimate=pl.CostEstimate(
            flops=groups * 5 * 10**9,
            bytes_accessed=20 * contacts * span,
            transcendentals=groups * HEADS * contacts * contacts,
        ),
        name="forward",
    )(place, *small, *features)


def backward(place, upstream, kept, w_out, tm_count):
    blocks, rows, span = upstream.shape
    contacts = rows * blocks
    width = w_out.shape[0]
    groups = span // width
    chunk = (4 * width // tm_count, width)
    return pl.pallas_call(
        functools.partial(backward_kernel, blocks),
        grid=(groups,),
        in_specs=[
            index_spec(), whole(w_out.shape),
            pl.BlockSpec((blocks, rows, width), lambda i: (0, 0, i)),
        ]
        + [
            pl.BlockSpec((item.shape[0], item.shape[1] // groups), lambda i: (0, i))
            for item in kept
        ],
        out_specs=[whole(chunk)] * tm_count,
        out_shape=[jax.ShapeDtypeStruct(chunk, BF16)] * tm_count,
        scratch_shapes=[
            pltpu.VMEM((4, width, width), F32),
            pltpu.VMEM((tm_count,) + chunk, BF16),
            pltpu.VMEM((contacts, HEADS * contacts), BF16),
        ],
        compiler_params=params(),
        cost_estimate=pl.CostEstimate(
            flops=groups * 5 * 10**9, bytes_accessed=20 * contacts * span, transcendentals=0
        ),
        name="backward",
    )(place, w_out, upstream, *kept)


def place_all(place, parts):
    rows, width = parts[0].shape
    ways = len(parts)

    def body(place_ref, *refs):
        for k in range(ways):
            refs[-1][place_ref[0] ^ k] = refs[k][...].astype(F32)

    shape = (ways, rows, width)
    return pl.pallas_call(
        body,
        in_specs=[index_spec()] + [pl.BlockSpec((rows, width), lambda: (0, 0))] * ways,
        out_specs=pl.BlockSpec(shape, lambda: (0, 0, 0)),
        out_shape=jax.ShapeDtypeStruct(shape, F32),
        compiler_params=params(),
        name="place_all",
    )(place, *parts)


def swap(value, axis, k):
    return lax.ppermute(value, axis, [(i, i ^ k) for i in range(lax.axis_size(axis))])


def swap_all(parts, axis):
    moved = [swap(parts[k], axis, k) for k in range(len(parts) - 1, 0, -1)]
    return [parts[0]] + moved[::-1]


def exchange(value, axis):
    return lax.all_to_all(value, axis, split_axis=0, concat_axis=0, tiled=True)


def local(
    signal, fir_taps, neighbours, live_mask, lap_coef, w_query, w_key, w_value, w_out, cotangent
):
    batch, contacts_here, slab = signal.shape
    rim_width = fir_taps.shape[1] - 1
    width = w_query.shape[0]
    tm_count = lax.axis_size("tm")
    count = lax.axis_size("contact")
    pieces = count // batch
    span = slab // pieces
    place = jnp.stack([lax.axis_index("tm"), lax.axis_index("contact")]).astype(jnp.int32)

    if pieces > 1:
        cotangent = cotangent.reshape(batch, contacts_here, pieces, span)
        cotangent = cotangent.transpose(0, 2, 1, 3).reshape(count, contacts_here, span)
    rim = lax.ppermute(
        signal[:, :, slab - rim_width :], "tm", [(i, i + 1) for i in range(tm_count - 1)]
    )
    filtered = filter_all(place, signal, rim, fir_taps, count)
    features = swap_all(filtered, "contact")
    arrived = count - max(2, count // 4)
    features[arrived:], cotangent = lax.optimization_barrier((features[arrived:], cotangent))
    upstream = exchange(cotangent, "contact")
    attended, *kept = forward(
        place, features, neighbours.T, live_mask[None], lap_coef[None],
        [w_query, w_key, w_value, w_out],
    )
    returned = exchange(attended, "contact")
    grads = backward(place, upstream, kept, w_out, tm_count)
    grads = swap_all(grads, "tm")
    part = sum(piece.astype(F32) for piece in grads).astype(BF16)
    part, _ = lax.optimization_barrier((part, returned))
    grad_scale = (batch * (slab // width) * tm_count * neighbours.shape[0]) ** (-0.5)
    step = 1
    while step < count:
        both = part.astype(F32) + swap(part, "contact", step).astype(F32)
        step *= 2
        part = lax.optimization_barrier((both * (1.0 if step < count else grad_scale)).astype(BF16))
    summed = place_all(place, swap_all([part] * tm_count, "tm"))
    if pieces > 1:
        returned = returned.reshape(batch, pieces, contacts_here, span)
        returned = returned.transpose(0, 2, 1, 3).reshape(batch, contacts_here, slab)
    return (returned, summed.reshape(4, width, width))


def solution(mesh):
    in_specs = (
        P(None, "contact", "tm"),
        P("contact", None),
        P(),
        P(),
        P(),
        P(),
        P(),
        P(),
        P(),
        P(None, "contact", "tm"),
    )
    out_specs = (P(None, "contact", "tm"), P())
    return jax.shard_map(local, mesh=mesh, in_specs=in_specs, out_specs=out_specs, check_vma=False)
```

```python
import functools

import jax
import jax.numpy as jnp
from jax import lax
from jax.experimental import pallas as pl
from jax.experimental.pallas import tpu as pltpu
from jax.sharding import PartitionSpec as P

HEADS = 4
F32 = jnp.float32
BF16 = jnp.bfloat16


def mm(left, right, left_dim=1, right_dim=0):
    return lax.dot_general(
        left, right, (((left_dim,), (right_dim,)), ((), ())), preferred_element_type=F32
    )


def index_spec():
    return pl.BlockSpec(memory_space=pltpu.SMEM)


def params():
    return pltpu.CompilerParams(vmem_limit_bytes=56 * 2**20)


def filter_kernel(place_ref, sig_ref, rim_ref, taps_ref, *refs):
    out_refs, kept = refs[:-1], refs[-1]
    batch, rows, slab = sig_ref.shape
    width = rim_ref.shape[2]
    blocks = slab // width
    pieces = len(out_refs) // batch
    span = slab // pieces
    signal = jnp.swapaxes(sig_ref[...].astype(F32), 0, 1)
    rim = jnp.swapaxes(rim_ref[...].astype(F32), 0, 1)
    taps = taps_ref[...].astype(F32)
    first = lax.broadcasted_iota(jnp.int32, (rows, width), 1) == 0
    taps = jnp.concatenate(
        [taps[:, :width], jnp.where(first, taps[:, width : width + 1], 0.0)], axis=1
    )
    results = []
    for row in range(rows):
        own = [signal[row, :, j * width : (j + 1) * width] for j in range(blocks)]
        current = jnp.concatenate(own, axis=0)
        before = jnp.concatenate([rim[row]] + own[:-1], axis=0)
        window = jnp.concatenate([before, current], axis=1).astype(BF16)
        spread = jnp.broadcast_to(taps[row : row + 1, :], (width, 2 * width))
        rolled = pltpu.roll(spread, 0, 1, stride=1, stride_axis=0)
        table = jnp.concatenate([rolled[:, width:], rolled[:, :width]], axis=0).astype(BF16)
        product = mm(window, table)
        results.append(
            jnp.concatenate(
                [product[j * batch : (j + 1) * batch] for j in range(blocks)], axis=1
            )
        )
    filtered = jnp.swapaxes(jnp.stack(results, axis=0), 0, 1).astype(BF16)
    for index in range(batch):
        for piece in range(pieces):
            kept[index * pieces + piece] = filtered[index, :, piece * span : (piece + 1) * span]
    me = place_ref[1]
    for k, out_ref in enumerate(out_refs):
        out_ref[...] = kept[me ^ k]


def filter_all(place, signal, rim, taps, count):
    batch, contacts, slab = signal.shape
    width = rim.shape[2]
    rows = 16
    span = slab * batch // count
    return pl.pallas_call(
        filter_kernel,
        grid=(contacts // rows,),
        in_specs=[
            index_spec(),
            pl.BlockSpec((batch, rows, slab), lambda i: (0, i, 0)),
            pl.BlockSpec((batch, rows, width), lambda i: (0, i, 0)),
            pl.BlockSpec((rows, taps.shape[1]), lambda i: (i, 0)),
        ],
        out_specs=[pl.BlockSpec((rows, span), lambda i: (i, 0))] * count,
        out_shape=[jax.ShapeDtypeStruct((contacts, span), BF16)] * count,
        scratch_shapes=[pltpu.VMEM((count, rows, span), BF16)],
        compiler_params=params(),
        cost_estimate=pl.CostEstimate(
            flops=4 * batch * contacts * slab * width,
            bytes_accessed=4 * batch * contacts * slab,
            transcendentals=0,
        ),
        name="filter",
    )(place, signal, rim, taps)


def pair_masks(pair):
    lane = lax.broadcasted_iota(jnp.int32, (1, pair), 1)
    return [(lane < pair // 2).astype(F32).astype(BF16), (lane >= pair // 2).astype(F32).astype(BF16)]


def head_masks(width):
    lane_head = lax.broadcasted_iota(jnp.int32, (1, width), 1) // (width // HEADS)
    return [(lane_head == h).astype(F32) for h in range(HEADS)]


def forward_kernel(
    blocks, place_ref, nbr_ref, live_ref, coef_ref, wq_ref, wk_ref, wv_ref, wo_ref, *refs
):
    feat_refs = refs[:blocks]
    (
        out_ref, prob_ref, value_ref, keys_ref, query_t_ref, normed_ref, normed_t_ref, mixed_ref,
        mixed_t_ref, inverse_ref, counts, columns, packed, live_row, turned_w,
    ) = refs[blocks:]
    rows, width = feat_refs[0].shape
    contacts = rows * blocks
    scale = (width // HEADS) ** (-0.5)
    slots = nbr_ref.shape[0]
    me = place_ref[1]

    @pl.when(pl.program_id(0) == 0)
    def _():
        packed[...] = jnp.zeros_like(packed)
        packed[0:1, :] = live_ref[...].astype(F32)
        packed[1:2, :] = coef_ref[...]
        for slot in range(slots):
            packed[2 + slot : 3 + slot, :] = nbr_ref[slot : slot + 1, :].astype(F32)
        columns[...] = packed[...].T
        turned = jnp.concatenate(
            [columns[pl.ds(pl.multiple_of((me ^ k) * rows, rows), rows), :] for k in range(blocks)],
            axis=0,
        )
        alive = turned.T[0:1]
        live_row[...] = alive
        ids = lax.broadcasted_iota(jnp.int32, (contacts, contacts), 1)
        total = jnp.zeros((contacts, contacts), F32)
        for slot in range(slots):
            here = turned[:, slot + 2 : slot + 3].astype(jnp.int32) ^ (me * rows)
            total = total + jnp.where(here == ids, alive, 0.0)
        counts[...] = total.astype(BF16)
        columns[:, 0:1] = turned[:, 0:1]
        columns[:, 1:2] = turned[:, 1:2]
        columns[:, 2:3] = jnp.sum(total, axis=1, keepdims=True)
        turned_w[0] = wq_ref[...].T
        turned_w[1] = wk_ref[...].T

    live = columns[:, 0:1]
    coef = columns[:, 1:2]
    field = jnp.concatenate([ref[...] for ref in feat_refs], axis=0)
    middle = field.astype(F32)
    beside = mm(counts[...], field)
    ready = live * (middle + coef * (beside - columns[:, 2:3] * middle))
    ready = ready.astype(BF16).astype(F32)
    mean_square = jnp.mean(ready * ready, axis=1, keepdims=True)
    normed = (ready * lax.rsqrt(mean_square + 1e-05)).astype(BF16)
    query = (mm(normed, wq_ref[...]) * scale).astype(BF16)
    keys = mm(normed, wk_ref[...]).astype(BF16)
    value = mm(normed, wv_ref[...]).astype(BF16)
    normed_t = normed.T
    keys_t = mm(turned_w[1], normed_t).astype(BF16)
    value_ref[...] = value
    keys_ref[...] = keys
    query_t_ref[...] = (mm(turned_w[0], normed_t) * scale).astype(BF16)
    normed_ref[...] = normed
    normed_t_ref[...] = normed_t
    pair = 2 * width // HEADS
    masks = pair_masks(pair)

    def score(h):
        lanes = slice(h // 2 * pair, (h // 2 + 1) * pair)
        return mm(query[:, lanes] * masks[h % 2], keys_t[lanes, :])

    bias = jnp.where(live_row[...] > 0, 0.0, -1e30)
    block = min(64, contacts)
    scores = score(0)
    products = []
    for h in range(HEADS):
        following = score(h + 1) if h + 1 < HEADS else None
        columns_h = slice(h * contacts, (h + 1) * contacts)
        for r in range(contacts // block):
            here = slice(r * block, (r + 1) * block)
            part = scores[here] + bias
            raised = jnp.exp(part - jnp.max(part, axis=1, keepdims=True))
            prob_ref[here, columns_h] = raised.astype(BF16)
        lanes = slice(h // 2 * pair, (h // 2 + 1) * pair)
        with_ones = value[:, lanes] * masks[h % 2] + masks[1 - h % 2]
        products.append(mm(prob_ref[:, columns_h], with_ones))
        scores = following
    low_lanes = lax.broadcasted_iota(jnp.int32, (contacts, pair), 1) < pair // 2
    mixed = []
    for p in range(HEADS // 2):
        even, odd = products[2 * p], products[2 * p + 1]
        inverse = 1.0 / pltpu.roll(jnp.where(low_lanes, odd, even), pair // 2, 1)
        inverse_ref[:, p * pair : (p + 1) * pair] = inverse
        mixed.append((jnp.where(low_lanes, even, odd) * inverse).astype(BF16))
    mixed = jnp.concatenate(mixed, axis=1)
    attended = mm(mixed, wo_ref[...]).astype(BF16)
    for k in range(blocks):
        out_ref[me ^ k] = attended[k * rows : (k + 1) * rows]
    mixed_ref[...] = mixed
    mixed_t_ref[...] = mixed.T


def backward_kernel(
    blocks, place_ref, wo_ref, up_ref, prob_ref, value_ref, keys_ref, query_t_ref, normed_ref,
    normed_t_ref, mixed_ref, mixed_t_ref, inverse_ref, *refs,
):
    out_refs, total, chunks, changes = refs[:-3], refs[-3], refs[-2], refs[-1]
    contacts, width = normed_ref.shape
    head = width // HEADS
    scale = head ** (-0.5)
    step = pl.program_id(0)

    @pl.when(step == 0)
    def _():
        total[...] = jnp.zeros_like(total)

    me = place_ref[1]
    upstream = jnp.concatenate([up_ref[me ^ k] for k in range(blocks)], axis=0)
    normed = normed_ref[...]
    value = value_ref[...]
    keys = keys_ref[...]
    back = mm(upstream, wo_ref[...], 1, 1).astype(BF16)
    back = (back.astype(F32) * inverse_ref[...]).astype(BF16)
    back_t = back.T
    inner = back.astype(F32) * mixed_ref[...].astype(F32)
    masks = head_masks(width)
    grad_value_t = []
    grad_key_t = []
    grad_query = None
    low = [m.astype(BF16) for m in masks]
    block = min(64, contacts)
    grad_prob = mm(back * low[0], value, 1, 1)
    for h in range(HEADS):
        following = mm(back * low[h + 1], value, 1, 1) if h + 1 < HEADS else None
        columns_h = slice(h * contacts, (h + 1) * contacts)
        grad_value_t.append(mm(back_t[h * head : (h + 1) * head], prob_ref[:, columns_h]))
        for r in range(contacts // block):
            here = slice(r * block, (r + 1) * block)
            row_inner = jnp.sum(inner[here] * masks[h], axis=1, keepdims=True)
            shift = (grad_prob[here] - row_inner).astype(BF16)
            changes[here, columns_h] = prob_ref[here, columns_h] * shift
        grad_score = changes[:, columns_h]
        grad_key_t.append(mm(query_t_ref[h * head : (h + 1) * head, :], grad_score))
        part = mm(grad_score, keys * low[h])
        grad_query = part if grad_query is None else grad_query + part
        grad_prob = following
    grad_query = (grad_query * scale).astype(BF16)
    total[0] += mm(normed_t_ref[...], grad_query)
    total[1] += mm(jnp.concatenate(grad_key_t, axis=0).astype(BF16), normed)
    total[2] += mm(jnp.concatenate(grad_value_t, axis=0).astype(BF16), normed)
    total[3] += mm(mixed_t_ref[...], upstream)

    @pl.when(step == pl.num_programs(0) - 1)
    def _():
        count, rows = chunks.shape[:2]
        parts = [total[0], total[1].T, total[2].T, total[3]]
        for c in range(count):
            first = (c * rows) % width
            chunks[c] = parts[c * rows // width][first : first + rows].astype(BF16)
        for k, out_ref in enumerate(out_refs):
            out_ref[...] = chunks[place_ref[0] ^ k]


def whole(shape):
    return pl.BlockSpec(shape, lambda i: (0,) * len(shape))


def forward(place, features, neighbours, live, coef, weights):
    blocks = len(features)
    rows, span = features[0].shape
    contacts = rows * blocks
    width = weights[0].shape[0]
    groups = span // width
    shapes = [
        (contacts, HEADS * contacts), (contacts, width),
        (contacts, width), (width, contacts), (contacts, width), (width, contacts),
        (contacts, width), (width, contacts), (contacts, width),
    ]
    small = [neighbours, live, coef] + list(weights)
    return pl.pallas_call(
        functools.partial(forward_kernel, blocks),
        grid=(groups,),
        in_specs=[index_spec()]
        + [whole(item.shape) for item in small]
        + [pl.BlockSpec((rows, width), lambda i: (0, i))] * blocks,
        out_specs=[pl.BlockSpec((blocks, rows, width), lambda i: (0, 0, i))]
        + [pl.BlockSpec(shape, lambda i: (0, i)) for shape in shapes],
        out_shape=[jax.ShapeDtypeStruct((blocks, rows, span), BF16)]
        + [
            jax.ShapeDtypeStruct((shape[0], groups * shape[1]), kind)
            for shape, kind in zip(shapes, [BF16] * (len(shapes) - 1) + [F32])
        ],
        scratch_shapes=[
            pltpu.VMEM((contacts, contacts), BF16),
            pltpu.VMEM((contacts, 128), F32),
            pltpu.VMEM((128, contacts), F32),
            pltpu.VMEM((1, contacts), F32),
            pltpu.VMEM((2, width, width), BF16),
        ],
        compiler_params=params(),
        cost_estimate=pl.CostEstimate(
            flops=groups * 5 * 10**9,
            bytes_accessed=20 * contacts * span,
            transcendentals=groups * HEADS * contacts * contacts,
        ),
        name="forward",
    )(place, *small, *features)


def backward(place, upstream, kept, w_out, tm_count):
    blocks, rows, span = upstream.shape
    contacts = rows * blocks
    width = w_out.shape[0]
    groups = span // width
    chunk = (4 * width // tm_count, width)
    return pl.pallas_call(
        functools.partial(backward_kernel, blocks),
        grid=(groups,),
        in_specs=[
            index_spec(), whole(w_out.shape),
            pl.BlockSpec((blocks, rows, width), lambda i: (0, 0, i)),
        ]
        + [
            pl.BlockSpec((item.shape[0], item.shape[1] // groups), lambda i: (0, i))
            for item in kept
        ],
        out_specs=[whole(chunk)] * tm_count,
        out_shape=[jax.ShapeDtypeStruct(chunk, BF16)] * tm_count,
        scratch_shapes=[
            pltpu.VMEM((4, width, width), F32),
            pltpu.VMEM((tm_count,) + chunk, BF16),
            pltpu.VMEM((contacts, HEADS * contacts), BF16),
        ],
        compiler_params=params(),
        cost_estimate=pl.CostEstimate(
            flops=groups * 5 * 10**9, bytes_accessed=20 * contacts * span, transcendentals=0
        ),
        name="backward",
    )(place, w_out, upstream, *kept)


def place_all(place, parts):
    rows, width = parts[0].shape
    ways = len(parts)

    def body(place_ref, *refs):
        for k in range(ways):
            refs[-1][place_ref[0] ^ k] = refs[k][...].astype(F32)

    shape = (ways, rows, width)
    return pl.pallas_call(
        body,
        in_specs=[index_spec()] + [pl.BlockSpec((rows, width), lambda: (0, 0))] * ways,
        out_specs=pl.BlockSpec(shape, lambda: (0, 0, 0)),
        out_shape=jax.ShapeDtypeStruct(shape, F32),
        compiler_params=params(),
        name="place_all",
    )(place, *parts)


def swap(value, axis, k):
    return lax.ppermute(value, axis, [(i, i ^ k) for i in range(lax.axis_size(axis))])


def swap_all(parts, axis):
    moved = [swap(parts[k], axis, k) for k in range(len(parts) - 1, 0, -1)]
    return [parts[0]] + moved[::-1]


def exchange(value, axis):
    return lax.all_to_all(value, axis, split_axis=0, concat_axis=0, tiled=True)


def local(
    signal, fir_taps, neighbours, live_mask, lap_coef, w_query, w_key, w_value, w_out, cotangent
):
    batch, contacts_here, slab = signal.shape
    rim_width = fir_taps.shape[1] - 1
    width = w_query.shape[0]
    tm_count = lax.axis_size("tm")
    count = lax.axis_size("contact")
    pieces = count // batch
    span = slab // pieces
    place = jnp.stack([lax.axis_index("tm"), lax.axis_index("contact")]).astype(jnp.int32)

    if pieces > 1:
        cotangent = cotangent.reshape(batch, contacts_here, pieces, span)
        cotangent = cotangent.transpose(0, 2, 1, 3).reshape(count, contacts_here, span)
    rim = lax.ppermute(
        signal[:, :, slab - rim_width :], "tm", [(i, i + 1) for i in range(tm_count - 1)]
    )
    filtered = filter_all(place, signal, rim, fir_taps, count)
    features = swap_all(filtered, "contact")
    arrived = count - max(2, count // 4)
    features[arrived:], cotangent = lax.optimization_barrier((features[arrived:], cotangent))
    upstream = exchange(cotangent, "contact")
    attended, *kept = forward(
        place, features, neighbours.T, live_mask[None], lap_coef[None],
        [w_query, w_key, w_value, w_out],
    )
    grads = backward(place, upstream, kept, w_out, tm_count)
    attended, grads = lax.optimization_barrier((attended, grads))
    returned = exchange(attended, "contact")
    grads = swap_all(grads, "tm")
    part = sum(piece.astype(F32) for piece in grads).astype(BF16)
    grad_scale = (batch * (slab // width) * tm_count * neighbours.shape[0]) ** (-0.5)
    step = 1
    while step < count:
        both = part.astype(F32) + swap(part, "contact", step).astype(F32)
        step *= 2
        part = lax.optimization_barrier((both * (1.0 if step < count else grad_scale)).astype(BF16))
    part, _ = lax.optimization_barrier((part, returned))
    summed = place_all(place, swap_all([part] * tm_count, "tm"))
    if pieces > 1:
        returned = returned.reshape(batch, pieces, contacts_here, span)
        returned = returned.transpose(0, 2, 1, 3).reshape(batch, contacts_here, slab)
    return (returned, summed.reshape(4, width, width))


def solution(mesh):
    in_specs = (
        P(None, "contact", "tm"),
        P("contact", None),
        P(),
        P(),
        P(),
        P(),
        P(),
        P(),
        P(),
        P(None, "contact", "tm"),
    )
    out_specs = (P(None, "contact", "tm"), P())
    return jax.shard_map(local, mesh=mesh, in_specs=in_specs, out_specs=out_specs, check_vma=False)
```

```python
import functools

import jax
import jax.numpy as jnp
from jax import lax
from jax.experimental import pallas as pl
from jax.experimental.pallas import tpu as pltpu
from jax.sharding import PartitionSpec as P

HEADS = 4
F32 = jnp.float32
BF16 = jnp.bfloat16


def mm(left, right, left_dim=1, right_dim=0):
    return lax.dot_general(
        left, right, (((left_dim,), (right_dim,)), ((), ())), preferred_element_type=F32
    )


def index_spec():
    return pl.BlockSpec(memory_space=pltpu.SMEM)


def params(mebibytes=56):
    return pltpu.CompilerParams(vmem_limit_bytes=mebibytes * 2**20)


def filter_kernel(place_ref, sig_ref, rim_ref, taps_ref, *refs):
    out_refs, kept = refs[:-1], refs[-1]
    batch, rows, slab = sig_ref.shape
    width = rim_ref.shape[2]
    blocks = slab // width
    pieces = len(out_refs) // batch
    span = slab // pieces
    signal = jnp.swapaxes(sig_ref[...].astype(F32), 0, 1)
    rim = jnp.swapaxes(rim_ref[...].astype(F32), 0, 1)
    taps = taps_ref[...].astype(F32)
    first = lax.broadcasted_iota(jnp.int32, (rows, width), 1) == 0
    taps = jnp.concatenate(
        [taps[:, :width], jnp.where(first, taps[:, width : width + 1], 0.0)], axis=1
    )
    results = []
    for row in range(rows):
        own = [signal[row, :, j * width : (j + 1) * width] for j in range(blocks)]
        current = jnp.concatenate(own, axis=0)
        before = jnp.concatenate([rim[row]] + own[:-1], axis=0)
        window = jnp.concatenate([before, current], axis=1).astype(BF16)
        spread = jnp.broadcast_to(taps[row : row + 1, :], (width, 2 * width))
        rolled = pltpu.roll(spread, 0, 1, stride=1, stride_axis=0)
        table = jnp.concatenate([rolled[:, width:], rolled[:, :width]], axis=0).astype(BF16)
        product = mm(window, table)
        results.append(
            jnp.concatenate(
                [product[j * batch : (j + 1) * batch] for j in range(blocks)], axis=1
            )
        )
    filtered = jnp.swapaxes(jnp.stack(results, axis=0), 0, 1).astype(BF16)
    for index in range(batch):
        for piece in range(pieces):
            kept[index * pieces + piece] = filtered[index, :, piece * span : (piece + 1) * span]
    me = place_ref[1]
    for k, out_ref in enumerate(out_refs):
        out_ref[...] = kept[me ^ k]


def filter_all(place, signal, rim, taps, count):
    batch, contacts, slab = signal.shape
    width = rim.shape[2]
    rows = 16
    span = slab * batch // count
    return pl.pallas_call(
        filter_kernel,
        grid=(contacts // rows,),
        in_specs=[
            index_spec(),
            pl.BlockSpec((batch, rows, slab), lambda i: (0, i, 0)),
            pl.BlockSpec((batch, rows, width), lambda i: (0, i, 0)),
            pl.BlockSpec((rows, taps.shape[1]), lambda i: (i, 0)),
        ],
        out_specs=[pl.BlockSpec((rows, span), lambda i: (i, 0))] * count,
        out_shape=[jax.ShapeDtypeStruct((contacts, span), BF16)] * count,
        scratch_shapes=[pltpu.VMEM((count, rows, span), BF16)],
        compiler_params=params(),
        cost_estimate=pl.CostEstimate(
            flops=4 * batch * contacts * slab * width,
            bytes_accessed=4 * batch * contacts * slab,
            transcendentals=0,
        ),
        name="filter",
    )(place, signal, rim, taps)


def pair_masks(pair):
    lane = lax.broadcasted_iota(jnp.int32, (1, pair), 1)
    return [(lane < pair // 2).astype(F32).astype(BF16), (lane >= pair // 2).astype(F32).astype(BF16)]


def head_masks(width):
    lane_head = lax.broadcasted_iota(jnp.int32, (1, width), 1) // (width // HEADS)
    return [(lane_head == h).astype(F32) for h in range(HEADS)]


def forward_kernel(
    blocks, place_ref, nbr_ref, live_ref, coef_ref, wq_ref, wk_ref, wv_ref, wo_ref, *refs
):
    feat_refs = refs[:blocks]
    (
        out_ref, prob_ref, value_ref, keys_ref, query_t_ref, normed_ref, normed_t_ref, mixed_ref,
        mixed_t_ref, inverse_ref, counts, columns, packed, live_row, turned_w,
    ) = refs[blocks:]
    rows, width = feat_refs[0].shape
    contacts = rows * blocks
    scale = (width // HEADS) ** (-0.5)
    slots = nbr_ref.shape[0]
    me = place_ref[1]

    @pl.when(pl.program_id(0) == 0)
    def _():
        packed[...] = jnp.zeros_like(packed)
        packed[0:1, :] = live_ref[...].astype(F32)
        packed[1:2, :] = coef_ref[...]
        for slot in range(slots):
            packed[2 + slot : 3 + slot, :] = nbr_ref[slot : slot + 1, :].astype(F32)
        columns[...] = packed[...].T
        turned = jnp.concatenate(
            [columns[pl.ds(pl.multiple_of((me ^ k) * rows, rows), rows), :] for k in range(blocks)],
            axis=0,
        )
        alive = turned.T[0:1]
        live_row[...] = alive
        ids = lax.broadcasted_iota(jnp.int32, (contacts, contacts), 1)
        total = jnp.zeros((contacts, contacts), F32)
        for slot in range(slots):
            here = turned[:, slot + 2 : slot + 3].astype(jnp.int32) ^ (me * rows)
            total = total + jnp.where(here == ids, alive, 0.0)
        counts[...] = total.astype(BF16)
        columns[:, 0:1] = turned[:, 0:1]
        columns[:, 1:2] = turned[:, 1:2]
        columns[:, 2:3] = jnp.sum(total, axis=1, keepdims=True)
        turned_w[0] = wq_ref[...].T
        turned_w[1] = wk_ref[...].T

    live = columns[:, 0:1]
    coef = columns[:, 1:2]
    field = jnp.concatenate([ref[...] for ref in feat_refs], axis=0)
    middle = field.astype(F32)
    beside = mm(counts[...], field)
    ready = live * (middle + coef * (beside - columns[:, 2:3] * middle))
    ready = ready.astype(BF16).astype(F32)
    mean_square = jnp.mean(ready * ready, axis=1, keepdims=True)
    normed = (ready * lax.rsqrt(mean_square + 1e-05)).astype(BF16)
    query = (mm(normed, wq_ref[...]) * scale).astype(BF16)
    keys = mm(normed, wk_ref[...]).astype(BF16)
    value = mm(normed, wv_ref[...]).astype(BF16)
    normed_t = normed.T
    keys_t = mm(turned_w[1], normed_t).astype(BF16)
    value_ref[...] = value
    keys_ref[...] = keys
    query_t_ref[...] = (mm(turned_w[0], normed_t) * scale).astype(BF16)
    normed_ref[...] = normed
    normed_t_ref[...] = normed_t
    pair = 2 * width // HEADS
    masks = pair_masks(pair)

    def score(h):
        lanes = slice(h // 2 * pair, (h // 2 + 1) * pair)
        return mm(query[:, lanes] * masks[h % 2], keys_t[lanes, :])

    bias = jnp.where(live_row[...] > 0, 0.0, -1e30)
    block = min(64, contacts)
    scores = score(0)
    products = []
    for h in range(HEADS):
        following = score(h + 1) if h + 1 < HEADS else None
        columns_h = slice(h * contacts, (h + 1) * contacts)
        for r in range(contacts // block):
            here = slice(r * block, (r + 1) * block)
            part = scores[here] + bias
            raised = jnp.exp(part - jnp.max(part, axis=1, keepdims=True))
            prob_ref[here, columns_h] = raised.astype(BF16)
        lanes = slice(h // 2 * pair, (h // 2 + 1) * pair)
        with_ones = value[:, lanes] * masks[h % 2] + masks[1 - h % 2]
        products.append(mm(prob_ref[:, columns_h], with_ones))
        scores = following
    low_lanes = lax.broadcasted_iota(jnp.int32, (contacts, pair), 1) < pair // 2
    mixed = []
    for p in range(HEADS // 2):
        even, odd = products[2 * p], products[2 * p + 1]
        inverse = 1.0 / pltpu.roll(jnp.where(low_lanes, odd, even), pair // 2, 1)
        inverse_ref[:, p * pair : (p + 1) * pair] = inverse
        mixed.append((jnp.where(low_lanes, even, odd) * inverse).astype(BF16))
    mixed = jnp.concatenate(mixed, axis=1)
    attended = mm(mixed, wo_ref[...]).astype(BF16)
    for k in range(blocks):
        out_ref[me ^ k] = attended[k * rows : (k + 1) * rows]
    mixed_ref[...] = mixed
    mixed_t_ref[...] = mixed.T


def backward_kernel(
    blocks, place_ref, wo_ref, up_ref, prob_ref, value_ref, keys_ref, query_t_ref, normed_ref,
    normed_t_ref, mixed_ref, mixed_t_ref, inverse_ref, *refs,
):
    out_refs, total, chunks, changes = refs[:-3], refs[-3], refs[-2], refs[-1]
    contacts, width = normed_ref.shape
    head = width // HEADS
    scale = head ** (-0.5)
    step = pl.program_id(0)

    @pl.when(step == 0)
    def _():
        total[...] = jnp.zeros_like(total)

    me = place_ref[1]
    upstream = jnp.concatenate([up_ref[me ^ k] for k in range(blocks)], axis=0)
    normed = normed_ref[...]
    value = value_ref[...]
    keys = keys_ref[...]
    back = mm(upstream, wo_ref[...], 1, 1).astype(BF16)
    back = (back.astype(F32) * inverse_ref[...]).astype(BF16)
    back_t = back.T
    inner = back.astype(F32) * mixed_ref[...].astype(F32)
    masks = head_masks(width)
    grad_value_t = []
    grad_key_t = []
    grad_query = None
    low = [m.astype(BF16) for m in masks]
    block = min(64, contacts)
    grad_prob = mm(back * low[0], value, 1, 1)
    for h in range(HEADS):
        following = mm(back * low[h + 1], value, 1, 1) if h + 1 < HEADS else None
        columns_h = slice(h * contacts, (h + 1) * contacts)
        grad_value_t.append(mm(back_t[h * head : (h + 1) * head], prob_ref[:, columns_h]))
        for r in range(contacts // block):
            here = slice(r * block, (r + 1) * block)
            row_inner = jnp.sum(inner[here] * masks[h], axis=1, keepdims=True)
            shift = (grad_prob[here] - row_inner).astype(BF16)
            changes[here, columns_h] = prob_ref[here, columns_h] * shift
        grad_score = changes[:, columns_h]
        grad_key_t.append(mm(query_t_ref[h * head : (h + 1) * head, :], grad_score))
        part = mm(grad_score, keys * low[h])
        grad_query = part if grad_query is None else grad_query + part
        grad_prob = following
    grad_query = (grad_query * scale).astype(BF16)
    total[0] += mm(normed_t_ref[...], grad_query)
    total[1] += mm(jnp.concatenate(grad_key_t, axis=0).astype(BF16), normed)
    total[2] += mm(jnp.concatenate(grad_value_t, axis=0).astype(BF16), normed)
    total[3] += mm(mixed_t_ref[...], upstream)

    @pl.when(step == pl.num_programs(0) - 1)
    def _():
        count, rows = chunks.shape[:2]
        parts = [total[0], total[1].T, total[2].T, total[3]]
        for c in range(count):
            first = (c * rows) % width
            chunks[c] = parts[c * rows // width][first : first + rows].astype(BF16)
        for k, out_ref in enumerate(out_refs):
            out_ref[...] = chunks[place_ref[0] ^ k]


def whole(shape):
    return pl.BlockSpec(shape, lambda i: (0,) * len(shape))


def forward(place, features, neighbours, live, coef, weights):
    blocks = len(features)
    rows, span = features[0].shape
    contacts = rows * blocks
    width = weights[0].shape[0]
    groups = span // width
    shapes = [
        (contacts, HEADS * contacts), (contacts, width),
        (contacts, width), (width, contacts), (contacts, width), (width, contacts),
        (contacts, width), (width, contacts), (contacts, width),
    ]
    small = [neighbours, live, coef] + list(weights)
    return pl.pallas_call(
        functools.partial(forward_kernel, blocks),
        grid=(groups,),
        in_specs=[index_spec()]
        + [whole(item.shape) for item in small]
        + [pl.BlockSpec((rows, width), lambda i: (0, i))] * blocks,
        out_specs=[pl.BlockSpec((blocks, rows, width), lambda i: (0, 0, i))]
        + [pl.BlockSpec(shape, lambda i: (0, i)) for shape in shapes],
        out_shape=[jax.ShapeDtypeStruct((blocks, rows, span), BF16)]
        + [
            jax.ShapeDtypeStruct((shape[0], groups * shape[1]), kind)
            for shape, kind in zip(shapes, [BF16] * (len(shapes) - 1) + [F32])
        ],
        scratch_shapes=[
            pltpu.VMEM((contacts, contacts), BF16),
            pltpu.VMEM((contacts, 128), F32),
            pltpu.VMEM((128, contacts), F32),
            pltpu.VMEM((1, contacts), F32),
            pltpu.VMEM((2, width, width), BF16),
        ],
        compiler_params=params(),
        cost_estimate=pl.CostEstimate(
            flops=groups * 5 * 10**9,
            bytes_accessed=20 * contacts * span,
            transcendentals=groups * HEADS * contacts * contacts,
        ),
        name="forward",
    )(place, *small, *features)


def backward(place, upstream, kept, w_out, tm_count):
    blocks, rows, span = upstream.shape
    contacts = rows * blocks
    width = w_out.shape[0]
    groups = span // width
    chunk = (4 * width // tm_count, width)
    return pl.pallas_call(
        functools.partial(backward_kernel, blocks),
        grid=(groups,),
        in_specs=[
            index_spec(), whole(w_out.shape),
            pl.BlockSpec((blocks, rows, width), lambda i: (0, 0, i)),
        ]
        + [
            pl.BlockSpec((item.shape[0], item.shape[1] // groups), lambda i: (0, i))
            for item in kept
        ],
        out_specs=[whole(chunk)] * tm_count,
        out_shape=[jax.ShapeDtypeStruct(chunk, BF16)] * tm_count,
        scratch_shapes=[
            pltpu.VMEM((4, width, width), F32),
            pltpu.VMEM((tm_count,) + chunk, BF16),
            pltpu.VMEM((contacts, HEADS * contacts), BF16),
        ],
        compiler_params=params(),
        cost_estimate=pl.CostEstimate(
            flops=groups * 5 * 10**9, bytes_accessed=20 * contacts * span, transcendentals=0
        ),
        name="backward",
    )(place, w_out, upstream, *kept)


def place_all(place, parts):
    rows, width = parts[0].shape
    ways = len(parts)

    def body(place_ref, *refs):
        for k in range(ways):
            refs[-1][place_ref[0] ^ k] = refs[k][...].astype(F32)

    shape = (ways, rows, width)
    return pl.pallas_call(
        body,
        in_specs=[index_spec()] + [pl.BlockSpec((rows, width), lambda: (0, 0))] * ways,
        out_specs=pl.BlockSpec(shape, lambda: (0, 0, 0)),
        out_shape=jax.ShapeDtypeStruct(shape, F32),
        compiler_params=params(63),
        name="place_all",
    )(place, *parts)


def write_out(value):
    def body(in_ref, out_ref):
        out_ref[...] = in_ref[...]

    spec = pl.BlockSpec((value.shape[0] // 2,) + value.shape[1:], lambda i: (i, 0, 0))
    return pl.pallas_call(
        body,
        grid=(2,),
        in_specs=[spec],
        out_specs=spec,
        out_shape=jax.ShapeDtypeStruct(value.shape, value.dtype),
        compiler_params=params(),
        cost_estimate=pl.CostEstimate(flops=0, bytes_accessed=4 * value.size, transcendentals=0),
        name="write_out",
    )(value)


def swap(value, axis, k):
    return lax.ppermute(value, axis, [(i, i ^ k) for i in range(lax.axis_size(axis))])


def swap_all(parts, axis):
    moved = [swap(parts[k], axis, k) for k in range(len(parts) - 1, 0, -1)]
    return [parts[0]] + moved[::-1]


def exchange(value, axis):
    return lax.all_to_all(value, axis, split_axis=0, concat_axis=0, tiled=True)


def local(
    signal, fir_taps, neighbours, live_mask, lap_coef, w_query, w_key, w_value, w_out, cotangent
):
    batch, contacts_here, slab = signal.shape
    rim_width = fir_taps.shape[1] - 1
    width = w_query.shape[0]
    tm_count = lax.axis_size("tm")
    count = lax.axis_size("contact")
    pieces = count // batch
    span = slab // pieces
    place = jnp.stack([lax.axis_index("tm"), lax.axis_index("contact")]).astype(jnp.int32)

    if pieces > 1:
        cotangent = cotangent.reshape(batch, contacts_here, pieces, span)
        cotangent = cotangent.transpose(0, 2, 1, 3).reshape(count, contacts_here, span)
    rim = lax.ppermute(
        signal[:, :, slab - rim_width :], "tm", [(i, i + 1) for i in range(tm_count - 1)]
    )
    filtered = filter_all(place, signal, rim, fir_taps, count)
    features = swap_all(filtered, "contact")
    arrived = count - max(2, count // 4)
    features[arrived:], cotangent = lax.optimization_barrier((features[arrived:], cotangent))
    upstream = exchange(cotangent, "contact")
    attended, *kept = forward(
        place, features, neighbours.T, live_mask[None], lap_coef[None],
        [w_query, w_key, w_value, w_out],
    )
    grads = backward(place, upstream, kept, w_out, tm_count)
    grads = swap_all(grads, "tm")
    attended, grads[1] = lax.optimization_barrier((attended, grads[1]))
    returned = exchange(attended, "contact")
    part = sum(piece.astype(F32) for piece in grads).astype(BF16)
    grad_scale = (batch * (slab // width) * tm_count * neighbours.shape[0]) ** (-0.5)
    step = 1
    while step < count:
        both = part.astype(F32) + swap(part, "contact", step).astype(F32)
        step *= 2
        part = lax.optimization_barrier((both * (1.0 if step < count else grad_scale)).astype(BF16))
    part, returned = lax.optimization_barrier((part, returned))
    returned = write_out(returned)
    summed = place_all(place, swap_all([part] * tm_count, "tm"))
    if pieces > 1:
        returned = returned.reshape(batch, pieces, contacts_here, span)
        returned = returned.transpose(0, 2, 1, 3).reshape(batch, contacts_here, slab)
    return (returned, summed.reshape(4, width, width))


def solution(mesh):
    in_specs = (
        P(None, "contact", "tm"),
        P("contact", None),
        P(),
        P(),
        P(),
        P(),
        P(),
        P(),
        P(),
        P(None, "contact", "tm"),
    )
    out_specs = (P(None, "contact", "tm"), P())
    return jax.shard_map(local, mesh=mesh, in_specs=in_specs, out_specs=out_specs, check_vma=False)
```

```python
import functools

import jax
import jax.numpy as jnp
from jax import lax
from jax.experimental import pallas as pl
from jax.experimental.pallas import tpu as pltpu
from jax.sharding import PartitionSpec as P

HEADS = 4
F32 = jnp.float32
BF16 = jnp.bfloat16


def mm(left, right, left_dim=1, right_dim=0):
    return lax.dot_general(
        left, right, (((left_dim,), (right_dim,)), ((), ())), preferred_element_type=F32
    )


def index_spec():
    return pl.BlockSpec(memory_space=pltpu.SMEM)


def params():
    return pltpu.CompilerParams(vmem_limit_bytes=56 * 2**20)


def table_kernel(taps_ref, out_ref):
    rows, depth, width = out_ref.shape
    taps = taps_ref[...].astype(F32)
    first = lax.broadcasted_iota(jnp.int32, (rows, width), 1) == 0
    taps = jnp.concatenate(
        [taps[:, :width], jnp.where(first, taps[:, width : width + 1], 0.0)], axis=1
    )
    for row in range(rows):
        spread = jnp.broadcast_to(taps[row : row + 1, :], (width, depth))
        rolled = pltpu.roll(spread, 0, 1, stride=1, stride_axis=0).astype(BF16)
        out_ref[row, :width, :] = rolled[:, width:]
        out_ref[row, width:, :] = rolled[:, :width]


def tables(taps):
    contacts, count = taps.shape
    width = count - 1
    rows = 16
    return pl.pallas_call(
        table_kernel,
        grid=(contacts // rows,),
        in_specs=[pl.BlockSpec((rows, count), lambda i: (i, 0))],
        out_specs=pl.BlockSpec((rows, 2 * width, width), lambda i: (i, 0, 0)),
        out_shape=jax.ShapeDtypeStruct((contacts, 2 * width, width), BF16),
        compiler_params=params(),
        cost_estimate=pl.CostEstimate(
            flops=contacts * width * width * 4,
            bytes_accessed=contacts * width * width * 4,
            transcendentals=0,
        ),
        name="tables",
    )(taps)


def filter_kernel(place_ref, sig_ref, rim_ref, table_ref, *refs):
    out_refs, kept = refs[:-1], refs[-1]
    batch, rows, slab = sig_ref.shape
    width = rim_ref.shape[2]
    blocks = slab // width
    pieces = len(out_refs) // batch
    span = slab // pieces
    signal = jnp.swapaxes(sig_ref[...].astype(F32), 0, 1)
    rim = jnp.swapaxes(rim_ref[...].astype(F32), 0, 1)
    results = []
    for row in range(rows):
        own = [signal[row, :, j * width : (j + 1) * width] for j in range(blocks)]
        current = jnp.concatenate(own, axis=0)
        before = jnp.concatenate([rim[row]] + own[:-1], axis=0)
        window = jnp.concatenate([before, current], axis=1).astype(BF16)
        product = mm(window, table_ref[row])
        results.append(
            jnp.concatenate(
                [product[j * batch : (j + 1) * batch] for j in range(blocks)], axis=1
            )
        )
    filtered = jnp.swapaxes(jnp.stack(results, axis=0), 0, 1).astype(BF16)
    for index in range(batch):
        for piece in range(pieces):
            kept[index * pieces + piece] = filtered[index, :, piece * span : (piece + 1) * span]
    me = place_ref[1]
    for k, out_ref in enumerate(out_refs):
        out_ref[...] = kept[me ^ k]


def filter_all(place, signal, rim, table, count):
    batch, contacts, slab = signal.shape
    width = rim.shape[2]
    rows = 16
    span = slab * batch // count
    return pl.pallas_call(
        filter_kernel,
        grid=(contacts // rows,),
        in_specs=[
            index_spec(),
            pl.BlockSpec((batch, rows, slab), lambda i: (0, i, 0)),
            pl.BlockSpec((batch, rows, width), lambda i: (0, i, 0)),
            pl.BlockSpec((rows, 2 * width, width), lambda i: (i, 0, 0)),
        ],
        out_specs=[pl.BlockSpec((rows, span), lambda i: (i, 0))] * count,
        out_shape=[jax.ShapeDtypeStruct((contacts, span), BF16)] * count,
        scratch_shapes=[pltpu.VMEM((count, rows, span), BF16)],
        compiler_params=params(),
        cost_estimate=pl.CostEstimate(
            flops=4 * batch * contacts * slab * width,
            bytes_accessed=4 * batch * contacts * slab,
            transcendentals=0,
        ),
        name="filter",
    )(place, signal, rim, table)


def pair_masks(pair):
    lane = lax.broadcasted_iota(jnp.int32, (1, pair), 1)
    return [(lane < pair // 2).astype(F32).astype(BF16), (lane >= pair // 2).astype(F32).astype(BF16)]


def head_masks(width):
    lane_head = lax.broadcasted_iota(jnp.int32, (1, width), 1) // (width // HEADS)
    return [(lane_head == h).astype(F32) for h in range(HEADS)]


def forward_kernel(
    blocks, place_ref, nbr_ref, live_ref, coef_ref, wq_ref, wk_ref, wv_ref, wo_ref, *refs
):
    feat_refs = refs[:blocks]
    (
        out_ref, prob_ref, value_ref, keys_ref, query_t_ref, normed_ref, normed_t_ref, mixed_ref,
        mixed_t_ref, inverse_ref, counts, columns, packed, live_row, turned_w,
    ) = refs[blocks:]
    rows, width = feat_refs[0].shape
    contacts = rows * blocks
    scale = (width // HEADS) ** (-0.5)
    slots = nbr_ref.shape[0]
    me = place_ref[1]

    @pl.when(pl.program_id(0) == 0)
    def _():
        packed[...] = jnp.zeros_like(packed)
        packed[0:1, :] = live_ref[...].astype(F32)
        packed[1:2, :] = coef_ref[...]
        for slot in range(slots):
            packed[2 + slot : 3 + slot, :] = nbr_ref[slot : slot + 1, :].astype(F32)
        columns[...] = packed[...].T
        turned = jnp.concatenate(
            [columns[pl.ds(pl.multiple_of((me ^ k) * rows, rows), rows), :] for k in range(blocks)],
            axis=0,
        )
        alive = turned.T[0:1]
        live_row[...] = alive
        ids = lax.broadcasted_iota(jnp.int32, (contacts, contacts), 1)
        total = jnp.zeros((contacts, contacts), F32)
        for slot in range(slots):
            here = turned[:, slot + 2 : slot + 3].astype(jnp.int32) ^ (me * rows)
            total = total + jnp.where(here == ids, alive, 0.0)
        counts[...] = total.astype(BF16)
        columns[:, 0:1] = turned[:, 0:1]
        columns[:, 1:2] = turned[:, 1:2]
        columns[:, 2:3] = jnp.sum(total, axis=1, keepdims=True)
        turned_w[0] = wq_ref[...].T
        turned_w[1] = wk_ref[...].T

    live = columns[:, 0:1]
    coef = columns[:, 1:2]
    field = jnp.concatenate([ref[...] for ref in feat_refs], axis=0)
    middle = field.astype(F32)
    beside = mm(counts[...], field)
    ready = live * (middle + coef * (beside - columns[:, 2:3] * middle))
    ready = ready.astype(BF16).astype(F32)
    mean_square = jnp.mean(ready * ready, axis=1, keepdims=True)
    normed = (ready * lax.rsqrt(mean_square + 1e-05)).astype(BF16)
    query = (mm(normed, wq_ref[...]) * scale).astype(BF16)
    keys = mm(normed, wk_ref[...]).astype(BF16)
    value = mm(normed, wv_ref[...]).astype(BF16)
    normed_t = normed.T
    keys_t = mm(turned_w[1], normed_t).astype(BF16)
    value_ref[...] = value
    keys_ref[...] = keys
    query_t_ref[...] = (mm(turned_w[0], normed_t) * scale).astype(BF16)
    normed_ref[...] = normed
    normed_t_ref[...] = normed_t
    pair = 2 * width // HEADS
    masks = pair_masks(pair)

    def score(h):
        lanes = slice(h // 2 * pair, (h // 2 + 1) * pair)
        return mm(query[:, lanes] * masks[h % 2], keys_t[lanes, :])

    bias = jnp.where(live_row[...] > 0, 0.0, -1e30)
    block = min(64, contacts)
    scores = score(0)
    products = []
    for h in range(HEADS):
        following = score(h + 1) if h + 1 < HEADS else None
        columns_h = slice(h * contacts, (h + 1) * contacts)
        for r in range(contacts // block):
            here = slice(r * block, (r + 1) * block)
            part = scores[here] + bias
            raised = jnp.exp(part - jnp.max(part, axis=1, keepdims=True))
            prob_ref[here, columns_h] = raised.astype(BF16)
        lanes = slice(h // 2 * pair, (h // 2 + 1) * pair)
        with_ones = value[:, lanes] * masks[h % 2] + masks[1 - h % 2]
        products.append(mm(prob_ref[:, columns_h], with_ones))
        scores = following
    low_lanes = lax.broadcasted_iota(jnp.int32, (contacts, pair), 1) < pair // 2
    mixed = []
    for p in range(HEADS // 2):
        even, odd = products[2 * p], products[2 * p + 1]
        inverse = 1.0 / pltpu.roll(jnp.where(low_lanes, odd, even), pair // 2, 1)
        inverse_ref[:, p * pair : (p + 1) * pair] = inverse
        mixed.append((jnp.where(low_lanes, even, odd) * inverse).astype(BF16))
    mixed = jnp.concatenate(mixed, axis=1)
    attended = mm(mixed, wo_ref[...]).astype(BF16)
    for k in range(blocks):
        out_ref[me ^ k] = attended[k * rows : (k + 1) * rows]
    mixed_ref[...] = mixed
    mixed_t_ref[...] = mixed.T


def backward_kernel(
    blocks, place_ref, wo_ref, up_ref, prob_ref, value_ref, keys_ref, query_t_ref, normed_ref,
    normed_t_ref, mixed_ref, mixed_t_ref, inverse_ref, *refs,
):
    out_refs, total, chunks, changes = refs[:-3], refs[-3], refs[-2], refs[-1]
    contacts, width = normed_ref.shape
    head = width // HEADS
    scale = head ** (-0.5)
    step = pl.program_id(0)

    @pl.when(step == 0)
    def _():
        total[...] = jnp.zeros_like(total)

    me = place_ref[1]
    upstream = jnp.concatenate([up_ref[me ^ k] for k in range(blocks)], axis=0)
    normed = normed_ref[...]
    value = value_ref[...]
    keys = keys_ref[...]
    back = mm(upstream, wo_ref[...], 1, 1).astype(BF16)
    back = (back.astype(F32) * inverse_ref[...]).astype(BF16)
    back_t = back.T
    inner = back.astype(F32) * mixed_ref[...].astype(F32)
    masks = head_masks(width)
    grad_value_t = []
    grad_key_t = []
    grad_query = None
    low = [m.astype(BF16) for m in masks]
    block = min(64, contacts)
    grad_prob = mm(back * low[0], value, 1, 1)
    for h in range(HEADS):
        following = mm(back * low[h + 1], value, 1, 1) if h + 1 < HEADS else None
        columns_h = slice(h * contacts, (h + 1) * contacts)
        grad_value_t.append(mm(back_t[h * head : (h + 1) * head], prob_ref[:, columns_h]))
        for r in range(contacts // block):
            here = slice(r * block, (r + 1) * block)
            row_inner = jnp.sum(inner[here] * masks[h], axis=1, keepdims=True)
            shift = (grad_prob[here] - row_inner).astype(BF16)
            changes[here, columns_h] = prob_ref[here, columns_h] * shift
        grad_score = changes[:, columns_h]
        grad_key_t.append(mm(query_t_ref[h * head : (h + 1) * head, :], grad_score))
        part = mm(grad_score, keys * low[h])
        grad_query = part if grad_query is None else grad_query + part
        grad_prob = following
    grad_query = (grad_query * scale).astype(BF16)
    total[0] += mm(normed_t_ref[...], grad_query)
    total[1] += mm(jnp.concatenate(grad_key_t, axis=0).astype(BF16), normed)
    total[2] += mm(jnp.concatenate(grad_value_t, axis=0).astype(BF16), normed)
    total[3] += mm(mixed_t_ref[...], upstream)

    @pl.when(step == pl.num_programs(0) - 1)
    def _():
        count, rows = chunks.shape[:2]
        parts = [total[0], total[1].T, total[2].T, total[3]]
        for c in range(count):
            first = (c * rows) % width
            chunks[c] = parts[c * rows // width][first : first + rows].astype(BF16)
        for k, out_ref in enumerate(out_refs):
            out_ref[...] = chunks[place_ref[0] ^ k]


def whole(shape):
    return pl.BlockSpec(shape, lambda i: (0,) * len(shape))


def forward(place, features, neighbours, live, coef, weights):
    blocks = len(features)
    rows, span = features[0].shape
    contacts = rows * blocks
    width = weights[0].shape[0]
    groups = span // width
    shapes = [
        (contacts, HEADS * contacts), (contacts, width),
        (contacts, width), (width, contacts), (contacts, width), (width, contacts),
        (contacts, width), (width, contacts), (contacts, width),
    ]
    small = [neighbours, live, coef] + list(weights)
    return pl.pallas_call(
        functools.partial(forward_kernel, blocks),
        grid=(groups,),
        in_specs=[index_spec()]
        + [whole(item.shape) for item in small]
        + [pl.BlockSpec((rows, width), lambda i: (0, i))] * blocks,
        out_specs=[pl.BlockSpec((blocks, rows, width), lambda i: (0, 0, i))]
        + [pl.BlockSpec(shape, lambda i: (0, i)) for shape in shapes],
        out_shape=[jax.ShapeDtypeStruct((blocks, rows, span), BF16)]
        + [
            jax.ShapeDtypeStruct((shape[0], groups * shape[1]), kind)
            for shape, kind in zip(shapes, [BF16] * (len(shapes) - 1) + [F32])
        ],
        scratch_shapes=[
            pltpu.VMEM((contacts, contacts), BF16),
            pltpu.VMEM((contacts, 128), F32),
            pltpu.VMEM((128, contacts), F32),
            pltpu.VMEM((1, contacts), F32),
            pltpu.VMEM((2, width, width), BF16),
        ],
        compiler_params=params(),
        cost_estimate=pl.CostEstimate(
            flops=groups * 5 * 10**9,
            bytes_accessed=20 * contacts * span,
            transcendentals=groups * HEADS * contacts * contacts,
        ),
        name="forward",
    )(place, *small, *features)


def backward(place, upstream, kept, w_out, tm_count):
    blocks, rows, span = upstream.shape
    contacts = rows * blocks
    width = w_out.shape[0]
    groups = span // width
    chunk = (4 * width // tm_count, width)
    return pl.pallas_call(
        functools.partial(backward_kernel, blocks),
        grid=(groups,),
        in_specs=[
            index_spec(), whole(w_out.shape),
            pl.BlockSpec((blocks, rows, width), lambda i: (0, 0, i)),
        ]
        + [
            pl.BlockSpec((item.shape[0], item.shape[1] // groups), lambda i: (0, i))
            for item in kept
        ],
        out_specs=[whole(chunk)] * tm_count,
        out_shape=[jax.ShapeDtypeStruct(chunk, BF16)] * tm_count,
        scratch_shapes=[
            pltpu.VMEM((4, width, width), F32),
            pltpu.VMEM((tm_count,) + chunk, BF16),
            pltpu.VMEM((contacts, HEADS * contacts), BF16),
        ],
        compiler_params=params(),
        cost_estimate=pl.CostEstimate(
            flops=groups * 5 * 10**9, bytes_accessed=20 * contacts * span, transcendentals=0
        ),
        name="backward",
    )(place, w_out, upstream, *kept)


def place_all(place, parts):
    rows, width = parts[0].shape
    ways = len(parts)

    def body(place_ref, *refs):
        for k in range(ways):
            refs[-1][place_ref[0] ^ k] = refs[k][...].astype(F32)

    shape = (ways, rows, width)
    return pl.pallas_call(
        body,
        in_specs=[index_spec()] + [pl.BlockSpec((rows, width), lambda: (0, 0))] * ways,
        out_specs=pl.BlockSpec(shape, lambda: (0, 0, 0)),
        out_shape=jax.ShapeDtypeStruct(shape, F32),
        compiler_params=params(),
        name="place_all",
    )(place, *parts)


def write_out(value):
    def body(in_ref, out_ref):
        out_ref[...] = in_ref[...]

    spec = pl.BlockSpec((value.shape[0] // 2,) + value.shape[1:], lambda i: (i, 0, 0))
    return pl.pallas_call(
        body,
        grid=(2,),
        in_specs=[spec],
        out_specs=spec,
        out_shape=jax.ShapeDtypeStruct(value.shape, value.dtype),
        compiler_params=params(),
        cost_estimate=pl.CostEstimate(flops=0, bytes_accessed=4 * value.size, transcendentals=0),
        name="write_out",
    )(value)


def swap(value, axis, k):
    return lax.ppermute(value, axis, [(i, i ^ k) for i in range(lax.axis_size(axis))])


def swap_all(parts, axis):
    moved = [swap(parts[k], axis, k) for k in range(len(parts) - 1, 0, -1)]
    return [parts[0]] + moved[::-1]


def exchange(value, axis):
    return lax.all_to_all(value, axis, split_axis=0, concat_axis=0, tiled=True)


def local(
    signal, fir_taps, neighbours, live_mask, lap_coef, w_query, w_key, w_value, w_out, cotangent
):
    batch, contacts_here, slab = signal.shape
    rim_width = fir_taps.shape[1] - 1
    width = w_query.shape[0]
    tm_count = lax.axis_size("tm")
    count = lax.axis_size("contact")
    pieces = count // batch
    span = slab // pieces
    place = jnp.stack([lax.axis_index("tm"), lax.axis_index("contact")]).astype(jnp.int32)

    if pieces > 1:
        cotangent = cotangent.reshape(batch, contacts_here, pieces, span)
        cotangent = cotangent.transpose(0, 2, 1, 3).reshape(count, contacts_here, span)
    rim = lax.ppermute(
        signal[:, :, slab - rim_width :], "tm", [(i, i + 1) for i in range(tm_count - 1)]
    )
    filtered = filter_all(place, signal, rim, tables(fir_taps), count)
    features = swap_all(filtered, "contact")
    arrived = count - max(2, count // 4)
    features[arrived:], cotangent = lax.optimization_barrier((features[arrived:], cotangent))
    upstream = exchange(cotangent, "contact")
    attended, *kept = forward(
        place, features, neighbours.T, live_mask[None], lap_coef[None],
        [w_query, w_key, w_value, w_out],
    )
    returned = exchange(attended, "contact")
    grads = backward(place, upstream, kept, w_out, tm_count)
    grads = swap_all(grads, "tm")
    part = sum(piece.astype(F32) for piece in grads).astype(BF16)
    part, returned = lax.optimization_barrier((part, returned))
    returned = write_out(returned)
    grad_scale = (batch * (slab // width) * tm_count * neighbours.shape[0]) ** (-0.5)
    step = 1
    while step < count:
        both = part.astype(F32) + swap(part, "contact", step).astype(F32)
        step *= 2
        part = lax.optimization_barrier((both * (1.0 if step < count else grad_scale)).astype(BF16))
    summed = place_all(place, swap_all([part] * tm_count, "tm"))
    if pieces > 1:
        returned = returned.reshape(batch, pieces, contacts_here, span)
        returned = returned.transpose(0, 2, 1, 3).reshape(batch, contacts_here, slab)
    return (returned, summed.reshape(4, width, width))


def solution(mesh):
    in_specs = (
        P(None, "contact", "tm"),
        P("contact", None),
        P(),
        P(),
        P(),
        P(),
        P(),
        P(),
        P(),
        P(None, "contact", "tm"),
    )
    out_specs = (P(None, "contact", "tm"), P())
    return jax.shard_map(local, mesh=mesh, in_specs=in_specs, out_specs=out_specs, check_vma=False)
```

```python
import functools

import jax
import jax.numpy as jnp
from jax import lax
from jax.experimental import pallas as pl
from jax.experimental.pallas import tpu as pltpu
from jax.sharding import PartitionSpec as P

HEADS = 4
F32 = jnp.float32
BF16 = jnp.bfloat16


def mm(left, right, left_dim=1, right_dim=0):
    return lax.dot_general(
        left, right, (((left_dim,), (right_dim,)), ((), ())), preferred_element_type=F32
    )


def index_spec():
    return pl.BlockSpec(memory_space=pltpu.SMEM)


def params():
    return pltpu.CompilerParams(vmem_limit_bytes=56 * 2**20)


def filter_kernel(place_ref, sig_ref, rim_ref, taps_ref, *refs):
    out_refs, kept = refs[:-1], refs[-1]
    batch, rows, slab = sig_ref.shape
    width = rim_ref.shape[2]
    blocks = slab // width
    pieces = len(out_refs) // batch
    span = slab // pieces
    signal = jnp.swapaxes(sig_ref[...].astype(F32), 0, 1)
    rim = jnp.swapaxes(rim_ref[...].astype(F32), 0, 1)
    taps = taps_ref[...].astype(F32)
    first = lax.broadcasted_iota(jnp.int32, (rows, width), 1) == 0
    taps = jnp.concatenate(
        [taps[:, :width], jnp.where(first, taps[:, width : width + 1], 0.0)], axis=1
    )
    results = []
    for row in range(rows):
        own = [signal[row, :, j * width : (j + 1) * width] for j in range(blocks)]
        current = jnp.concatenate(own, axis=0)
        before = jnp.concatenate([rim[row]] + own[:-1], axis=0)
        window = jnp.concatenate([before, current], axis=1).astype(BF16)
        spread = jnp.broadcast_to(taps[row : row + 1, :], (width, 2 * width))
        rolled = pltpu.roll(spread, 0, 1, stride=1, stride_axis=0)
        table = jnp.concatenate([rolled[:, width:], rolled[:, :width]], axis=0).astype(BF16)
        product = mm(window, table)
        results.append(
            jnp.concatenate(
                [product[j * batch : (j + 1) * batch] for j in range(blocks)], axis=1
            )
        )
    filtered = jnp.swapaxes(jnp.stack(results, axis=0), 0, 1).astype(BF16)
    for index in range(batch):
        for piece in range(pieces):
            kept[index * pieces + piece] = filtered[index, :, piece * span : (piece + 1) * span]
    me = place_ref[1]
    for k, out_ref in enumerate(out_refs):
        out_ref[...] = kept[me ^ k]


def filter_all(place, signal, rim, taps, count):
    batch, contacts, slab = signal.shape
    width = rim.shape[2]
    rows = 16
    span = slab * batch // count
    return pl.pallas_call(
        filter_kernel,
        grid=(contacts // rows,),
        in_specs=[
            index_spec(),
            pl.BlockSpec((batch, rows, slab), lambda i: (0, i, 0)),
            pl.BlockSpec((batch, rows, width), lambda i: (0, i, 0)),
            pl.BlockSpec((rows, taps.shape[1]), lambda i: (i, 0)),
        ],
        out_specs=[pl.BlockSpec((rows, span), lambda i: (i, 0))] * count,
        out_shape=[jax.ShapeDtypeStruct((contacts, span), BF16)] * count,
        scratch_shapes=[pltpu.VMEM((count, rows, span), BF16)],
        compiler_params=params(),
        cost_estimate=pl.CostEstimate(
            flops=4 * batch * contacts * slab * width,
            bytes_accessed=4 * batch * contacts * slab,
            transcendentals=0,
        ),
        name="filter",
    )(place, signal, rim, taps)


def pair_masks(pair):
    lane = lax.broadcasted_iota(jnp.int32, (1, pair), 1)
    return [(lane < pair // 2).astype(F32).astype(BF16), (lane >= pair // 2).astype(F32).astype(BF16)]


def head_masks(width):
    lane_head = lax.broadcasted_iota(jnp.int32, (1, width), 1) // (width // HEADS)
    return [(lane_head == h).astype(F32) for h in range(HEADS)]


def forward_kernel(
    blocks, place_ref, nbr_ref, live_ref, coef_ref, wq_ref, wk_ref, wv_ref, wo_ref, *refs
):
    feat_refs = refs[:blocks]
    (
        out_ref, prob_ref, value_ref, keys_ref, query_t_ref, normed_ref, normed_t_ref, mixed_ref,
        mixed_t_ref, inverse_ref, counts, columns, packed, live_row, turned_w,
    ) = refs[blocks:]
    rows, width = feat_refs[0].shape
    contacts = rows * blocks
    scale = (width // HEADS) ** (-0.5)
    slots = nbr_ref.shape[0]
    me = place_ref[1]

    @pl.when(pl.program_id(0) == 0)
    def _():
        packed[...] = jnp.zeros_like(packed)
        packed[0:1, :] = live_ref[...].astype(F32)
        packed[1:2, :] = coef_ref[...]
        for slot in range(slots):
            packed[2 + slot : 3 + slot, :] = nbr_ref[slot : slot + 1, :].astype(F32)
        columns[...] = packed[...].T
        turned = jnp.concatenate(
            [columns[pl.ds(pl.multiple_of((me ^ k) * rows, rows), rows), :] for k in range(blocks)],
            axis=0,
        )
        alive = turned.T[0:1]
        live_row[...] = alive
        ids = lax.broadcasted_iota(jnp.int32, (contacts, contacts), 1)
        total = jnp.zeros((contacts, contacts), F32)
        for slot in range(slots):
            here = turned[:, slot + 2 : slot + 3].astype(jnp.int32) ^ (me * rows)
            total = total + jnp.where(here == ids, alive, 0.0)
        counts[...] = total.astype(BF16)
        columns[:, 0:1] = turned[:, 0:1]
        columns[:, 1:2] = turned[:, 1:2]
        columns[:, 2:3] = jnp.sum(total, axis=1, keepdims=True)
        turned_w[0] = wq_ref[...].T
        turned_w[1] = wk_ref[...].T

    live = columns[:, 0:1]
    coef = columns[:, 1:2]
    field = jnp.concatenate([ref[...] for ref in feat_refs], axis=0)
    middle = field.astype(F32)
    beside = mm(counts[...], field)
    ready = live * (middle + coef * (beside - columns[:, 2:3] * middle))
    ready = ready.astype(BF16).astype(F32)
    mean_square = jnp.mean(ready * ready, axis=1, keepdims=True)
    normed = (ready * lax.rsqrt(mean_square + 1e-05)).astype(BF16)
    query = (mm(normed, wq_ref[...]) * scale).astype(BF16)
    keys = mm(normed, wk_ref[...]).astype(BF16)
    value = mm(normed, wv_ref[...]).astype(BF16)
    normed_t = normed.T
    keys_t = mm(turned_w[1], normed_t).astype(BF16)
    value_ref[...] = value
    keys_ref[...] = keys
    query_t_ref[...] = (mm(turned_w[0], normed_t) * scale).astype(BF16)
    normed_ref[...] = normed
    normed_t_ref[...] = normed_t
    pair = 2 * width // HEADS
    masks = pair_masks(pair)

    def score(h):
        lanes = slice(h // 2 * pair, (h // 2 + 1) * pair)
        return mm(query[:, lanes] * masks[h % 2], keys_t[lanes, :])

    bias = jnp.where(live_row[...] > 0, 0.0, -1e30)
    block = min(64, contacts)
    scores = score(0)
    products = []
    for h in range(HEADS):
        following = score(h + 1) if h + 1 < HEADS else None
        columns_h = slice(h * contacts, (h + 1) * contacts)
        for r in range(contacts // block):
            here = slice(r * block, (r + 1) * block)
            part = scores[here] + bias
            raised = jnp.exp(part - jnp.max(part, axis=1, keepdims=True))
            prob_ref[here, columns_h] = raised.astype(BF16)
        lanes = slice(h // 2 * pair, (h // 2 + 1) * pair)
        with_ones = value[:, lanes] * masks[h % 2] + masks[1 - h % 2]
        products.append(mm(prob_ref[:, columns_h], with_ones))
        scores = following
    low_lanes = lax.broadcasted_iota(jnp.int32, (contacts, pair), 1) < pair // 2
    mixed = []
    for p in range(HEADS // 2):
        even, odd = products[2 * p], products[2 * p + 1]
        inverse = 1.0 / pltpu.roll(jnp.where(low_lanes, odd, even), pair // 2, 1)
        inverse_ref[:, p * pair : (p + 1) * pair] = inverse
        mixed.append((jnp.where(low_lanes, even, odd) * inverse).astype(BF16))
    mixed = jnp.concatenate(mixed, axis=1)
    attended = mm(mixed, wo_ref[...]).astype(BF16)
    for k in range(blocks):
        out_ref[me ^ k] = attended[k * rows : (k + 1) * rows]
    mixed_ref[...] = mixed
    mixed_t_ref[...] = mixed.T


def backward_kernel(
    blocks, place_ref, wo_ref, up_ref, prob_ref, value_ref, keys_ref, query_t_ref, normed_ref,
    normed_t_ref, mixed_ref, mixed_t_ref, inverse_ref, *refs,
):
    out_refs, total, chunks, changes = refs[:-3], refs[-3], refs[-2], refs[-1]
    contacts, width = normed_ref.shape
    head = width // HEADS
    scale = head ** (-0.5)
    step = pl.program_id(0)

    @pl.when(step == 0)
    def _():
        total[...] = jnp.zeros_like(total)

    me = place_ref[1]
    upstream = jnp.concatenate([up_ref[me ^ k] for k in range(blocks)], axis=0)
    normed = normed_ref[...]
    value = value_ref[...]
    keys = keys_ref[...]
    back = mm(upstream, wo_ref[...], 1, 1).astype(BF16)
    back = (back.astype(F32) * inverse_ref[...]).astype(BF16)
    back_t = back.T
    inner = back.astype(F32) * mixed_ref[...].astype(F32)
    masks = head_masks(width)
    grad_value_t = []
    grad_key_t = []
    grad_query = None
    low = [m.astype(BF16) for m in masks]
    block = min(64, contacts)
    grad_prob = mm(back * low[0], value, 1, 1)
    for h in range(HEADS):
        following = mm(back * low[h + 1], value, 1, 1) if h + 1 < HEADS else None
        columns_h = slice(h * contacts, (h + 1) * contacts)
        grad_value_t.append(mm(back_t[h * head : (h + 1) * head], prob_ref[:, columns_h]))
        for r in range(contacts // block):
            here = slice(r * block, (r + 1) * block)
            row_inner = jnp.sum(inner[here] * masks[h], axis=1, keepdims=True)
            shift = (grad_prob[here] - row_inner).astype(BF16)
            changes[here, columns_h] = prob_ref[here, columns_h] * shift
        grad_score = changes[:, columns_h]
        grad_key_t.append(mm(query_t_ref[h * head : (h + 1) * head, :], grad_score))
        part = mm(grad_score, keys * low[h])
        grad_query = part if grad_query is None else grad_query + part
        grad_prob = following
    grad_query = (grad_query * scale).astype(BF16)
    total[0] += mm(normed_t_ref[...], grad_query)
    total[1] += mm(jnp.concatenate(grad_key_t, axis=0).astype(BF16), normed)
    total[2] += mm(jnp.concatenate(grad_value_t, axis=0).astype(BF16), normed)
    total[3] += mm(mixed_t_ref[...], upstream)

    @pl.when(step == pl.num_programs(0) - 1)
    def _():
        count, rows = chunks.shape[:2]
        parts = [total[0], total[1].T, total[2].T, total[3]]
        for c in range(count):
            first = (c * rows) % width
            chunks[c] = parts[c * rows // width][first : first + rows].astype(BF16)
        for k, out_ref in enumerate(out_refs):
            out_ref[...] = chunks[place_ref[0] ^ k]


def whole(shape):
    return pl.BlockSpec(shape, lambda i: (0,) * len(shape))


def forward(place, features, neighbours, live, coef, weights):
    blocks = len(features)
    rows, span = features[0].shape
    contacts = rows * blocks
    width = weights[0].shape[0]
    groups = span // width
    shapes = [
        (contacts, HEADS * contacts), (contacts, width),
        (contacts, width), (width, contacts), (contacts, width), (width, contacts),
        (contacts, width), (width, contacts), (contacts, width),
    ]
    small = [neighbours, live, coef] + list(weights)
    return pl.pallas_call(
        functools.partial(forward_kernel, blocks),
        grid=(groups,),
        in_specs=[index_spec()]
        + [whole(item.shape) for item in small]
        + [pl.BlockSpec((rows, width), lambda i: (0, i))] * blocks,
        out_specs=[pl.BlockSpec((blocks, rows, width), lambda i: (0, 0, i))]
        + [pl.BlockSpec(shape, lambda i: (0, i)) for shape in shapes],
        out_shape=[jax.ShapeDtypeStruct((blocks, rows, span), BF16)]
        + [
            jax.ShapeDtypeStruct((shape[0], groups * shape[1]), kind)
            for shape, kind in zip(shapes, [BF16] * (len(shapes) - 1) + [F32])
        ],
        scratch_shapes=[
            pltpu.VMEM((contacts, contacts), BF16),
            pltpu.VMEM((contacts, 128), F32),
            pltpu.VMEM((128, contacts), F32),
            pltpu.VMEM((1, contacts), F32),
            pltpu.VMEM((2, width, width), BF16),
        ],
        compiler_params=params(),
        cost_estimate=pl.CostEstimate(
            flops=groups * 5 * 10**9,
            bytes_accessed=20 * contacts * span,
            transcendentals=groups * HEADS * contacts * contacts,
        ),
        name="forward",
    )(place, *small, *features)


def backward(place, upstream, kept, w_out, tm_count):
    blocks, rows, span = upstream.shape
    contacts = rows * blocks
    width = w_out.shape[0]
    groups = span // width
    chunk = (4 * width // tm_count, width)
    return pl.pallas_call(
        functools.partial(backward_kernel, blocks),
        grid=(groups,),
        in_specs=[
            index_spec(), whole(w_out.shape),
            pl.BlockSpec((blocks, rows, width), lambda i: (0, 0, i)),
        ]
        + [
            pl.BlockSpec((item.shape[0], item.shape[1] // groups), lambda i: (0, i))
            for item in kept
        ],
        out_specs=[whole(chunk)] * tm_count,
        out_shape=[jax.ShapeDtypeStruct(chunk, BF16)] * tm_count,
        scratch_shapes=[
            pltpu.VMEM((4, width, width), F32),
            pltpu.VMEM((tm_count,) + chunk, BF16),
            pltpu.VMEM((contacts, HEADS * contacts), BF16),
        ],
        compiler_params=params(),
        cost_estimate=pl.CostEstimate(
            flops=groups * 5 * 10**9, bytes_accessed=20 * contacts * span, transcendentals=0
        ),
        name="backward",
    )(place, w_out, upstream, *kept)


def place_all(place, parts):
    rows, width = parts[0].shape
    ways = len(parts)

    def body(place_ref, *refs):
        for k in range(ways):
            refs[-1][place_ref[0] ^ k] = refs[k][...].astype(F32)

    shape = (ways, rows, width)
    return pl.pallas_call(
        body,
        in_specs=[index_spec()] + [pl.BlockSpec((rows, width), lambda: (0, 0))] * ways,
        out_specs=pl.BlockSpec(shape, lambda: (0, 0, 0)),
        out_shape=jax.ShapeDtypeStruct(shape, F32),
        compiler_params=params(),
        name="place_all",
    )(place, *parts)


def write_out(value):
    def body(in_ref, out_ref):
        out_ref[...] = in_ref[...]

    spec = pl.BlockSpec((value.shape[0] // 2,) + value.shape[1:], lambda i: (i, 0, 0))
    return pl.pallas_call(
        body,
        grid=(2,),
        in_specs=[spec],
        out_specs=spec,
        out_shape=jax.ShapeDtypeStruct(value.shape, value.dtype),
        compiler_params=params(),
        cost_estimate=pl.CostEstimate(flops=0, bytes_accessed=4 * value.size, transcendentals=0),
        name="write_out",
    )(value)


def swap(value, axis, k):
    return lax.ppermute(value, axis, [(i, i ^ k) for i in range(lax.axis_size(axis))])


def swap_all(parts, axis):
    moved = [swap(parts[k], axis, k) for k in range(len(parts) - 1, 0, -1)]
    return [parts[0]] + moved[::-1]


def exchange(value, axis):
    return lax.all_to_all(value, axis, split_axis=0, concat_axis=0, tiled=True)


def local(
    signal, fir_taps, neighbours, live_mask, lap_coef, w_query, w_key, w_value, w_out, cotangent
):
    batch, contacts_here, slab = signal.shape
    rim_width = fir_taps.shape[1] - 1
    width = w_query.shape[0]
    tm_count = lax.axis_size("tm")
    count = lax.axis_size("contact")
    pieces = count // batch
    span = slab // pieces
    place = jnp.stack([lax.axis_index("tm"), lax.axis_index("contact")]).astype(jnp.int32)

    if pieces > 1:
        cotangent = cotangent.reshape(batch, contacts_here, pieces, span)
        cotangent = cotangent.transpose(0, 2, 1, 3).reshape(count, contacts_here, span)
    rim = lax.ppermute(
        signal[:, :, slab - rim_width :], "tm", [(i, i + 1) for i in range(tm_count - 1)]
    )
    filtered = filter_all(place, signal, rim, fir_taps, count)
    features = swap_all(filtered, "contact")
    arrived = count - max(2, count // 4)
    features[arrived:], cotangent = lax.optimization_barrier((features[arrived:], cotangent))
    upstream = exchange(cotangent, "contact")
    attended, *kept = forward(
        place, features, neighbours.T, live_mask[None], lap_coef[None],
        [w_query, w_key, w_value, w_out],
    )
    returned = exchange(attended, "contact")
    grads = backward(place, upstream, kept, w_out, tm_count)
    grads = swap_all(grads, "tm")
    part = sum(piece.astype(F32) for piece in grads).astype(BF16)
    part, returned = lax.optimization_barrier((part, returned))
    returned = write_out(returned)
    grad_scale = (batch * (slab // width) * tm_count * neighbours.shape[0]) ** (-0.5)
    step = 1
    while step < count:
        both = part.astype(F32) + swap(part, "contact", step).astype(F32)
        step *= 2
        part = lax.optimization_barrier((both * (1.0 if step < count else grad_scale)).astype(BF16))
    summed = place_all(place, swap_all([part] * tm_count, "tm"))
    if pieces > 1:
        returned = returned.reshape(batch, pieces, contacts_here, span)
        returned = returned.transpose(0, 2, 1, 3).reshape(batch, contacts_here, slab)
    return (returned, summed.reshape(4, width, width))


def solution(mesh):
    in_specs = (
        P(None, "contact", "tm"),
        P("contact", None),
        P(),
        P(),
        P(),
        P(),
        P(),
        P(),
        P(),
        P(None, "contact", "tm"),
    )
    out_specs = (P(None, "contact", "tm"), P())
    return jax.shard_map(local, mesh=mesh, in_specs=in_specs, out_specs=out_specs, check_vma=False)
```

```python
import functools

import jax
import jax.numpy as jnp
from jax import lax
from jax.experimental import pallas as pl
from jax.experimental.pallas import tpu as pltpu
from jax.sharding import PartitionSpec as P

HEADS = 4
F32 = jnp.float32
BF16 = jnp.bfloat16


def mm(left, right, left_dim=1, right_dim=0):
    return lax.dot_general(
        left, right, (((left_dim,), (right_dim,)), ((), ())), preferred_element_type=F32
    )


def index_spec():
    return pl.BlockSpec(memory_space=pltpu.SMEM)


def params():
    return pltpu.CompilerParams(vmem_limit_bytes=56 * 2**20)


def filter_kernel(place_ref, sig_ref, rim_ref, taps_ref, *refs):
    out_refs, kept = refs[:-1], refs[-1]
    batch, rows, slab = sig_ref.shape
    width = rim_ref.shape[2]
    blocks = slab // width
    pieces = len(out_refs) // batch
    span = slab // pieces
    signal = jnp.swapaxes(sig_ref[...].astype(F32), 0, 1)
    rim = jnp.swapaxes(rim_ref[...].astype(F32), 0, 1)
    taps = taps_ref[...].astype(F32)
    first = lax.broadcasted_iota(jnp.int32, (rows, width), 1) == 0
    taps = jnp.concatenate(
        [taps[:, :width], jnp.where(first, taps[:, width : width + 1], 0.0)], axis=1
    )
    results = []
    for row in range(rows):
        own = [signal[row, :, j * width : (j + 1) * width] for j in range(blocks)]
        current = jnp.concatenate(own, axis=0)
        before = jnp.concatenate([rim[row]] + own[:-1], axis=0)
        window = jnp.concatenate([before, current], axis=1).astype(BF16)
        spread = jnp.broadcast_to(taps[row : row + 1, :], (width, 2 * width))
        rolled = pltpu.roll(spread, 0, 1, stride=1, stride_axis=0)
        table = jnp.concatenate([rolled[:, width:], rolled[:, :width]], axis=0).astype(BF16)
        product = mm(window, table)
        results.append(
            jnp.concatenate(
                [product[j * batch : (j + 1) * batch] for j in range(blocks)], axis=1
            )
        )
    filtered = jnp.swapaxes(jnp.stack(results, axis=0), 0, 1).astype(BF16)
    for index in range(batch):
        for piece in range(pieces):
            kept[index * pieces + piece] = filtered[index, :, piece * span : (piece + 1) * span]
    me = place_ref[1]
    for k, out_ref in enumerate(out_refs):
        out_ref[...] = kept[me ^ k]


def filter_all(place, signal, rim, taps, count):
    batch, contacts, slab = signal.shape
    width = rim.shape[2]
    rows = min(32, contacts)
    span = slab * batch // count
    return pl.pallas_call(
        filter_kernel,
        grid=(contacts // rows,),
        in_specs=[
            index_spec(),
            pl.BlockSpec((batch, rows, slab), lambda i: (0, i, 0)),
            pl.BlockSpec((batch, rows, width), lambda i: (0, i, 0)),
            pl.BlockSpec((rows, taps.shape[1]), lambda i: (i, 0)),
        ],
        out_specs=[pl.BlockSpec((rows, span), lambda i: (i, 0))] * count,
        out_shape=[jax.ShapeDtypeStruct((contacts, span), BF16)] * count,
        scratch_shapes=[pltpu.VMEM((count, rows, span), BF16)],
        compiler_params=params(),
        cost_estimate=pl.CostEstimate(
            flops=4 * batch * contacts * slab * width,
            bytes_accessed=4 * batch * contacts * slab,
            transcendentals=0,
        ),
        name="filter",
    )(place, signal, rim, taps)


def pair_masks(pair):
    lane = lax.broadcasted_iota(jnp.int32, (1, pair), 1)
    return [(lane < pair // 2).astype(F32).astype(BF16), (lane >= pair // 2).astype(F32).astype(BF16)]


def head_masks(width):
    lane_head = lax.broadcasted_iota(jnp.int32, (1, width), 1) // (width // HEADS)
    return [(lane_head == h).astype(F32) for h in range(HEADS)]


def forward_kernel(
    blocks, place_ref, nbr_ref, live_ref, coef_ref, wq_ref, wk_ref, wv_ref, wo_ref, *refs
):
    feat_refs = refs[:blocks]
    (
        out_ref, prob_ref, value_ref, keys_ref, query_t_ref, normed_ref, normed_t_ref, mixed_ref,
        mixed_t_ref, inverse_ref, counts, columns, packed, live_row, turned_w,
    ) = refs[blocks:]
    rows, width = feat_refs[0].shape
    contacts = rows * blocks
    scale = (width // HEADS) ** (-0.5)
    slots = nbr_ref.shape[0]
    me = place_ref[1]

    @pl.when(pl.program_id(0) == 0)
    def _():
        packed[...] = jnp.zeros_like(packed)
        packed[0:1, :] = live_ref[...].astype(F32)
        packed[1:2, :] = coef_ref[...]
        for slot in range(slots):
            packed[2 + slot : 3 + slot, :] = nbr_ref[slot : slot + 1, :].astype(F32)
        columns[...] = packed[...].T
        turned = jnp.concatenate(
            [columns[pl.ds(pl.multiple_of((me ^ k) * rows, rows), rows), :] for k in range(blocks)],
            axis=0,
        )
        alive = turned.T[0:1]
        live_row[...] = alive
        ids = lax.broadcasted_iota(jnp.int32, (contacts, contacts), 1)
        total = jnp.zeros((contacts, contacts), F32)
        for slot in range(slots):
            here = turned[:, slot + 2 : slot + 3].astype(jnp.int32) ^ (me * rows)
            total = total + jnp.where(here == ids, alive, 0.0)
        counts[...] = total.astype(BF16)
        columns[:, 0:1] = turned[:, 0:1]
        columns[:, 1:2] = turned[:, 1:2]
        columns[:, 2:3] = jnp.sum(total, axis=1, keepdims=True)
        turned_w[0] = wq_ref[...].T
        turned_w[1] = wk_ref[...].T

    live = columns[:, 0:1]
    coef = columns[:, 1:2]
    field = jnp.concatenate([ref[...] for ref in feat_refs], axis=0)
    middle = field.astype(F32)
    beside = mm(counts[...], field)
    ready = live * (middle + coef * (beside - columns[:, 2:3] * middle))
    ready = ready.astype(BF16).astype(F32)
    mean_square = jnp.mean(ready * ready, axis=1, keepdims=True)
    normed = (ready * lax.rsqrt(mean_square + 1e-05)).astype(BF16)
    query = (mm(normed, wq_ref[...]) * scale).astype(BF16)
    keys = mm(normed, wk_ref[...]).astype(BF16)
    value = mm(normed, wv_ref[...]).astype(BF16)
    normed_t = normed.T
    keys_t = mm(turned_w[1], normed_t).astype(BF16)
    value_ref[...] = value
    keys_ref[...] = keys
    query_t_ref[...] = (mm(turned_w[0], normed_t) * scale).astype(BF16)
    normed_ref[...] = normed
    normed_t_ref[...] = normed_t
    pair = 2 * width // HEADS
    masks = pair_masks(pair)

    def score(h):
        lanes = slice(h // 2 * pair, (h // 2 + 1) * pair)
        return mm(query[:, lanes] * masks[h % 2], keys_t[lanes, :])

    bias = jnp.where(live_row[...] > 0, 0.0, -1e30)
    block = min(64, contacts)
    scores = score(0)
    products = []
    for h in range(HEADS):
        following = score(h + 1) if h + 1 < HEADS else None
        columns_h = slice(h * contacts, (h + 1) * contacts)
        for r in range(contacts // block):
            here = slice(r * block, (r + 1) * block)
            part = scores[here] + bias
            raised = jnp.exp(part - jnp.max(part, axis=1, keepdims=True))
            prob_ref[here, columns_h] = raised.astype(BF16)
        lanes = slice(h // 2 * pair, (h // 2 + 1) * pair)
        with_ones = value[:, lanes] * masks[h % 2] + masks[1 - h % 2]
        products.append(mm(prob_ref[:, columns_h], with_ones))
        scores = following
    low_lanes = lax.broadcasted_iota(jnp.int32, (contacts, pair), 1) < pair // 2
    mixed = []
    for p in range(HEADS // 2):
        even, odd = products[2 * p], products[2 * p + 1]
        inverse = 1.0 / pltpu.roll(jnp.where(low_lanes, odd, even), pair // 2, 1)
        inverse_ref[:, p * pair : (p + 1) * pair] = inverse
        mixed.append((jnp.where(low_lanes, even, odd) * inverse).astype(BF16))
    mixed = jnp.concatenate(mixed, axis=1)
    attended = mm(mixed, wo_ref[...]).astype(BF16)
    for k in range(blocks):
        out_ref[me ^ k] = attended[k * rows : (k + 1) * rows]
    mixed_ref[...] = mixed
    mixed_t_ref[...] = mixed.T


def backward_kernel(
    blocks, place_ref, wo_ref, up_ref, prob_ref, value_ref, keys_ref, query_t_ref, normed_ref,
    normed_t_ref, mixed_ref, mixed_t_ref, inverse_ref, *refs,
):
    out_refs, total, chunks, changes = refs[:-3], refs[-3], refs[-2], refs[-1]
    contacts, width = normed_ref.shape
    head = width // HEADS
    scale = head ** (-0.5)
    step = pl.program_id(0)

    @pl.when(step == 0)
    def _():
        total[...] = jnp.zeros_like(total)

    me = place_ref[1]
    upstream = jnp.concatenate([up_ref[me ^ k] for k in range(blocks)], axis=0)
    normed = normed_ref[...]
    value = value_ref[...]
    keys = keys_ref[...]
    back = mm(upstream, wo_ref[...], 1, 1).astype(BF16)
    back = (back.astype(F32) * inverse_ref[...]).astype(BF16)
    back_t = back.T
    inner = back.astype(F32) * mixed_ref[...].astype(F32)
    masks = head_masks(width)
    grad_value_t = []
    grad_key_t = []
    grad_query = None
    low = [m.astype(BF16) for m in masks]
    block = min(64, contacts)
    grad_prob = mm(back * low[0], value, 1, 1)
    for h in range(HEADS):
        following = mm(back * low[h + 1], value, 1, 1) if h + 1 < HEADS else None
        columns_h = slice(h * contacts, (h + 1) * contacts)
        grad_value_t.append(mm(back_t[h * head : (h + 1) * head], prob_ref[:, columns_h]))
        for r in range(contacts // block):
            here = slice(r * block, (r + 1) * block)
            row_inner = jnp.sum(inner[here] * masks[h], axis=1, keepdims=True)
            shift = (grad_prob[here] - row_inner).astype(BF16)
            changes[here, columns_h] = prob_ref[here, columns_h] * shift
        grad_score = changes[:, columns_h]
        grad_key_t.append(mm(query_t_ref[h * head : (h + 1) * head, :], grad_score))
        part = mm(grad_score, keys * low[h])
        grad_query = part if grad_query is None else grad_query + part
        grad_prob = following
    grad_query = (grad_query * scale).astype(BF16)
    total[0] += mm(normed_t_ref[...], grad_query)
    total[1] += mm(jnp.concatenate(grad_key_t, axis=0).astype(BF16), normed)
    total[2] += mm(jnp.concatenate(grad_value_t, axis=0).astype(BF16), normed)
    total[3] += mm(mixed_t_ref[...], upstream)

    @pl.when(step == pl.num_programs(0) - 1)
    def _():
        count, rows = chunks.shape[:2]
        parts = [total[0], total[1].T, total[2].T, total[3]]
        for c in range(count):
            first = (c * rows) % width
            chunks[c] = parts[c * rows // width][first : first + rows].astype(BF16)
        for k, out_ref in enumerate(out_refs):
            out_ref[...] = chunks[place_ref[0] ^ k]


def whole(shape):
    return pl.BlockSpec(shape, lambda i: (0,) * len(shape))


def forward(place, features, neighbours, live, coef, weights):
    blocks = len(features)
    rows, span = features[0].shape
    contacts = rows * blocks
    width = weights[0].shape[0]
    groups = span // width
    shapes = [
        (contacts, HEADS * contacts), (contacts, width),
        (contacts, width), (width, contacts), (contacts, width), (width, contacts),
        (contacts, width), (width, contacts), (contacts, width),
    ]
    small = [neighbours, live, coef] + list(weights)
    return pl.pallas_call(
        functools.partial(forward_kernel, blocks),
        grid=(groups,),
        in_specs=[index_spec()]
        + [whole(item.shape) for item in small]
        + [pl.BlockSpec((rows, width), lambda i: (0, i))] * blocks,
        out_specs=[pl.BlockSpec((blocks, rows, width), lambda i: (0, 0, i))]
        + [pl.BlockSpec(shape, lambda i: (0, i)) for shape in shapes],
        out_shape=[jax.ShapeDtypeStruct((blocks, rows, span), BF16)]
        + [
            jax.ShapeDtypeStruct((shape[0], groups * shape[1]), kind)
            for shape, kind in zip(shapes, [BF16] * (len(shapes) - 1) + [F32])
        ],
        scratch_shapes=[
            pltpu.VMEM((contacts, contacts), BF16),
            pltpu.VMEM((contacts, 128), F32),
            pltpu.VMEM((128, contacts), F32),
            pltpu.VMEM((1, contacts), F32),
            pltpu.VMEM((2, width, width), BF16),
        ],
        compiler_params=params(),
        cost_estimate=pl.CostEstimate(
            flops=groups * 5 * 10**9,
            bytes_accessed=20 * contacts * span,
            transcendentals=groups * HEADS * contacts * contacts,
        ),
        name="forward",
    )(place, *small, *features)


def backward(place, upstream, kept, w_out, tm_count):
    blocks, rows, span = upstream.shape
    contacts = rows * blocks
    width = w_out.shape[0]
    groups = span // width
    chunk = (4 * width // tm_count, width)
    return pl.pallas_call(
        functools.partial(backward_kernel, blocks),
        grid=(groups,),
        in_specs=[
            index_spec(), whole(w_out.shape),
            pl.BlockSpec((blocks, rows, width), lambda i: (0, 0, i)),
        ]
        + [
            pl.BlockSpec((item.shape[0], item.shape[1] // groups), lambda i: (0, i))
            for item in kept
        ],
        out_specs=[whole(chunk)] * tm_count,
        out_shape=[jax.ShapeDtypeStruct(chunk, BF16)] * tm_count,
        scratch_shapes=[
            pltpu.VMEM((4, width, width), F32),
            pltpu.VMEM((tm_count,) + chunk, BF16),
            pltpu.VMEM((contacts, HEADS * contacts), BF16),
        ],
        compiler_params=params(),
        cost_estimate=pl.CostEstimate(
            flops=groups * 5 * 10**9, bytes_accessed=20 * contacts * span, transcendentals=0
        ),
        name="backward",
    )(place, w_out, upstream, *kept)


def place_all(place, parts):
    rows, width = parts[0].shape
    ways = len(parts)

    def body(place_ref, *refs):
        for k in range(ways):
            refs[-1][place_ref[0] ^ k] = refs[k][...].astype(F32)

    shape = (ways, rows, width)
    return pl.pallas_call(
        body,
        in_specs=[index_spec()] + [pl.BlockSpec((rows, width), lambda: (0, 0))] * ways,
        out_specs=pl.BlockSpec(shape, lambda: (0, 0, 0)),
        out_shape=jax.ShapeDtypeStruct(shape, F32),
        compiler_params=params(),
        name="place_all",
    )(place, *parts)


def write_out(value):
    def body(in_ref, out_ref):
        out_ref[...] = in_ref[...]

    spec = pl.BlockSpec((value.shape[0] // 2,) + value.shape[1:], lambda i: (i, 0, 0))
    return pl.pallas_call(
        body,
        grid=(2,),
        in_specs=[spec],
        out_specs=spec,
        out_shape=jax.ShapeDtypeStruct(value.shape, value.dtype),
        compiler_params=params(),
        cost_estimate=pl.CostEstimate(flops=0, bytes_accessed=4 * value.size, transcendentals=0),
        name="write_out",
    )(value)


def swap(value, axis, k):
    return lax.ppermute(value, axis, [(i, i ^ k) for i in range(lax.axis_size(axis))])


def swap_all(parts, axis):
    moved = [swap(parts[k], axis, k) for k in range(len(parts) - 1, 0, -1)]
    return [parts[0]] + moved[::-1]


def exchange(value, axis):
    return lax.all_to_all(value, axis, split_axis=0, concat_axis=0, tiled=True)


def local(
    signal, fir_taps, neighbours, live_mask, lap_coef, w_query, w_key, w_value, w_out, cotangent
):
    batch, contacts_here, slab = signal.shape
    rim_width = fir_taps.shape[1] - 1
    width = w_query.shape[0]
    tm_count = lax.axis_size("tm")
    count = lax.axis_size("contact")
    pieces = count // batch
    span = slab // pieces
    place = jnp.stack([lax.axis_index("tm"), lax.axis_index("contact")]).astype(jnp.int32)

    if pieces > 1:
        cotangent = cotangent.reshape(batch, contacts_here, pieces, span)
        cotangent = cotangent.transpose(0, 2, 1, 3).reshape(count, contacts_here, span)
    rim = lax.ppermute(
        signal[:, :, slab - rim_width :], "tm", [(i, i + 1) for i in range(tm_count - 1)]
    )
    filtered = filter_all(place, signal, rim, fir_taps, count)
    features = swap_all(filtered, "contact")
    arrived = count - max(2, 3 * count // 8)
    features[arrived:], cotangent = lax.optimization_barrier((features[arrived:], cotangent))
    upstream = exchange(cotangent, "contact")
    attended, *kept = forward(
        place, features, neighbours.T, live_mask[None], lap_coef[None],
        [w_query, w_key, w_value, w_out],
    )
    returned = exchange(attended, "contact")
    grads = backward(place, upstream, kept, w_out, tm_count)
    grads = swap_all(grads, "tm")
    part = sum(piece.astype(F32) for piece in grads).astype(BF16)
    part, returned = lax.optimization_barrier((part, returned))
    returned = write_out(returned)
    grad_scale = (batch * (slab // width) * tm_count * neighbours.shape[0]) ** (-0.5)
    step = 1
    while step < count:
        both = part.astype(F32) + swap(part, "contact", step).astype(F32)
        step *= 2
        part = lax.optimization_barrier((both * (1.0 if step < count else grad_scale)).astype(BF16))
    summed = place_all(place, swap_all([part] * tm_count, "tm"))
    if pieces > 1:
        returned = returned.reshape(batch, pieces, contacts_here, span)
        returned = returned.transpose(0, 2, 1, 3).reshape(batch, contacts_here, slab)
    return (returned, summed.reshape(4, width, width))


def solution(mesh):
    in_specs = (
        P(None, "contact", "tm"),
        P("contact", None),
        P(),
        P(),
        P(),
        P(),
        P(),
        P(),
        P(),
        P(None, "contact", "tm"),
    )
    out_specs = (P(None, "contact", "tm"), P())
    return jax.shard_map(local, mesh=mesh, in_specs=in_specs, out_specs=out_specs, check_vma=False)
```

```python
import functools

import jax
import jax.numpy as jnp
from jax import lax
from jax.experimental import pallas as pl
from jax.experimental.pallas import tpu as pltpu
from jax.sharding import PartitionSpec as P

HEADS = 4
F32 = jnp.float32
BF16 = jnp.bfloat16


def mm(left, right, left_dim=1, right_dim=0):
    return lax.dot_general(
        left, right, (((left_dim,), (right_dim,)), ((), ())), preferred_element_type=F32
    )


def index_spec():
    return pl.BlockSpec(memory_space=pltpu.SMEM)


def params():
    return pltpu.CompilerParams(vmem_limit_bytes=56 * 2**20)


def filter_kernel(place_ref, sig_ref, rim_ref, taps_ref, *refs):
    out_refs, kept = refs[:-1], refs[-1]
    batch, rows, slab = sig_ref.shape
    width = rim_ref.shape[2]
    blocks = slab // width
    pieces = len(out_refs) // batch
    span = slab // pieces
    signal = jnp.swapaxes(sig_ref[...].astype(F32), 0, 1)
    rim = jnp.swapaxes(rim_ref[...].astype(F32), 0, 1)
    taps = taps_ref[...].astype(F32)
    first = lax.broadcasted_iota(jnp.int32, (rows, width), 1) == 0
    taps = jnp.concatenate(
        [taps[:, :width], jnp.where(first, taps[:, width : width + 1], 0.0)], axis=1
    )
    results = []
    for row in range(rows):
        own = [signal[row, :, j * width : (j + 1) * width] for j in range(blocks)]
        current = jnp.concatenate(own, axis=0)
        before = jnp.concatenate([rim[row]] + own[:-1], axis=0)
        window = jnp.concatenate([before, current], axis=1).astype(BF16)
        spread = jnp.broadcast_to(taps[row : row + 1, :], (width, 2 * width))
        rolled = pltpu.roll(spread, 0, 1, stride=1, stride_axis=0)
        table = jnp.concatenate([rolled[:, width:], rolled[:, :width]], axis=0).astype(BF16)
        product = mm(window, table)
        results.append(
            jnp.concatenate(
                [product[j * batch : (j + 1) * batch] for j in range(blocks)], axis=1
            )
        )
    filtered = jnp.swapaxes(jnp.stack(results, axis=0), 0, 1).astype(BF16)
    for index in range(batch):
        for piece in range(pieces):
            kept[index * pieces + piece] = filtered[index, :, piece * span : (piece + 1) * span]
    me = place_ref[1]
    for k, out_ref in enumerate(out_refs):
        out_ref[...] = kept[me ^ k]


def filter_all(place, signal, rim, taps, count):
    batch, contacts, slab = signal.shape
    width = rim.shape[2]
    rows = min(32, contacts)
    span = slab * batch // count
    return pl.pallas_call(
        filter_kernel,
        grid=(contacts // rows,),
        in_specs=[
            index_spec(),
            pl.BlockSpec((batch, rows, slab), lambda i: (0, i, 0)),
            pl.BlockSpec((batch, rows, width), lambda i: (0, i, 0)),
            pl.BlockSpec((rows, taps.shape[1]), lambda i: (i, 0)),
        ],
        out_specs=[pl.BlockSpec((rows, span), lambda i: (i, 0))] * count,
        out_shape=[jax.ShapeDtypeStruct((contacts, span), BF16)] * count,
        scratch_shapes=[pltpu.VMEM((count, rows, span), BF16)],
        compiler_params=params(),
        cost_estimate=pl.CostEstimate(
            flops=4 * batch * contacts * slab * width,
            bytes_accessed=4 * batch * contacts * slab,
            transcendentals=0,
        ),
        name="filter",
    )(place, signal, rim, taps)


def pair_masks(pair):
    lane = lax.broadcasted_iota(jnp.int32, (1, pair), 1)
    return [(lane < pair // 2).astype(F32).astype(BF16), (lane >= pair // 2).astype(F32).astype(BF16)]


def head_masks(width):
    lane_head = lax.broadcasted_iota(jnp.int32, (1, width), 1) // (width // HEADS)
    return [(lane_head == h).astype(F32) for h in range(HEADS)]


def forward_kernel(
    blocks, place_ref, nbr_ref, live_ref, coef_ref, wq_ref, wk_ref, wv_ref, wo_ref, *refs
):
    feat_refs = refs[:blocks]
    (
        out_ref, prob_ref, value_ref, keys_ref, query_t_ref, normed_ref, normed_t_ref, mixed_ref,
        mixed_t_ref, inverse_ref, counts, columns, packed, live_row, turned_w,
    ) = refs[blocks:]
    rows, width = feat_refs[0].shape
    contacts = rows * blocks
    scale = (width // HEADS) ** (-0.5)
    slots = nbr_ref.shape[0]
    me = place_ref[1]

    @pl.when(pl.program_id(0) == 0)
    def _():
        packed[...] = jnp.zeros_like(packed)
        packed[0:1, :] = live_ref[...].astype(F32)
        packed[1:2, :] = coef_ref[...]
        for slot in range(slots):
            packed[2 + slot : 3 + slot, :] = nbr_ref[slot : slot + 1, :].astype(F32)
        columns[...] = packed[...].T
        turned = jnp.concatenate(
            [columns[pl.ds(pl.multiple_of((me ^ k) * rows, rows), rows), :] for k in range(blocks)],
            axis=0,
        )
        alive = turned.T[0:1]
        live_row[...] = alive
        ids = lax.broadcasted_iota(jnp.int32, (contacts, contacts), 1)
        total = jnp.zeros((contacts, contacts), F32)
        for slot in range(slots):
            here = turned[:, slot + 2 : slot + 3].astype(jnp.int32) ^ (me * rows)
            total = total + jnp.where(here == ids, alive, 0.0)
        counts[...] = total.astype(BF16)
        columns[:, 0:1] = turned[:, 0:1]
        columns[:, 1:2] = turned[:, 1:2]
        columns[:, 2:3] = jnp.sum(total, axis=1, keepdims=True)
        turned_w[0] = wq_ref[...].T
        turned_w[1] = wk_ref[...].T

    live = columns[:, 0:1]
    coef = columns[:, 1:2]
    field = jnp.concatenate([ref[...] for ref in feat_refs], axis=0)
    middle = field.astype(F32)
    beside = mm(counts[...], field)
    ready = live * (middle + coef * (beside - columns[:, 2:3] * middle))
    ready = ready.astype(BF16).astype(F32)
    mean_square = jnp.mean(ready * ready, axis=1, keepdims=True)
    normed = (ready * lax.rsqrt(mean_square + 1e-05)).astype(BF16)
    query = (mm(normed, wq_ref[...]) * scale).astype(BF16)
    keys = mm(normed, wk_ref[...]).astype(BF16)
    value = mm(normed, wv_ref[...]).astype(BF16)
    normed_t = normed.T
    keys_t = mm(turned_w[1], normed_t).astype(BF16)
    value_ref[...] = value
    keys_ref[...] = keys
    query_t_ref[...] = (mm(turned_w[0], normed_t) * scale).astype(BF16)
    normed_ref[...] = normed
    normed_t_ref[...] = normed_t
    pair = 2 * width // HEADS
    masks = pair_masks(pair)

    def score(h):
        lanes = slice(h // 2 * pair, (h // 2 + 1) * pair)
        return mm(query[:, lanes] * masks[h % 2], keys_t[lanes, :])

    bias = jnp.where(live_row[...] > 0, 0.0, -1e30)
    block = min(64, contacts)
    scores = score(0)
    products = []
    for h in range(HEADS):
        following = score(h + 1) if h + 1 < HEADS else None
        columns_h = slice(h * contacts, (h + 1) * contacts)
        for r in range(contacts // block):
            here = slice(r * block, (r + 1) * block)
            part = scores[here] + bias
            raised = jnp.exp(part - jnp.max(part, axis=1, keepdims=True))
            prob_ref[here, columns_h] = raised.astype(BF16)
        lanes = slice(h // 2 * pair, (h // 2 + 1) * pair)
        with_ones = value[:, lanes] * masks[h % 2] + masks[1 - h % 2]
        products.append(mm(prob_ref[:, columns_h], with_ones))
        scores = following
    low_lanes = lax.broadcasted_iota(jnp.int32, (contacts, pair), 1) < pair // 2
    mixed = []
    for p in range(HEADS // 2):
        even, odd = products[2 * p], products[2 * p + 1]
        inverse = 1.0 / pltpu.roll(jnp.where(low_lanes, odd, even), pair // 2, 1)
        inverse_ref[:, p * pair : (p + 1) * pair] = inverse
        mixed.append((jnp.where(low_lanes, even, odd) * inverse).astype(BF16))
    mixed = jnp.concatenate(mixed, axis=1)
    attended = mm(mixed, wo_ref[...]).astype(BF16)
    for k in range(blocks):
        out_ref[me ^ k] = attended[k * rows : (k + 1) * rows]
    mixed_ref[...] = mixed
    mixed_t_ref[...] = mixed.T


def backward_kernel(
    blocks, place_ref, wo_ref, up_ref, prob_ref, value_ref, keys_ref, query_t_ref, normed_ref,
    normed_t_ref, mixed_ref, mixed_t_ref, inverse_ref, *refs,
):
    out_refs, total, chunks, changes = refs[:-3], refs[-3], refs[-2], refs[-1]
    contacts, width = normed_ref.shape
    head = width // HEADS
    scale = head ** (-0.5)
    step = pl.program_id(0)

    @pl.when(step == 0)
    def _():
        total[...] = jnp.zeros_like(total)

    me = place_ref[1]
    upstream = jnp.concatenate([up_ref[me ^ k] for k in range(blocks)], axis=0)
    normed = normed_ref[...]
    value = value_ref[...]
    keys = keys_ref[...]
    back = mm(upstream, wo_ref[...], 1, 1).astype(BF16)
    back = (back.astype(F32) * inverse_ref[...]).astype(BF16)
    back_t = back.T
    inner = back.astype(F32) * mixed_ref[...].astype(F32)
    masks = head_masks(width)
    grad_value_t = []
    grad_key_t = []
    grad_query = None
    low = [m.astype(BF16) for m in masks]
    block = min(64, contacts)
    grad_prob = mm(back * low[0], value, 1, 1)
    for h in range(HEADS):
        following = mm(back * low[h + 1], value, 1, 1) if h + 1 < HEADS else None
        columns_h = slice(h * contacts, (h + 1) * contacts)
        grad_value_t.append(mm(back_t[h * head : (h + 1) * head], prob_ref[:, columns_h]))
        for r in range(contacts // block):
            here = slice(r * block, (r + 1) * block)
            row_inner = jnp.sum(inner[here] * masks[h], axis=1, keepdims=True)
            shift = (grad_prob[here] - row_inner).astype(BF16)
            changes[here, columns_h] = prob_ref[here, columns_h] * shift
        grad_score = changes[:, columns_h]
        grad_key_t.append(mm(query_t_ref[h * head : (h + 1) * head, :], grad_score))
        part = mm(grad_score, keys * low[h])
        grad_query = part if grad_query is None else grad_query + part
        grad_prob = following
    grad_query = (grad_query * scale).astype(BF16)
    total[0] += mm(normed_t_ref[...], grad_query)
    total[1] += mm(jnp.concatenate(grad_key_t, axis=0).astype(BF16), normed)
    total[2] += mm(jnp.concatenate(grad_value_t, axis=0).astype(BF16), normed)
    total[3] += mm(mixed_t_ref[...], upstream)

    @pl.when(step == pl.num_programs(0) - 1)
    def _():
        count, rows = chunks.shape[:2]
        parts = [total[0], total[1].T, total[2].T, total[3]]
        for c in range(count):
            first = (c * rows) % width
            chunks[c] = parts[c * rows // width][first : first + rows].astype(BF16)
        for k, out_ref in enumerate(out_refs):
            out_ref[...] = chunks[place_ref[0] ^ k]


def whole(shape):
    return pl.BlockSpec(shape, lambda i: (0,) * len(shape))


def forward(place, features, neighbours, live, coef, weights):
    blocks = len(features)
    rows, span = features[0].shape
    contacts = rows * blocks
    width = weights[0].shape[0]
    groups = span // width
    shapes = [
        (contacts, HEADS * contacts), (contacts, width),
        (contacts, width), (width, contacts), (contacts, width), (width, contacts),
        (contacts, width), (width, contacts), (contacts, width),
    ]
    small = [neighbours, live, coef] + list(weights)
    return pl.pallas_call(
        functools.partial(forward_kernel, blocks),
        grid=(groups,),
        in_specs=[index_spec()]
        + [whole(item.shape) for item in small]
        + [pl.BlockSpec((rows, width), lambda i: (0, i))] * blocks,
        out_specs=[pl.BlockSpec((blocks, rows, width), lambda i: (0, 0, i))]
        + [pl.BlockSpec(shape, lambda i: (0, i)) for shape in shapes],
        out_shape=[jax.ShapeDtypeStruct((blocks, rows, span), BF16)]
        + [
            jax.ShapeDtypeStruct((shape[0], groups * shape[1]), kind)
            for shape, kind in zip(shapes, [BF16] * (len(shapes) - 1) + [F32])
        ],
        scratch_shapes=[
            pltpu.VMEM((contacts, contacts), BF16),
            pltpu.VMEM((contacts, 128), F32),
            pltpu.VMEM((128, contacts), F32),
            pltpu.VMEM((1, contacts), F32),
            pltpu.VMEM((2, width, width), BF16),
        ],
        compiler_params=params(),
        cost_estimate=pl.CostEstimate(
            flops=groups * 5 * 10**9,
            bytes_accessed=20 * contacts * span,
            transcendentals=groups * HEADS * contacts * contacts,
        ),
        name="forward",
    )(place, *small, *features)


def backward(place, upstream, kept, w_out, tm_count):
    blocks, rows, span = upstream.shape
    contacts = rows * blocks
    width = w_out.shape[0]
    groups = span // width
    chunk = (4 * width // tm_count, width)
    return pl.pallas_call(
        functools.partial(backward_kernel, blocks),
        grid=(groups,),
        in_specs=[
            index_spec(), whole(w_out.shape),
            pl.BlockSpec((blocks, rows, width), lambda i: (0, 0, i)),
        ]
        + [
            pl.BlockSpec((item.shape[0], item.shape[1] // groups), lambda i: (0, i))
            for item in kept
        ],
        out_specs=[whole(chunk)] * tm_count,
        out_shape=[jax.ShapeDtypeStruct(chunk, BF16)] * tm_count,
        scratch_shapes=[
            pltpu.VMEM((4, width, width), F32),
            pltpu.VMEM((tm_count,) + chunk, BF16),
            pltpu.VMEM((contacts, HEADS * contacts), BF16),
        ],
        compiler_params=params(),
        cost_estimate=pl.CostEstimate(
            flops=groups * 5 * 10**9, bytes_accessed=20 * contacts * span, transcendentals=0
        ),
        name="backward",
    )(place, w_out, upstream, *kept)


def place_all(place, parts):
    rows, width = parts[0].shape
    ways = len(parts)

    def body(place_ref, *refs):
        for k in range(ways):
            refs[-1][place_ref[0] ^ k] = refs[k][...].astype(F32)

    shape = (ways, rows, width)
    return pl.pallas_call(
        body,
        in_specs=[index_spec()] + [pl.BlockSpec((rows, width), lambda: (0, 0))] * ways,
        out_specs=pl.BlockSpec(shape, lambda: (0, 0, 0)),
        out_shape=jax.ShapeDtypeStruct(shape, F32),
        compiler_params=params(),
        name="place_all",
    )(place, *parts)


def write_out(value):
    def body(in_ref, out_ref):
        out_ref[...] = in_ref[...]

    spec = pl.BlockSpec((value.shape[0] // 2,) + value.shape[1:], lambda i: (i, 0, 0))
    return pl.pallas_call(
        body,
        grid=(2,),
        in_specs=[spec],
        out_specs=spec,
        out_shape=jax.ShapeDtypeStruct(value.shape, value.dtype),
        compiler_params=params(),
        cost_estimate=pl.CostEstimate(flops=0, bytes_accessed=4 * value.size, transcendentals=0),
        name="write_out",
    )(value)


def swap(value, axis, k):
    return lax.ppermute(value, axis, [(i, i ^ k) for i in range(lax.axis_size(axis))])


def swap_all(parts, axis):
    moved = [swap(parts[k], axis, k) for k in range(len(parts) - 1, 0, -1)]
    return [parts[0]] + moved[::-1]


def exchange(value, axis):
    return lax.all_to_all(value, axis, split_axis=0, concat_axis=0, tiled=True)


def local(
    signal, fir_taps, neighbours, live_mask, lap_coef, w_query, w_key, w_value, w_out, cotangent
):
    batch, contacts_here, slab = signal.shape
    rim_width = fir_taps.shape[1] - 1
    width = w_query.shape[0]
    tm_count = lax.axis_size("tm")
    count = lax.axis_size("contact")
    pieces = count // batch
    span = slab // pieces
    place = jnp.stack([lax.axis_index("tm"), lax.axis_index("contact")]).astype(jnp.int32)

    if pieces > 1:
        cotangent = cotangent.reshape(batch, contacts_here, pieces, span)
        cotangent = cotangent.transpose(0, 2, 1, 3).reshape(count, contacts_here, span)
    rim = lax.ppermute(
        signal[:, :, slab - rim_width :], "tm", [(i, i + 1) for i in range(tm_count - 1)]
    )
    filtered = filter_all(place, signal, rim, fir_taps, count)
    features = swap_all(filtered, "contact")
    arrived = count - max(2, count // 2)
    features[arrived:], cotangent = lax.optimization_barrier((features[arrived:], cotangent))
    upstream = exchange(cotangent, "contact")
    attended, *kept = forward(
        place, features, neighbours.T, live_mask[None], lap_coef[None],
        [w_query, w_key, w_value, w_out],
    )
    returned = exchange(attended, "contact")
    grads = backward(place, upstream, kept, w_out, tm_count)
    grads = swap_all(grads, "tm")
    part = sum(piece.astype(F32) for piece in grads).astype(BF16)
    part, returned = lax.optimization_barrier((part, returned))
    returned = write_out(returned)
    grad_scale = (batch * (slab // width) * tm_count * neighbours.shape[0]) ** (-0.5)
    step = 1
    while step < count:
        both = part.astype(F32) + swap(part, "contact", step).astype(F32)
        step *= 2
        part = lax.optimization_barrier((both * (1.0 if step < count else grad_scale)).astype(BF16))
    summed = place_all(place, swap_all([part] * tm_count, "tm"))
    if pieces > 1:
        returned = returned.reshape(batch, pieces, contacts_here, span)
        returned = returned.transpose(0, 2, 1, 3).reshape(batch, contacts_here, slab)
    return (returned, summed.reshape(4, width, width))


def solution(mesh):
    in_specs = (
        P(None, "contact", "tm"),
        P("contact", None),
        P(),
        P(),
        P(),
        P(),
        P(),
        P(),
        P(),
        P(None, "contact", "tm"),
    )
    out_specs = (P(None, "contact", "tm"), P())
    return jax.shard_map(local, mesh=mesh, in_specs=in_specs, out_specs=out_specs, check_vma=False)
```

```python
import functools

import jax
import jax.numpy as jnp
from jax import lax
from jax.experimental import pallas as pl
from jax.experimental.pallas import tpu as pltpu
from jax.sharding import PartitionSpec as P

HEADS = 4
F32 = jnp.float32
BF16 = jnp.bfloat16


def mm(left, right, left_dim=1, right_dim=0):
    return lax.dot_general(
        left, right, (((left_dim,), (right_dim,)), ((), ())), preferred_element_type=F32
    )


def index_spec():
    return pl.BlockSpec(memory_space=pltpu.SMEM)


def params():
    return pltpu.CompilerParams(vmem_limit_bytes=56 * 2**20)


def filter_kernel(place_ref, sig_ref, rim_ref, taps_ref, *refs):
    out_refs, kept = refs[:-1], refs[-1]
    batch, rows, slab = sig_ref.shape
    width = rim_ref.shape[2]
    blocks = slab // width
    pieces = len(out_refs) // batch
    span = slab // pieces
    signal = jnp.swapaxes(sig_ref[...].astype(F32), 0, 1)
    rim = jnp.swapaxes(rim_ref[...].astype(F32), 0, 1)
    taps = taps_ref[...].astype(F32)
    first = lax.broadcasted_iota(jnp.int32, (rows, width), 1) == 0
    taps = jnp.concatenate(
        [taps[:, :width], jnp.where(first, taps[:, width : width + 1], 0.0)], axis=1
    )
    results = []
    for row in range(rows):
        own = [signal[row, :, j * width : (j + 1) * width] for j in range(blocks)]
        current = jnp.concatenate(own, axis=0)
        before = jnp.concatenate([rim[row]] + own[:-1], axis=0)
        window = jnp.concatenate([before, current], axis=1).astype(BF16)
        spread = jnp.broadcast_to(taps[row : row + 1, :], (width, 2 * width))
        rolled = pltpu.roll(spread, 0, 1, stride=1, stride_axis=0)
        table = jnp.concatenate([rolled[:, width:], rolled[:, :width]], axis=0).astype(BF16)
        product = mm(window, table)
        results.append(
            jnp.concatenate(
                [product[j * batch : (j + 1) * batch] for j in range(blocks)], axis=1
            )
        )
    filtered = jnp.swapaxes(jnp.stack(results, axis=0), 0, 1).astype(BF16)
    for index in range(batch):
        for piece in range(pieces):
            kept[index * pieces + piece] = filtered[index, :, piece * span : (piece + 1) * span]
    me = place_ref[1]
    for k, out_ref in enumerate(out_refs):
        out_ref[...] = kept[me ^ k]


def filter_all(place, signal, rim, taps, count):
    batch, contacts, slab = signal.shape
    width = rim.shape[2]
    rows = min(64, contacts)
    span = slab * batch // count
    return pl.pallas_call(
        filter_kernel,
        grid=(contacts // rows,),
        in_specs=[
            index_spec(),
            pl.BlockSpec((batch, rows, slab), lambda i: (0, i, 0)),
            pl.BlockSpec((batch, rows, width), lambda i: (0, i, 0)),
            pl.BlockSpec((rows, taps.shape[1]), lambda i: (i, 0)),
        ],
        out_specs=[pl.BlockSpec((rows, span), lambda i: (i, 0))] * count,
        out_shape=[jax.ShapeDtypeStruct((contacts, span), BF16)] * count,
        scratch_shapes=[pltpu.VMEM((count, rows, span), BF16)],
        compiler_params=params(),
        cost_estimate=pl.CostEstimate(
            flops=4 * batch * contacts * slab * width,
            bytes_accessed=4 * batch * contacts * slab,
            transcendentals=0,
        ),
        name="filter",
    )(place, signal, rim, taps)


def pair_masks(pair):
    lane = lax.broadcasted_iota(jnp.int32, (1, pair), 1)
    return [(lane < pair // 2).astype(F32).astype(BF16), (lane >= pair // 2).astype(F32).astype(BF16)]


def head_masks(width):
    lane_head = lax.broadcasted_iota(jnp.int32, (1, width), 1) // (width // HEADS)
    return [(lane_head == h).astype(F32) for h in range(HEADS)]


def forward_kernel(
    blocks, place_ref, nbr_ref, live_ref, coef_ref, wq_ref, wk_ref, wv_ref, wo_ref, *refs
):
    feat_refs = refs[:blocks]
    (
        out_ref, prob_ref, value_ref, keys_ref, query_t_ref, normed_ref, normed_t_ref, mixed_ref,
        mixed_t_ref, inverse_ref, counts, columns, packed, live_row, turned_w,
    ) = refs[blocks:]
    rows, width = feat_refs[0].shape
    contacts = rows * blocks
    scale = (width // HEADS) ** (-0.5)
    slots = nbr_ref.shape[0]
    me = place_ref[1]

    @pl.when(pl.program_id(0) == 0)
    def _():
        packed[...] = jnp.zeros_like(packed)
        packed[0:1, :] = live_ref[...].astype(F32)
        packed[1:2, :] = coef_ref[...]
        for slot in range(slots):
            packed[2 + slot : 3 + slot, :] = nbr_ref[slot : slot + 1, :].astype(F32)
        columns[...] = packed[...].T
        turned = jnp.concatenate(
            [columns[pl.ds(pl.multiple_of((me ^ k) * rows, rows), rows), :] for k in range(blocks)],
            axis=0,
        )
        alive = turned.T[0:1]
        live_row[...] = alive
        ids = lax.broadcasted_iota(jnp.int32, (contacts, contacts), 1)
        total = jnp.zeros((contacts, contacts), F32)
        for slot in range(slots):
            here = turned[:, slot + 2 : slot + 3].astype(jnp.int32) ^ (me * rows)
            total = total + jnp.where(here == ids, alive, 0.0)
        counts[...] = total.astype(BF16)
        columns[:, 0:1] = turned[:, 0:1]
        columns[:, 1:2] = turned[:, 1:2]
        columns[:, 2:3] = jnp.sum(total, axis=1, keepdims=True)
        turned_w[0] = wq_ref[...].T
        turned_w[1] = wk_ref[...].T

    live = columns[:, 0:1]
    coef = columns[:, 1:2]
    field = jnp.concatenate([ref[...] for ref in feat_refs], axis=0)
    middle = field.astype(F32)
    beside = mm(counts[...], field)
    ready = live * (middle + coef * (beside - columns[:, 2:3] * middle))
    ready = ready.astype(BF16).astype(F32)
    mean_square = jnp.mean(ready * ready, axis=1, keepdims=True)
    normed = (ready * lax.rsqrt(mean_square + 1e-05)).astype(BF16)
    query = (mm(normed, wq_ref[...]) * scale).astype(BF16)
    keys = mm(normed, wk_ref[...]).astype(BF16)
    value = mm(normed, wv_ref[...]).astype(BF16)
    normed_t = normed.T
    keys_t = mm(turned_w[1], normed_t).astype(BF16)
    value_ref[...] = value
    keys_ref[...] = keys
    query_t_ref[...] = (mm(turned_w[0], normed_t) * scale).astype(BF16)
    normed_ref[...] = normed
    normed_t_ref[...] = normed_t
    pair = 2 * width // HEADS
    masks = pair_masks(pair)

    def score(h):
        lanes = slice(h // 2 * pair, (h // 2 + 1) * pair)
        return mm(query[:, lanes] * masks[h % 2], keys_t[lanes, :])

    bias = jnp.where(live_row[...] > 0, 0.0, -1e30)
    block = min(64, contacts)
    scores = score(0)
    products = []
    for h in range(HEADS):
        following = score(h + 1) if h + 1 < HEADS else None
        columns_h = slice(h * contacts, (h + 1) * contacts)
        for r in range(contacts // block):
            here = slice(r * block, (r + 1) * block)
            part = scores[here] + bias
            raised = jnp.exp(part - jnp.max(part, axis=1, keepdims=True))
            prob_ref[here, columns_h] = raised.astype(BF16)
        lanes = slice(h // 2 * pair, (h // 2 + 1) * pair)
        with_ones = value[:, lanes] * masks[h % 2] + masks[1 - h % 2]
        products.append(mm(prob_ref[:, columns_h], with_ones))
        scores = following
    low_lanes = lax.broadcasted_iota(jnp.int32, (contacts, pair), 1) < pair // 2
    mixed = []
    for p in range(HEADS // 2):
        even, odd = products[2 * p], products[2 * p + 1]
        inverse = 1.0 / pltpu.roll(jnp.where(low_lanes, odd, even), pair // 2, 1)
        inverse_ref[:, p * pair : (p + 1) * pair] = inverse
        mixed.append((jnp.where(low_lanes, even, odd) * inverse).astype(BF16))
    mixed = jnp.concatenate(mixed, axis=1)
    attended = mm(mixed, wo_ref[...]).astype(BF16)
    for k in range(blocks):
        out_ref[me ^ k] = attended[k * rows : (k + 1) * rows]
    mixed_ref[...] = mixed
    mixed_t_ref[...] = mixed.T


def backward_kernel(
    blocks, place_ref, wo_ref, up_ref, prob_ref, value_ref, keys_ref, query_t_ref, normed_ref,
    normed_t_ref, mixed_ref, mixed_t_ref, inverse_ref, *refs,
):
    out_refs, total, chunks, changes = refs[:-3], refs[-3], refs[-2], refs[-1]
    contacts, width = normed_ref.shape
    head = width // HEADS
    scale = head ** (-0.5)
    step = pl.program_id(0)

    @pl.when(step == 0)
    def _():
        total[...] = jnp.zeros_like(total)

    me = place_ref[1]
    upstream = jnp.concatenate([up_ref[me ^ k] for k in range(blocks)], axis=0)
    normed = normed_ref[...]
    value = value_ref[...]
    keys = keys_ref[...]
    back = mm(upstream, wo_ref[...], 1, 1).astype(BF16)
    back = (back.astype(F32) * inverse_ref[...]).astype(BF16)
    back_t = back.T
    inner = back.astype(F32) * mixed_ref[...].astype(F32)
    masks = head_masks(width)
    grad_value_t = []
    grad_key_t = []
    grad_query = None
    low = [m.astype(BF16) for m in masks]
    block = min(64, contacts)
    grad_prob = mm(back * low[0], value, 1, 1)
    for h in range(HEADS):
        following = mm(back * low[h + 1], value, 1, 1) if h + 1 < HEADS else None
        columns_h = slice(h * contacts, (h + 1) * contacts)
        grad_value_t.append(mm(back_t[h * head : (h + 1) * head], prob_ref[:, columns_h]))
        for r in range(contacts // block):
            here = slice(r * block, (r + 1) * block)
            row_inner = jnp.sum(inner[here] * masks[h], axis=1, keepdims=True)
            shift = (grad_prob[here] - row_inner).astype(BF16)
            changes[here, columns_h] = prob_ref[here, columns_h] * shift
        grad_score = changes[:, columns_h]
        grad_key_t.append(mm(query_t_ref[h * head : (h + 1) * head, :], grad_score))
        part = mm(grad_score, keys * low[h])
        grad_query = part if grad_query is None else grad_query + part
        grad_prob = following
    grad_query = (grad_query * scale).astype(BF16)
    total[0] += mm(normed_t_ref[...], grad_query)
    total[1] += mm(jnp.concatenate(grad_key_t, axis=0).astype(BF16), normed)
    total[2] += mm(jnp.concatenate(grad_value_t, axis=0).astype(BF16), normed)
    total[3] += mm(mixed_t_ref[...], upstream)

    @pl.when(step == pl.num_programs(0) - 1)
    def _():
        count, rows = chunks.shape[:2]
        parts = [total[0], total[1].T, total[2].T, total[3]]
        for c in range(count):
            first = (c * rows) % width
            chunks[c] = parts[c * rows // width][first : first + rows].astype(BF16)
        for k, out_ref in enumerate(out_refs):
            out_ref[...] = chunks[place_ref[0] ^ k]


def whole(shape):
    return pl.BlockSpec(shape, lambda i: (0,) * len(shape))


def forward(place, features, neighbours, live, coef, weights):
    blocks = len(features)
    rows, span = features[0].shape
    contacts = rows * blocks
    width = weights[0].shape[0]
    groups = span // width
    shapes = [
        (contacts, HEADS * contacts), (contacts, width),
        (contacts, width), (width, contacts), (contacts, width), (width, contacts),
        (contacts, width), (width, contacts), (contacts, width),
    ]
    small = [neighbours, live, coef] + list(weights)
    return pl.pallas_call(
        functools.partial(forward_kernel, blocks),
        grid=(groups,),
        in_specs=[index_spec()]
        + [whole(item.shape) for item in small]
        + [pl.BlockSpec((rows, width), lambda i: (0, i))] * blocks,
        out_specs=[pl.BlockSpec((blocks, rows, width), lambda i: (0, 0, i))]
        + [pl.BlockSpec(shape, lambda i: (0, i)) for shape in shapes],
        out_shape=[jax.ShapeDtypeStruct((blocks, rows, span), BF16)]
        + [
            jax.ShapeDtypeStruct((shape[0], groups * shape[1]), kind)
            for shape, kind in zip(shapes, [BF16] * (len(shapes) - 1) + [F32])
        ],
        scratch_shapes=[
            pltpu.VMEM((contacts, contacts), BF16),
            pltpu.VMEM((contacts, 128), F32),
            pltpu.VMEM((128, contacts), F32),
            pltpu.VMEM((1, contacts), F32),
            pltpu.VMEM((2, width, width), BF16),
        ],
        compiler_params=params(),
        cost_estimate=pl.CostEstimate(
            flops=groups * 5 * 10**9,
            bytes_accessed=20 * contacts * span,
            transcendentals=groups * HEADS * contacts * contacts,
        ),
        name="forward",
    )(place, *small, *features)


def backward(place, upstream, kept, w_out, tm_count):
    blocks, rows, span = upstream.shape
    contacts = rows * blocks
    width = w_out.shape[0]
    groups = span // width
    chunk = (4 * width // tm_count, width)
    return pl.pallas_call(
        functools.partial(backward_kernel, blocks),
        grid=(groups,),
        in_specs=[
            index_spec(), whole(w_out.shape),
            pl.BlockSpec((blocks, rows, width), lambda i: (0, 0, i)),
        ]
        + [
            pl.BlockSpec((item.shape[0], item.shape[1] // groups), lambda i: (0, i))
            for item in kept
        ],
        out_specs=[whole(chunk)] * tm_count,
        out_shape=[jax.ShapeDtypeStruct(chunk, BF16)] * tm_count,
        scratch_shapes=[
            pltpu.VMEM((4, width, width), F32),
            pltpu.VMEM((tm_count,) + chunk, BF16),
            pltpu.VMEM((contacts, HEADS * contacts), BF16),
        ],
        compiler_params=params(),
        cost_estimate=pl.CostEstimate(
            flops=groups * 5 * 10**9, bytes_accessed=20 * contacts * span, transcendentals=0
        ),
        name="backward",
    )(place, w_out, upstream, *kept)


def place_all(place, parts):
    rows, width = parts[0].shape
    ways = len(parts)

    def body(place_ref, *refs):
        for k in range(ways):
            refs[-1][place_ref[0] ^ k] = refs[k][...].astype(F32)

    shape = (ways, rows, width)
    return pl.pallas_call(
        body,
        in_specs=[index_spec()] + [pl.BlockSpec((rows, width), lambda: (0, 0))] * ways,
        out_specs=pl.BlockSpec(shape, lambda: (0, 0, 0)),
        out_shape=jax.ShapeDtypeStruct(shape, F32),
        compiler_params=params(),
        name="place_all",
    )(place, *parts)


def write_out(value):
    def body(in_ref, out_ref):
        out_ref[...] = in_ref[...]

    spec = pl.BlockSpec((value.shape[0] // 2,) + value.shape[1:], lambda i: (i, 0, 0))
    return pl.pallas_call(
        body,
        grid=(2,),
        in_specs=[spec],
        out_specs=spec,
        out_shape=jax.ShapeDtypeStruct(value.shape, value.dtype),
        compiler_params=params(),
        cost_estimate=pl.CostEstimate(flops=0, bytes_accessed=4 * value.size, transcendentals=0),
        name="write_out",
    )(value)


def swap(value, axis, k):
    return lax.ppermute(value, axis, [(i, i ^ k) for i in range(lax.axis_size(axis))])


def swap_all(parts, axis):
    moved = [swap(parts[k], axis, k) for k in range(len(parts) - 1, 0, -1)]
    return [parts[0]] + moved[::-1]


def exchange(value, axis):
    return lax.all_to_all(value, axis, split_axis=0, concat_axis=0, tiled=True)


def local(
    signal, fir_taps, neighbours, live_mask, lap_coef, w_query, w_key, w_value, w_out, cotangent
):
    batch, contacts_here, slab = signal.shape
    rim_width = fir_taps.shape[1] - 1
    width = w_query.shape[0]
    tm_count = lax.axis_size("tm")
    count = lax.axis_size("contact")
    pieces = count // batch
    span = slab // pieces
    place = jnp.stack([lax.axis_index("tm"), lax.axis_index("contact")]).astype(jnp.int32)

    if pieces > 1:
        cotangent = cotangent.reshape(batch, contacts_here, pieces, span)
        cotangent = cotangent.transpose(0, 2, 1, 3).reshape(count, contacts_here, span)
    rim = lax.ppermute(
        signal[:, :, slab - rim_width :], "tm", [(i, i + 1) for i in range(tm_count - 1)]
    )
    filtered = filter_all(place, signal, rim, fir_taps, count)
    features = swap_all(filtered, "contact")
    arrived = count - max(2, 3 * count // 8)
    features[arrived:], cotangent = lax.optimization_barrier((features[arrived:], cotangent))
    upstream = exchange(cotangent, "contact")
    attended, *kept = forward(
        place, features, neighbours.T, live_mask[None], lap_coef[None],
        [w_query, w_key, w_value, w_out],
    )
    returned = exchange(attended, "contact")
    grads = backward(place, upstream, kept, w_out, tm_count)
    grads = swap_all(grads, "tm")
    part = sum(piece.astype(F32) for piece in grads).astype(BF16)
    part, returned = lax.optimization_barrier((part, returned))
    returned = write_out(returned)
    grad_scale = (batch * (slab // width) * tm_count * neighbours.shape[0]) ** (-0.5)
    step = 1
    while step < count:
        both = part.astype(F32) + swap(part, "contact", step).astype(F32)
        step *= 2
        part = lax.optimization_barrier((both * (1.0 if step < count else grad_scale)).astype(BF16))
    summed = place_all(place, swap_all([part] * tm_count, "tm"))
    if pieces > 1:
        returned = returned.reshape(batch, pieces, contacts_here, span)
        returned = returned.transpose(0, 2, 1, 3).reshape(batch, contacts_here, slab)
    return (returned, summed.reshape(4, width, width))


def solution(mesh):
    in_specs = (
        P(None, "contact", "tm"),
        P("contact", None),
        P(),
        P(),
        P(),
        P(),
        P(),
        P(),
        P(),
        P(None, "contact", "tm"),
    )
    out_specs = (P(None, "contact", "tm"), P())
    return jax.shard_map(local, mesh=mesh, in_specs=in_specs, out_specs=out_specs, check_vma=False)
```
